512 devices in a mesh: front: 4 (over x), row: 16 (over z), col: 8 (over y, core).
Axes of the slice: x: 4, y: 4, z: 16, core: 2. Of those that a mesh axis runs over, the one named last changes fastest.
Arguments:
- front_entries: float32 [4, 2, 2, 16, 8, 16, 8, 4, 256], P('front', None, None, 'row', 'col'), may hold values from -5 to 5
- child_updates: float32 [8, 12, 2, 16, 8, 12, 256], P('front', None, None, 'row', 'col'), may hold values from -1.5 to 1.5
- diag_boost: float32 [4, 32, 256], P('front'), may hold values from 96 to 192
- tile_mask: int32 [4, 32, 32], P('front'), may hold values 0 or 1
- child_parent: int32 [8], replicated, may hold values from 0 to 3, as said below
- child_index: int32 [8, 12], replicated, may hold values from 0 to 31, as said below
Outputs:
- factored_front: float32 [4, 2, 16, 256, 4, 8, 256], P('front', None, 'row', None, None, 'col')
The draws below stay inside these ranges and needn't reach their ends.
Inputs may be any that keep to these rules, and one draw needn't show every extreme that they name: `child_parent`: the 2 children stored in group g of the front axis, numbers g * 2 to g * 2 + 1, go to distinct parent fronts. `child_index`: each row lists 12 distinct parent tiles in increasing order.
All inputs are finite; a program needn't handle non-finite values. No bound on the sum of `tile_mask` on one device may be relied on, other than what follows from the above.
Results may differ from the reference program's by a relative error of at most 0.0001.
Values sent between devices are 32-bit elements; how exact they have to be, the bound alone decides.
No kernel may reach another device: no remote copies, remote signals or barrier semaphores. Data moves between devices by JAX's collectives and lax.ppermute only.
A program may use at most 64 MiB of HBM per device.

```python
import math
import jax
import jax.numpy as jnp
from jax import lax

TILE_ROWS = 256
LOCAL_ROWS = 2
CHILD_HELD = 2
PANELS = 4
ROW_SLICES = 2
PARENT_TILES = 32
CHILD_TILES = 12
FRONTS = 4
GRID_ROWS = 16
GRID_COLS = 8
LOCAL_COLS = 4
CHILDREN = 8


def draw_front_entries(key, part):
    key = jax.random.fold_in(key, 11)
    shape = (FRONTS, LOCAL_ROWS, ROW_SLICES, GRID_ROWS, GRID_COLS, GRID_ROWS, GRID_COLS, LOCAL_COLS, TILE_ROWS)
    values = jnp.clip(jax.random.normal(key, shape, jnp.float32), -5.0, 5.0)
    return values


def draw_child_updates(key, part):
    key = jax.random.fold_in(key, 12)
    shape = (CHILDREN, CHILD_TILES, ROW_SLICES, GRID_ROWS, GRID_COLS, CHILD_TILES, TILE_ROWS)
    values = jnp.clip(0.35 * jax.random.normal(key, shape, jnp.float32), -1.5, 1.5)
    return values


def draw_child_parent(key, part):
    key = jax.random.fold_in(key, 13)
    group_keys = jax.random.split(key, FRONTS)
    chosen = jax.vmap(lambda single: jax.random.permutation(single, FRONTS)[:CHILD_HELD])(group_keys)
    return chosen.reshape(CHILDREN).astype(jnp.int32)


def draw_child_index(key, part):
    key = jax.random.fold_in(key, 14)
    child_keys = jax.random.split(key, CHILDREN)
    chosen = jax.vmap(lambda single: jnp.sort(jax.random.permutation(single, PARENT_TILES)[:CHILD_TILES]))(child_keys)
    return chosen.astype(jnp.int32)


def touch_ends(drawn, stream_key, least, top_value):
    longest = drawn.shape.index(max(drawn.shape))
    spots = []
    for shift in (0, 1):
        where = [jax.random.randint(jax.random.fold_in(stream_key, axis), (), 0, length) for axis, length in enumerate(drawn.shape)]
        where[longest] = (where[longest] + shift) % drawn.shape[longest]
        spots.append(tuple(where))
    return drawn.at[spots[0]].set(least).at[spots[1]].set(top_value)


def levels(own_key, dims, cuts, least, top_value):
    factor_of = 1.0
    for axis_at, shards_of in cuts:
        heights = jax.random.uniform(jax.random.fold_in(jax.random.fold_in(own_key, 6), axis_at), (shards_of,), jnp.float32, least / len(cuts), top_value / len(cuts))
        factor_of = factor_of * jnp.repeat(jnp.exp(heights), dims[axis_at] // shards_of).reshape((-1,) + (1,) * (len(dims) - 1 - axis_at))
    return factor_of


def setup_inputs(seed: int = 0) -> dict:
    key_list = jax.random.split(jax.random.key(seed), 7)
    front_entries = draw_front_entries(jax.random.fold_in(key_list[6], 71), 0)
    child_updates = draw_child_updates(jax.random.fold_in(key_list[6], 71), 0)
    diag_boost = jnp.clip(jnp.exp(math.log(192.0) - 0.6931472 * jax.random.uniform(key_list[2], (FRONTS, PARENT_TILES, TILE_ROWS), jnp.float32) ** levels(key_list[2], (FRONTS, PARENT_TILES, TILE_ROWS), ((0, 4),), -0.2, 0.2)), 96.0, 192.0)
    tile_mask = touch_ends((jax.random.randint(key_list[3], (FRONTS, PARENT_TILES, PARENT_TILES), 0, 3) < 2).astype(jnp.int32), jax.random.fold_in(key_list[3], 1), 0, 1)
    child_parent = draw_child_parent(jax.random.fold_in(key_list[6], 71), 0)
    child_index = draw_child_index(jax.random.fold_in(key_list[6], 71), 0)
    return {"front_entries": front_entries, "child_updates": child_updates, "diag_boost": diag_boost, "tile_mask": tile_mask, "child_parent": child_parent, "child_index": child_index}


def mirror_lower(block):
    return jnp.tril(block) + jnp.transpose(jnp.tril(block, -1))

def eliminate(front_tiles):
    tile_count = front_tiles.shape[0]
    tile_size = front_tiles.shape[1]
    tile_ids = jnp.arange(tile_count).reshape(tile_count, 1, 1)
    for panel_step in range(PANELS):
        pivot_factor = jnp.linalg.cholesky(mirror_lower(front_tiles[panel_step, :, panel_step, :]))
        column = front_tiles[:, :, panel_step, :].reshape(tile_count * tile_size, tile_size)
        solved = lax.linalg.triangular_solve(pivot_factor, column, left_side=False, lower=True, transpose_a=True)
        solved = solved.reshape(tile_count, tile_size, tile_size)
        column = jnp.where(tile_ids > panel_step, solved, jnp.where(tile_ids == panel_step, pivot_factor[None], 0.0))
        front_tiles = front_tiles.at[:, :, panel_step, :].set(column)
        update = jnp.where(tile_ids > panel_step, column, 0.0)
        front_tiles = front_tiles - jnp.einsum('isk,tek->iste', update, update, precision=lax.Precision.HIGHEST)
    return front_tiles

def reference(front_entries, child_updates, diag_boost, tile_mask, child_parent, child_index):
    order_total = PARENT_TILES * TILE_ROWS
    children_tiles = child_updates.reshape(CHILDREN, CHILD_TILES, TILE_ROWS, CHILD_TILES, TILE_ROWS)
    diagonal_ids = jnp.arange(order_total)
    results = []
    for front_id in range(FRONTS):
        entries = jnp.transpose(front_entries[front_id], (0, 4, 1, 2, 3, 6, 5, 7))
        entries = entries.reshape(PARENT_TILES, TILE_ROWS, PARENT_TILES, TILE_ROWS)
        front_tiles = jnp.where(tile_mask[front_id][:, None, :, None] == 1, entries, 0.0)
        for child_id in range(CHILDREN):
            weight = (child_parent[child_id] == front_id).astype(jnp.float32)
            positions = child_index[child_id].astype(jnp.int32)
            added = jnp.transpose(children_tiles[child_id], (0, 2, 1, 3)) * weight
            front_tiles = front_tiles.at[positions[:, None], :, positions[None, :], :].add(added)
        flat_front = front_tiles.reshape(order_total, order_total)
        flat_front = flat_front.at[diagonal_ids, diagonal_ids].add(diag_boost[front_id].reshape(order_total))
        front_tiles = eliminate(flat_front.reshape(PARENT_TILES, TILE_ROWS, PARENT_TILES, TILE_ROWS))
        results.append(front_tiles.reshape(LOCAL_ROWS, GRID_ROWS, TILE_ROWS, LOCAL_COLS, GRID_COLS, TILE_ROWS))
    return jnp.stack(results, axis=0)
```

```python
import jax
import jax.numpy as jnp
from jax import lax
from jax.experimental import pallas as pl
from jax.experimental.pallas import tpu as pltpu
from jax.sharding import PartitionSpec as P

PANELS = 4
BLOCK = 128
HIGHEST = lax.Precision.HIGHEST
ROWS_BY_ROWS = (((1,), (1,)), ((), ()))
ROWS_BY_COLUMNS = (((1,), (0,)), ((), ()))


def times(left, right, numbers):
    return lax.dot_general(left, right, numbers, precision=HIGHEST, preferred_element_type=jnp.float32)


def over_lanes(value, lane):
    return jnp.broadcast_to(value[:, lane : lane + 1], value.shape)


def over_sublanes(value, sublane):
    return jnp.broadcast_to(value[sublane : sublane + 1, :], value.shape)


def factor_block(block):
    groups = BLOCK // 8
    row = lax.broadcasted_iota(jnp.int32, (8, BLOCK), 0)
    lane = lax.broadcasted_iota(jnp.int32, (8, BLOCK), 1)
    rest = [block[8 * g : 8 * g + 8, :] for g in range(groups)]
    extra = [jnp.where(lane == row + 8 * g, 1.0, 0.0).astype(jnp.float32) for g in range(groups)]
    upper, inverse = [], []
    for g in range(groups):
        base = 8 * g
        raw = [[over_lanes(rest[h], base + k) for k in range(8)] for h in range(g, groups)]
        small = [[over_sublanes(raw[0][k], i) if i >= k else None for k in range(8)] for i in range(8)]
        scale = []
        for k in range(8):
            inv = lax.rsqrt(small[k][k])
            inv = inv * (1.5 - 0.5 * small[k][k] * inv * inv)
            scale.append(inv)
            for i in range(k + 1, 8):
                small[i][k] = small[i][k] * inv
            for j in range(k + 1, 8):
                for i in range(j, 8):
                    small[i][j] = small[i][j] - small[i][k] * small[j][k]

        def forward(parts, small=small, scale=scale):
            done = []
            for k in range(8):
                part = parts[k]
                for m in range(k):
                    part = part - small[k][m] * done[m]
                done.append(part * scale[k])
            return done

        wide = forward([over_sublanes(rest[g], k) for k in range(8)])
        solved = forward([over_sublanes(extra[g], k) for k in range(8)])
        upper_rows, inverse_rows = wide[0], solved[0]
        for k in range(1, 8):
            upper_rows = jnp.where(row == k, wide[k], upper_rows)
            inverse_rows = jnp.where(row == k, solved[k], inverse_rows)
        upper.append(jnp.where(lane >= row + base, upper_rows, 0.0))
        inverse.append(inverse_rows)
        for h in range(g + 1, groups):
            tall = forward(raw[h - g])
            for k in range(8):
                rest[h] = rest[h] - tall[k] * wide[k]
                extra[h] = extra[h] - tall[k] * solved[k]
    return jnp.concatenate(upper, 0), jnp.concatenate(inverse, 0)


def factor_kernel(top_ref, held_ref, diagonal_ref):
    blocks = held_ref.shape[0] // BLOCK
    held_ref[...] = top_ref[...]
    row = lax.broadcasted_iota(jnp.int32, (BLOCK, BLOCK), 0)
    col = lax.broadcasted_iota(jnp.int32, (BLOCK, BLOCK), 1)

    @pl.loop(0, blocks)
    def _(k):
        here = pl.ds(pl.multiple_of(k * BLOCK, BLOCK), BLOCK)
        block = held_ref[here, here]
        block = jnp.where(row >= col, block, 0.0) + jnp.where(col > row, jnp.where(row > col, block, 0.0).T, 0.0)
        upper, inverse = factor_block(block)
        diagonal_ref[here, :] = upper.T

        @pl.loop(k + 1, blocks)
        def _(j):
            held_ref[here, pl.ds(pl.multiple_of(j * BLOCK, BLOCK), BLOCK)] = jnp.zeros((BLOCK, BLOCK), jnp.float32)

        held_ref[here, here] = jnp.where(row == col, 1.0, 0.0).astype(jnp.float32)
        held_ref[:, here] = times(held_ref[:, here], inverse, ROWS_BY_ROWS)

        @pl.loop(k + 1, blocks)
        def _(j):
            there = pl.ds(pl.multiple_of(j * BLOCK, BLOCK), BLOCK)
            held_ref[:, there] = held_ref[:, there] - times(held_ref[:, here], held_ref[there, here], ROWS_BY_ROWS)


def factor(top):
    order = top.shape[0]
    whole = pl.BlockSpec(memory_space=pltpu.VMEM)
    return pl.pallas_call(
        factor_kernel,
        out_shape=(
            jax.ShapeDtypeStruct((order, order), jnp.float32),
            jax.ShapeDtypeStruct((order, BLOCK), jnp.float32),
        ),
        in_specs=[whole],
        out_specs=(whole, whole),
        compiler_params=pltpu.CompilerParams(vmem_limit_bytes=40 * 2**20),
        cost_estimate=pl.CostEstimate(flops=50 * 10**9, bytes_accessed=16 * 2**20, transcendentals=1024),
        name="factor",
    )(top)


def body(front_entries, child_updates, diag_boost, tile_mask, child_parent, child_index):
    grid_rows = lax.axis_size("row")
    grid_cols = lax.axis_size("col")
    groups = lax.axis_size("front")
    my_group = lax.axis_index("front")
    my_row = lax.axis_index("row")
    my_col = lax.axis_index("col")
    local_rows = front_entries.shape[1]
    slices = front_entries.shape[2]
    local_cols = front_entries.shape[7]
    size = front_entries.shape[8]
    held = child_updates.shape[0]
    child_tiles = child_updates.shape[1]
    halves = grid_rows // grid_cols
    order = PANELS * size

    pieces = child_updates.reshape(held, child_tiles, slices, child_tiles, size)
    parents = child_parent.reshape(groups, held)
    mine = lax.dynamic_index_in_dim(parents, my_group, 0, keepdims=False)
    goes = (mine[None, :] == jnp.arange(groups)[:, None])[:, :, None, None, None, None]
    slots = jnp.sum(jnp.where(goes, pieces[None], 0.0), axis=1)
    arrived = lax.all_to_all(slots, "front", split_axis=0, concat_axis=0, tiled=True)
    comes = parents == my_group
    index = jnp.sum(jnp.where(comes[:, :, None], child_index.reshape(groups, held, child_tiles), 0), axis=1)
    weight = jnp.any(comes, axis=1).astype(jnp.float32)

    entries = front_entries.reshape(local_rows, slices, grid_rows, grid_cols, local_cols, size)
    mask_tiles = jnp.transpose(tile_mask[0].reshape(local_rows, grid_rows, local_cols, grid_cols), (0, 1, 3, 2))
    masked = jnp.where(mask_tiles[:, None, :, :, :, None] == 1, entries, 0.0)
    row_ids = jnp.arange(local_rows)[:, None] * grid_rows + jnp.arange(grid_rows)[None, :]
    col_ids = jnp.arange(local_cols)[:, None] * grid_cols + jnp.arange(grid_cols)[None, :]
    row_hits = (index[:, None, None, :] == row_ids[None, :, :, None]).astype(jnp.float32) * weight[:, None, None, None]
    col_hits = (index[:, None, None, :] == col_ids[None, :, :, None]).astype(jnp.float32)
    spread = jnp.einsum("naube,ntpb->nautpe", arrived, col_hits, precision=HIGHEST)
    assembled = masked + jnp.einsum("niqa,nautpe->iuqpte", row_hits, spread, precision=HIGHEST)

    panel = assembled[:, :, :, :PANELS, 0, :]
    within = jnp.arange(slices) * grid_rows * grid_cols + my_row * grid_cols + my_col
    boost = jnp.where(
        within[:, None, None, None] == jnp.arange(size),
        jnp.where(jnp.eye(PANELS, dtype=bool)[:, :, None], diag_boost[0, :PANELS, None, :], 0.0),
        0.0,
    )
    panel = panel.at[0, :, :PANELS].add(boost)

    top = jnp.transpose(panel[0, :, :PANELS], (1, 0, 2, 3)).reshape(PANELS * slices, order)
    gathered = lax.all_gather(top, ("row", "col"), axis=0)
    top_block = jnp.transpose(gathered, (1, 0, 2)).reshape(order, order)

    assembled, panel, top_block = lax.optimization_barrier((assembled, panel, top_block))
    joined = assembled.reshape(local_rows, slices, grid_rows * grid_cols, local_cols, size)
    relaid = lax.all_to_all(joined, ("row", "col"), split_axis=2, concat_axis=2, tiled=True)
    tiles = relaid.reshape(local_rows, size, local_cols, size)

    for_rows = lax.all_to_all(panel, "row", split_axis=2, concat_axis=2, tiled=True)
    for_rows = lax.all_gather(for_rows, "col", axis=3)
    row_panel = for_rows.reshape(local_rows * size, order)
    split = panel.reshape(local_rows, slices, halves, grid_cols, PANELS, size)
    for_cols = lax.all_to_all(split, "col", split_axis=3, concat_axis=3, tiled=True)
    for_cols = jnp.transpose(for_cols, (0, 2, 1, 3, 4, 5))
    for_cols = lax.all_gather(for_cols, "row", axis=3)
    col_panel = for_cols.reshape(local_cols, size, order)

    both, diagonal = factor(top_block)
    block_row = jnp.arange(order)[:, None] // BLOCK
    block_col = jnp.arange(order)[None, :] // BLOCK
    lower = jnp.where(block_row > block_col, both, 0.0)
    lower = jnp.where(block_row == block_col, jnp.tile(diagonal, (1, order // BLOCK)), lower)
    inverse = jnp.where(block_row > block_col, 0.0, both)

    solved = times(row_panel, inverse, ROWS_BY_COLUMNS).reshape(local_rows, size, order)
    own = lax.dynamic_slice_in_dim(lower, jnp.minimum(my_row, PANELS - 1) * size, size, 0)
    solved = solved.at[0].set(jnp.where(my_row < PANELS, own, solved[0]))
    tile_ids = jnp.arange(local_rows) * grid_rows + my_row
    panel_ids = jnp.arange(order) // size
    update = jnp.where(tile_ids[:, None, None] > panel_ids[None, None, :], solved, 0.0)
    both_sides = times(update.reshape(local_rows * size, order), inverse, ROWS_BY_ROWS)

    change = lax.dot_general(
        both_sides, col_panel, (((1,), (2,)), ((), ())), precision=HIGHEST, preferred_element_type=jnp.float32
    )
    tiles = tiles - change.reshape(local_rows, size, local_cols, size)
    global_rows = jnp.arange(local_rows) * grid_rows + my_row
    global_cols = jnp.arange(local_cols) * grid_cols + my_col
    boosts = jnp.take(diag_boost[0], global_rows, axis=0)
    on_diagonal = global_rows[:, None] == global_cols[None, :]
    placed = on_diagonal[:, None, :, None] & jnp.eye(size, dtype=bool)[None, :, None, :]
    tiles = tiles + jnp.where(placed, boosts[:, :, None, None], 0.0)
    column = lax.dynamic_slice_in_dim(solved, jnp.minimum(my_col, PANELS - 1) * size, size, 2)
    tiles = tiles.at[:, :, 0, :].set(jnp.where(my_col < PANELS, column, tiles[:, :, 0, :]))
    return tiles.reshape(1, local_rows, 1, size, local_cols, 1, size)


def solution(mesh):
    placed = (
        P("front", None, None, "row", "col", None, None, None, None),
        P("front", None, None, "row", "col", None, None),
        P("front", None, None),
        P("front", None, None),
        P(),
        P(),
    )
    return jax.shard_map(
        body,
        mesh=mesh,
        in_specs=placed,
        out_specs=P("front", None, "row", None, None, "col", None),
        check_vma=False,
    )
```

```python
import functools

import jax
import jax.numpy as jnp
from jax import lax
from jax.experimental import pallas as pl
from jax.experimental.pallas import tpu as pltpu
from jax.sharding import PartitionSpec as P

PANELS = 4
BLOCK = 128
HIGHEST = lax.Precision.HIGHEST
ROWS_BY_ROWS = (((1,), (1,)), ((), ()))
ROWS_BY_COLUMNS = (((1,), (0,)), ((), ()))
WHOLE = pl.BlockSpec(memory_space=pltpu.VMEM)
SCALARS = pl.BlockSpec(memory_space=pltpu.SMEM)


def times(left, right, numbers):
    return lax.dot_general(left, right, numbers, precision=HIGHEST, preferred_element_type=jnp.float32)


def parts_of(value):
    high = value.astype(jnp.bfloat16)
    return high, (value - high.astype(jnp.float32)).astype(jnp.bfloat16)


def times_parts(left, right, numbers):
    pairs = ((left[0], right[0]), (left[0], right[1]), (left[1], right[0]))
    products = [lax.dot_general(x, y, numbers, preferred_element_type=jnp.float32) for x, y in pairs]
    return products[0] + (products[1] + products[2])


def over_lanes(value, lane):
    return jnp.broadcast_to(value[:, lane : lane + 1], value.shape)


def over_sublanes(value, sublane):
    return jnp.broadcast_to(value[sublane : sublane + 1, :], value.shape)


def factor_block(block):
    groups = BLOCK // 8
    row = lax.broadcasted_iota(jnp.int32, (8, BLOCK), 0)
    lane = lax.broadcasted_iota(jnp.int32, (8, BLOCK), 1)
    rest = [block[8 * g : 8 * g + 8, :] for g in range(groups)]
    extra = [jnp.where(lane == row + 8 * g, 1.0, 0.0).astype(jnp.float32) for g in range(groups)]
    upper, inverse = [], []
    for g in range(groups):
        base = 8 * g
        raw = [[over_lanes(rest[h], base + k) for k in range(8)] for h in range(g, groups)]
        small = [[over_sublanes(raw[0][k], i) if i >= k else None for k in range(8)] for i in range(8)]
        scale = []
        for k in range(8):
            inv = lax.rsqrt(small[k][k])
            inv = inv * (1.5 - 0.5 * small[k][k] * inv * inv)
            scale.append(inv)
            for i in range(k + 1, 8):
                small[i][k] = small[i][k] * inv
            for j in range(k + 1, 8):
                for i in range(j, 8):
                    small[i][j] = small[i][j] - small[i][k] * small[j][k]

        def forward(parts, small=small, scale=scale):
            done = []
            for k in range(8):
                part = parts[k]
                for m in range(k):
                    part = part - small[k][m] * done[m]
                done.append(part * scale[k])
            return done

        wide = forward([over_sublanes(rest[g], k) for k in range(8)])
        solved = forward([over_sublanes(extra[g], k) for k in range(8)])
        upper_rows, inverse_rows = wide[0], solved[0]
        for k in range(1, 8):
            upper_rows = jnp.where(row == k, wide[k], upper_rows)
            inverse_rows = jnp.where(row == k, solved[k], inverse_rows)
        upper.append(jnp.where(lane >= row + base, upper_rows, 0.0))
        inverse.append(inverse_rows)
        for h in range(g + 1, groups):
            tall = forward(raw[h - g])
            for k in range(8):
                rest[h] = rest[h] - tall[k] * wide[k]
                extra[h] = extra[h] - tall[k] * solved[k]
    return jnp.concatenate(upper, 0), jnp.concatenate(inverse, 0)


def lower_pairs(blocks):
    return [(m, n) for m in range(blocks) for n in range(m + 1)]


def factor_kernel(packed_ref, lower_ref, inverse_ref, held_ref, diagonal_ref):
    blocks = held_ref.shape[0] // BLOCK
    row = lax.broadcasted_iota(jnp.int32, (BLOCK, BLOCK), 0)
    col = lax.broadcasted_iota(jnp.int32, (BLOCK, BLOCK), 1)
    zeros = jnp.zeros((BLOCK, BLOCK), jnp.float32)

    def at(ref, m, n):
        return ref.at[m * BLOCK : (m + 1) * BLOCK, n * BLOCK : (n + 1) * BLOCK]

    for place, (m, n) in enumerate(lower_pairs(blocks)):
        at(held_ref, m, n)[...] = packed_ref[:, place * BLOCK : (place + 1) * BLOCK]
        if m > n:
            at(held_ref, n, m)[...] = zeros

    @pl.loop(0, blocks)
    def _(k):
        here = pl.ds(pl.multiple_of(k * BLOCK, BLOCK), BLOCK)
        block = held_ref[here, here]
        block = jnp.where(row >= col, block, 0.0) + jnp.where(col > row, jnp.where(row > col, block, 0.0).T, 0.0)
        upper, inverse = factor_block(block)
        diagonal_ref[here, :] = upper.T

        @pl.loop(k + 1, blocks)
        def _(j):
            held_ref[here, pl.ds(pl.multiple_of(j * BLOCK, BLOCK), BLOCK)] = zeros

        held_ref[here, here] = jnp.where(row == col, 1.0, 0.0).astype(jnp.float32)
        held_ref[:, here] = times(held_ref[:, here], inverse, ROWS_BY_ROWS)

        @pl.loop(k + 1, blocks)
        def _(j):
            there = pl.ds(pl.multiple_of(j * BLOCK, BLOCK), BLOCK)
            held_ref[:, there] = held_ref[:, there] - times(held_ref[:, here], held_ref[there, here], ROWS_BY_ROWS)

    for m, n in lower_pairs(blocks):
        if m > n:
            at(lower_ref, m, n)[...] = at(held_ref, m, n)[...]
            at(lower_ref, n, m)[...] = zeros
            at(inverse_ref, n, m)[...] = at(held_ref, n, m)[...]
            at(inverse_ref, m, n)[...] = zeros
        else:
            at(lower_ref, m, m)[...] = diagonal_ref[m * BLOCK : (m + 1) * BLOCK, :]
            at(inverse_ref, m, m)[...] = at(held_ref, m, m)[...]


def factor(packed, order):
    square = jax.ShapeDtypeStruct((order, order), jnp.float32)
    return pl.pallas_call(
        factor_kernel,
        out_shape=(square, square),
        in_specs=[WHOLE],
        out_specs=(WHOLE, WHOLE),
        scratch_shapes=[pltpu.VMEM((order, order), jnp.float32), pltpu.VMEM((order, BLOCK), jnp.float32)],
        compiler_params=pltpu.CompilerParams(vmem_limit_bytes=40 * 2**20),
        cost_estimate=pl.CostEstimate(flops=50 * 10**9, bytes_accessed=16 * 2**20, transcendentals=1024),
        name="factor",
    )(packed)


def solve_kernel(grid_rows, place_ref, rows_ref, lower_ref, inverse_ref, solved_ref, sides_ref):
    total, order = solved_ref.shape
    size = order // PANELS
    per = size // BLOCK
    my_row = place_ref[0]
    inverse = [
        [parts_of(inverse_ref[j * size : (j + 1) * size, k * size : (k + 1) * size]) if k >= j else None for k in range(PANELS)]
        for j in range(PANELS)
    ]
    rows = [parts_of(jnp.concatenate([rows_ref[per * k + h] for h in range(per)], axis=1)) for k in range(PANELS)]
    for k in range(PANELS):
        total_k = times_parts(rows[0], inverse[0][k], ROWS_BY_COLUMNS)
        for j in range(1, k + 1):
            total_k = total_k + times_parts(rows[j], inverse[j][k], ROWS_BY_COLUMNS)
        solved_ref[:, k * size : (k + 1) * size] = total_k

    @pl.when(my_row < PANELS)
    def _():
        solved_ref[0:size, :] = lower_ref[pl.ds(pl.multiple_of(my_row * size, size), size), :]

    tile = lax.broadcasted_iota(jnp.int32, (total, size), 0) // size * grid_rows + my_row
    used = [parts_of(jnp.where(tile > k, solved_ref[:, k * size : (k + 1) * size], 0.0)) for k in range(PANELS)]
    for j in range(PANELS):
        total_j = times_parts(used[j], inverse[j][j], ROWS_BY_ROWS)
        for k in range(j + 1, PANELS):
            total_j = total_j + times_parts(used[k], inverse[j][k], ROWS_BY_ROWS)
        sides_ref[:, j * size : (j + 1) * size] = total_j


def solve(place, rows, lower, inverse, grid_rows):
    out = jax.ShapeDtypeStruct((rows.shape[1], lower.shape[0]), jnp.float32)
    return pl.pallas_call(
        functools.partial(solve_kernel, grid_rows),
        out_shape=(out, out),
        in_specs=[SCALARS, WHOLE, WHOLE, WHOLE],
        out_specs=(WHOLE, WHOLE),
        compiler_params=pltpu.CompilerParams(vmem_limit_bytes=48 * 2**20),
        cost_estimate=pl.CostEstimate(flops=8 * 10**9, bytes_accessed=14 * 2**20, transcendentals=0),
        name="solve",
    )(place, rows, lower, inverse)


def finish_kernel(grid_rows, grid_cols, place_ref, tiles_ref, sides_ref, across_ref, solved_ref, boost_ref, out_ref):
    t = pl.program_id(0)
    my_row, my_col = place_ref[0], place_ref[1]
    size = boost_ref.shape[2]
    halves = size // BLOCK
    local_rows = sides_ref.shape[0] // size
    lines = tiles_ref.shape[0] // BLOCK
    per = lines // (local_rows * halves)
    order = sides_ref.shape[1]
    across = jnp.concatenate([across_ref[:, u].reshape(BLOCK, order) for u in range(halves)], axis=0)
    change = times_parts(parts_of(sides_ref[...]), parts_of(across), ROWS_BY_ROWS)
    row = lax.broadcasted_iota(jnp.int32, (BLOCK, BLOCK), 0)
    col = lax.broadcasted_iota(jnp.int32, (BLOCK, BLOCK), 1)
    in_panel = jnp.logical_and(t == 0, my_col < PANELS)
    for i in range(local_rows):
        on_diagonal = i * grid_rows + my_row == t * grid_cols + my_col
        for u in range(halves):
            for h in range(halves):
                start = i * size + u * BLOCK
                value = tiles_ref[pl.ds((i * halves + u) * per + t * halves + h, BLOCK, stride=lines), :]
                value = value - change[start : start + BLOCK, h * BLOCK : (h + 1) * BLOCK]
                if u == h:
                    line = boost_ref[i * grid_rows + my_row][:, h * BLOCK : (h + 1) * BLOCK]
                    value = value + jnp.where(jnp.logical_and(on_diagonal, row == col), line, 0.0)
                lane = pl.multiple_of(jnp.minimum(my_col, PANELS - 1) * size + h * BLOCK, BLOCK)
                value = jnp.where(in_panel, solved_ref[start : start + BLOCK, pl.ds(lane, BLOCK)], value)
                out_ref[pl.ds(start * per + t * halves + h, BLOCK, stride=per), :] = value


def finish(place, tiles, sides, across, solved, boost, grid_rows, grid_cols):
    ranks, lines, cols, order = across.shape
    halves = boost.shape[2] // BLOCK
    steps = lines // halves

    def still(*shape):
        return pl.BlockSpec(shape, lambda t: (0,) * len(shape))

    return pl.pallas_call(
        functools.partial(finish_kernel, grid_rows, grid_cols),
        grid=(steps,),
        out_shape=jax.ShapeDtypeStruct(tiles.shape, jnp.float32),
        in_specs=[
            SCALARS,
            still(*tiles.shape),
            still(*sides.shape),
            pl.BlockSpec((ranks, halves, cols, order), lambda t: (0, t, 0, 0)),
            still(*solved.shape),
            still(*boost.shape),
        ],
        out_specs=still(*tiles.shape),
        compiler_params=pltpu.CompilerParams(vmem_limit_bytes=48 * 2**20),
        cost_estimate=pl.CostEstimate(flops=4 * 10**9, bytes_accessed=12 * 2**20, transcendentals=0),
        name="finish",
    )(place, tiles, sides, across, solved, boost)


def body(front_entries, child_updates, diag_boost, tile_mask, child_parent, child_index):
    grid_rows = lax.axis_size("row")
    grid_cols = lax.axis_size("col")
    groups = lax.axis_size("front")
    my_group = lax.axis_index("front")
    my_row = lax.axis_index("row")
    my_col = lax.axis_index("col")
    local_rows = front_entries.shape[1]
    slices = front_entries.shape[2]
    local_cols = front_entries.shape[7]
    size = front_entries.shape[8]
    held = child_updates.shape[0]
    child_tiles = child_updates.shape[1]
    halves = grid_rows // grid_cols
    order = PANELS * size

    pieces = child_updates.reshape(held, child_tiles, slices, child_tiles, size)
    parents = child_parent.reshape(groups, held)
    mine = lax.dynamic_index_in_dim(parents, my_group, 0, keepdims=False)
    goes = (mine[None, :] == jnp.arange(groups)[:, None])[:, :, None, None, None, None]
    slots = jnp.sum(jnp.where(goes, pieces[None], 0.0), axis=1)
    arrived = lax.all_to_all(slots, "front", split_axis=0, concat_axis=0, tiled=True)
    comes = parents == my_group
    index = jnp.sum(jnp.where(comes[:, :, None], child_index.reshape(groups, held, child_tiles), 0), axis=1)
    weight = jnp.any(comes, axis=1).astype(jnp.float32)

    entries = front_entries.reshape(local_rows, slices, grid_rows, grid_cols, local_cols, size)
    mask_tiles = jnp.transpose(tile_mask[0].reshape(local_rows, grid_rows, local_cols, grid_cols), (0, 1, 3, 2))
    kept = (mask_tiles == 1)[:, None, :, :, :, None]
    row_ids = jnp.arange(local_rows)[:, None] * grid_rows + jnp.arange(grid_rows)[None, :]
    col_ids = jnp.arange(local_cols)[:, None] * grid_cols + jnp.arange(grid_cols)[None, :]
    row_hits = (index[:, None, None, :] == row_ids[None, :, :, None]).astype(jnp.float32) * weight[:, None, None, None]
    col_hits = (index[:, None, None, :] == col_ids[None, :, :, None]).astype(jnp.float32)
    first = index[:, :PANELS, None] == jnp.arange(PANELS)
    narrow = jnp.sum(
        jnp.where(first[:, None, None, :, :, None], arrived[:, :, :, :PANELS, None, :], 0.0), axis=3
    )
    panel = jnp.where(kept[:, :, :, :PANELS, 0], entries[:, :, :, :PANELS, 0, :], 0.0)
    panel = panel + jnp.einsum("niqa,nauke->iuqke", row_hits, narrow, precision=HIGHEST)
    within = jnp.arange(slices) * grid_rows * grid_cols + my_row * grid_cols + my_col
    boost = jnp.where(
        within[:, None, None, None] == jnp.arange(size),
        jnp.where(jnp.eye(PANELS, dtype=bool)[:, :, None], diag_boost[0, :PANELS, None, :], 0.0),
        0.0,
    )
    panel = panel.at[0, :, :PANELS].add(boost)

    blocks = order // BLOCK
    top = jnp.transpose(panel[0, :, :PANELS], (1, 0, 2, 3)).reshape(blocks, order)
    packed = jnp.concatenate([top[m, : (m + 1) * BLOCK] for m in range(blocks)])
    over_row = lax.all_gather(packed, "row", axis=0)

    split = panel.reshape(local_rows, slices, halves, grid_cols, order)
    split = jnp.transpose(split, (3, 0, 2, 1, 4)).reshape(grid_cols, local_cols * slices, 1, order)
    for_cols = lax.all_to_all(split, "col", split_axis=0, concat_axis=2, tiled=True)
    for_cols = for_cols.reshape(local_cols * slices, grid_cols, order)
    lines = jnp.transpose(panel.reshape(local_rows, slices, grid_rows, grid_cols, BLOCK), (2, 3, 0, 1, 4))
    lines = lines.reshape(grid_rows * grid_cols, local_rows * slices, BLOCK)
    for_rows = lax.all_to_all(lines, ("row", "col"), split_axis=0, concat_axis=0, tiled=True)
    for_rows = jnp.transpose(for_rows, (1, 0, 2)).reshape(local_rows * size, BLOCK)

    spread = jnp.einsum("naube,ntpb->nautpe", arrived, col_hits, precision=HIGHEST)
    assembled = jnp.where(kept, entries, 0.0) + jnp.einsum("niqa,nautpe->iuqpte", row_hits, spread, precision=HIGHEST)
    joined = jnp.transpose(assembled, (2, 3, 0, 1, 4, 5))
    joined = joined.reshape(grid_rows * grid_cols, local_rows * slices, local_cols * size // BLOCK, BLOCK)

    over_row, joined, for_cols = lax.optimization_barrier((over_row, joined, for_cols))
    across = lax.all_gather(for_cols, "row", axis=0)
    copies = jnp.broadcast_to(over_row[None], (grid_cols,) + over_row.shape)
    over_both = lax.all_to_all(copies, "col", split_axis=0, concat_axis=0, tiled=True)
    over_both = jnp.transpose(over_both, (1, 0, 2)).reshape(grid_rows * grid_cols, packed.shape[0])
    copies = jnp.broadcast_to(for_rows[None], (grid_cols,) + for_rows.shape)
    row_panel = lax.all_to_all(copies, "col", split_axis=0, concat_axis=0, tiled=True)
    tiles = lax.all_to_all(joined, ("row", "col"), split_axis=0, concat_axis=0, tiled=True)
    tiles = tiles.reshape(-1, BLOCK)

    place = jnp.stack([my_row, my_col]).astype(jnp.int32)
    lower, inverse = factor(over_both, order)
    solved, sides = solve(place, row_panel, lower, inverse, grid_rows)
    out = finish(place, tiles, sides, across, solved, diag_boost[0][:, None, :], grid_rows, grid_cols)
    return out.reshape(1, local_rows, 1, size, local_cols, 1, size)


def solution(mesh):
    placed = (
        P("front", None, None, "row", "col", None, None, None, None),
        P("front", None, None, "row", "col", None, None),
        P("front", None, None),
        P("front", None, None),
        P(),
        P(),
    )
    return jax.shard_map(
        body,
        mesh=mesh,
        in_specs=placed,
        out_specs=P("front", None, "row", None, None, "col", None),
        check_vma=False,
    )
```

```python
import functools

import jax
import jax.numpy as jnp
from jax import lax
from jax.experimental import pallas as pl
from jax.experimental.pallas import tpu as pltpu
from jax.sharding import PartitionSpec as P

PANELS = 4
BLOCK = 128
HIGHEST = lax.Precision.HIGHEST
ROWS_BY_ROWS = (((1,), (1,)), ((), ()))
ROWS_BY_COLUMNS = (((1,), (0,)), ((), ()))
WHOLE = pl.BlockSpec(memory_space=pltpu.VMEM)
SCALARS = pl.BlockSpec(memory_space=pltpu.SMEM)


def times(left, right, numbers):
    return lax.dot_general(left, right, numbers, precision=HIGHEST, preferred_element_type=jnp.float32)


def parts_of(value):
    high = value.astype(jnp.bfloat16)
    return high, (value - high.astype(jnp.float32)).astype(jnp.bfloat16)


def times_parts(left, right, numbers):
    pairs = ((left[0], right[0]), (left[0], right[1]), (left[1], right[0]))
    products = [lax.dot_general(x, y, numbers, preferred_element_type=jnp.float32) for x, y in pairs]
    return products[0] + (products[1] + products[2])


def over_lanes(value, lane):
    return jnp.broadcast_to(value[:, lane : lane + 1], value.shape)


def over_sublanes(value, sublane):
    return jnp.broadcast_to(value[sublane : sublane + 1, :], value.shape)


def factor_block(block):
    groups = BLOCK // 8
    row = lax.broadcasted_iota(jnp.int32, (8, BLOCK), 0)
    lane = lax.broadcasted_iota(jnp.int32, (8, BLOCK), 1)
    rest = [block[8 * g : 8 * g + 8, :] for g in range(groups)]
    extra = [jnp.where(lane == row + 8 * g, 1.0, 0.0).astype(jnp.float32) for g in range(groups)]
    upper, inverse = [], []
    for g in range(groups):
        base = 8 * g
        raw = [[over_lanes(rest[h], base + k) for k in range(8)] for h in range(g, groups)]
        small = [[over_sublanes(raw[0][k], i) if i >= k else None for k in range(8)] for i in range(8)]
        scale = []
        for k in range(8):
            inv = lax.rsqrt(small[k][k])
            inv = inv * (1.5 - 0.5 * small[k][k] * inv * inv)
            scale.append(inv)
            for i in range(k + 1, 8):
                small[i][k] = small[i][k] * inv
            for j in range(k + 1, 8):
                for i in range(j, 8):
                    small[i][j] = small[i][j] - small[i][k] * small[j][k]

        def forward(parts, small=small, scale=scale):
            done = []
            for k in range(8):
                part = parts[k]
                for m in range(k):
                    part = part - small[k][m] * done[m]
                done.append(part * scale[k])
            return done

        wide = forward([over_sublanes(rest[g], k) for k in range(8)])
        solved = forward([over_sublanes(extra[g], k) for k in range(8)])
        upper_rows, inverse_rows = wide[0], solved[0]
        for k in range(1, 8):
            upper_rows = jnp.where(row == k, wide[k], upper_rows)
            inverse_rows = jnp.where(row == k, solved[k], inverse_rows)
        upper.append(jnp.where(lane >= row + base, upper_rows, 0.0))
        inverse.append(inverse_rows)
        for h in range(g + 1, groups):
            tall = forward(raw[h - g])
            for k in range(8):
                rest[h] = rest[h] - tall[k] * wide[k]
                extra[h] = extra[h] - tall[k] * solved[k]
    return jnp.concatenate(upper, 0), jnp.concatenate(inverse, 0)


def dealt_pairs(blocks):
    share = (blocks + 2) // 2
    dealt = [None] * blocks
    for a in range(blocks // 2):
        both = [(m, a) for m in range(a, blocks)] + [(m, blocks - 1 - a) for m in range(blocks - 1 - a, blocks)]
        dealt[a], dealt[blocks - 1 - a] = both[:share], both[share:]
    return [pairs + [(0, blocks - 1)] * (share - len(pairs)) for pairs in dealt]


def panel_kernel(grid_rows, index_ref, base_ref, narrow_ref, lines_ref, split_ref, rows_ref):
    groups, child_tiles = index_ref.shape
    total, blocks, _ = base_ref.shape
    slices = narrow_ref.shape[0] // (groups * child_tiles)
    local_rows = total // (slices * grid_rows)
    dealt = dealt_pairs(blocks)
    share = len(dealt[0])
    per = local_rows * slices + share
    rows_ref[...] = base_ref[...]
    for g in range(groups):
        for a in range(child_tiles):
            tile = index_ref[g, a]
            for u in range(slices):
                at = (tile // grid_rows * slices + u) * grid_rows + lax.rem(tile, grid_rows)
                rows_ref[at] = rows_ref[at] + narrow_ref[(g * child_tiles + a) * slices + u]
    for q in range(grid_rows):
        for line in range(local_rows * slices):
            lines_ref[pl.ds(q * blocks * per + line, blocks, stride=per), :] = rows_ref[line * grid_rows + q]
    for p in range(blocks):
        for j, (m, n) in enumerate(dealt[p]):
            value = rows_ref[m % slices * grid_rows + m // slices][n : n + 1, :]
            start = p * per + local_rows * slices + j
            lines_ref[pl.ds(start, grid_rows, stride=blocks * per), :] = jnp.broadcast_to(value, (grid_rows, BLOCK))
    halves = grid_rows // blocks
    for p in range(blocks):
        for i in range(local_rows):
            for h in range(halves):
                for u in range(slices):
                    split_ref[p, (i * halves + h) * slices + u] = rows_ref[(i * slices + u) * grid_rows + h * blocks + p]


def make_panel(index, base, narrow, grid_rows):
    total, blocks, _ = base.shape
    per = total // grid_rows + len(dealt_pairs(blocks)[0])
    return pl.pallas_call(
        functools.partial(panel_kernel, grid_rows),
        out_shape=(
            jax.ShapeDtypeStruct((grid_rows * blocks * per, BLOCK), jnp.float32),
            jax.ShapeDtypeStruct((blocks, total // blocks, blocks, BLOCK), jnp.float32),
        ),
        in_specs=[SCALARS, WHOLE, WHOLE],
        out_specs=(WHOLE, WHOLE),
        scratch_shapes=[pltpu.VMEM(base.shape, jnp.float32)],
        cost_estimate=pl.CostEstimate(flops=10**6, bytes_accessed=2 * 2**20, transcendentals=0),
        name="panel",
    )(index, base, narrow)


SOURCES = (0, 1, -1, 2)


def source_col(place_ref, step, core):
    chip = lax.rem(place_ref[1] // 2 - SOURCES[step] + 4, 4)
    mine = lax.rem(place_ref[1], 2)
    return chip * 2 + (mine if core == 0 else 1 - mine)


def factor_kernel(place_ref, pairs_ref, own_ref, other_ref, lower_ref, inverse_ref, held_ref, diagonal_ref):
    blocks = held_ref.shape[0] // BLOCK
    share = own_ref.shape[1]
    row = lax.broadcasted_iota(jnp.int32, (BLOCK, BLOCK), 0)
    col = lax.broadcasted_iota(jnp.int32, (BLOCK, BLOCK), 1)
    zeros = jnp.zeros((BLOCK, BLOCK), jnp.float32)

    def at(ref, m, n):
        return ref.at[m * BLOCK : (m + 1) * BLOCK, n * BLOCK : (n + 1) * BLOCK]

    for core, source in enumerate((own_ref, other_ref)):
        for step in range(len(SOURCES)):
            first = source_col(place_ref, step, core) * share
            for j in range(share):
                m, n = pairs_ref[0, first + j], pairs_ref[1, first + j]
                down = pl.ds(pl.multiple_of(m * BLOCK, BLOCK), BLOCK)
                along = pl.ds(pl.multiple_of(n * BLOCK, BLOCK), BLOCK)
                held_ref[down, along] = source[step, j]

    @pl.loop(0, blocks)
    def _(k):
        here = pl.ds(pl.multiple_of(k * BLOCK, BLOCK), BLOCK)
        block = held_ref[here, here]
        block = jnp.where(row >= col, block, 0.0) + jnp.where(col > row, jnp.where(row > col, block, 0.0).T, 0.0)
        upper, inverse = factor_block(block)
        diagonal_ref[here, :] = upper.T

        @pl.loop(k + 1, blocks)
        def _(j):
            held_ref[here, pl.ds(pl.multiple_of(j * BLOCK, BLOCK), BLOCK)] = zeros

        held_ref[here, here] = jnp.where(row == col, 1.0, 0.0).astype(jnp.float32)
        held_ref[:, here] = times(held_ref[:, here], inverse, ROWS_BY_ROWS)

        @pl.loop(k + 1, blocks)
        def _(j):
            there = pl.ds(pl.multiple_of(j * BLOCK, BLOCK), BLOCK)
            held_ref[:, there] = held_ref[:, there] - times(held_ref[:, here], held_ref[there, here], ROWS_BY_ROWS)

    for m, n in [(m, n) for m in range(blocks) for n in range(m + 1)]:
        if m > n:
            at(lower_ref, m, n)[...] = at(held_ref, m, n)[...]
            at(lower_ref, n, m)[...] = zeros
            at(inverse_ref, n, m)[...] = at(held_ref, n, m)[...]
            at(inverse_ref, m, n)[...] = zeros
        else:
            at(lower_ref, m, m)[...] = diagonal_ref[m * BLOCK : (m + 1) * BLOCK, :]
            at(inverse_ref, m, m)[...] = at(held_ref, m, m)[...]


def factor(place, own, other, order):
    square = jax.ShapeDtypeStruct((order, order), jnp.float32)
    pairs = [pair for dealt in dealt_pairs(order // BLOCK) for pair in dealt]
    pairs = jnp.asarray([[m for m, _ in pairs], [n for _, n in pairs]], jnp.int32)
    return pl.pallas_call(
        factor_kernel,
        out_shape=(square, square),
        in_specs=[SCALARS, SCALARS, WHOLE, WHOLE],
        out_specs=(WHOLE, WHOLE),
        scratch_shapes=[pltpu.VMEM((order, order), jnp.float32), pltpu.VMEM((order, BLOCK), jnp.float32)],
        compiler_params=pltpu.CompilerParams(vmem_limit_bytes=40 * 2**20),
        cost_estimate=pl.CostEstimate(flops=10**9, bytes_accessed=2**20, transcendentals=1024),
        name="factor",
    )(place, pairs, own, other)


def solve_kernel(grid_rows, place_ref, *refs):
    *sources, lower_ref, inverse_ref, solved_ref, sides_ref, rows_ref = refs
    total, order = solved_ref.shape
    size = order // PANELS
    per = size // BLOCK
    my_row = place_ref[0]
    for shift, source in enumerate(sources):
        rows_ref[lax.rem(place_ref[1] - shift + len(sources), len(sources))] = source[...]
    inverse = [
        [parts_of(inverse_ref[j * size : (j + 1) * size, k * size : (k + 1) * size]) if k >= j else None for k in range(PANELS)]
        for j in range(PANELS)
    ]
    rows = [parts_of(jnp.concatenate([rows_ref[per * k + h] for h in range(per)], axis=1)) for k in range(PANELS)]
    for k in range(PANELS):
        total_k = times_parts(rows[0], inverse[0][k], ROWS_BY_COLUMNS)
        for j in range(1, k + 1):
            total_k = total_k + times_parts(rows[j], inverse[j][k], ROWS_BY_COLUMNS)
        solved_ref[:, k * size : (k + 1) * size] = total_k

    @pl.when(my_row < PANELS)
    def _():
        solved_ref[0:size, :] = lower_ref[pl.ds(pl.multiple_of(my_row * size, size), size), :]

    tile = lax.broadcasted_iota(jnp.int32, (total, size), 0) // size * grid_rows + my_row
    used = [parts_of(jnp.where(tile > k, solved_ref[:, k * size : (k + 1) * size], 0.0)) for k in range(PANELS)]
    for j in range(PANELS):
        total_j = times_parts(used[j], inverse[j][j], ROWS_BY_ROWS)
        for k in range(j + 1, PANELS):
            total_j = total_j + times_parts(used[k], inverse[j][k], ROWS_BY_ROWS)
        sides_ref[:, j * size : (j + 1) * size] = total_j


def solve(place, rows, lower, inverse, grid_rows):
    out = jax.ShapeDtypeStruct((rows[0].shape[0], lower.shape[0]), jnp.float32)
    return pl.pallas_call(
        functools.partial(solve_kernel, grid_rows),
        out_shape=(out, out),
        in_specs=[SCALARS] + [WHOLE] * (len(rows) + 2),
        out_specs=(WHOLE, WHOLE),
        scratch_shapes=[pltpu.VMEM((len(rows),) + rows[0].shape, jnp.float32)],
        compiler_params=pltpu.CompilerParams(vmem_limit_bytes=48 * 2**20),
        cost_estimate=pl.CostEstimate(flops=8 * 10**9, bytes_accessed=14 * 2**20, transcendentals=0),
        name="solve",
    )(place, *rows, lower, inverse)


def finish_kernel(grid_rows, grid_cols, place_ref, tiles_ref, sides_ref, across_ref, solved_ref, boost_ref, out_ref):
    t = pl.program_id(0)
    my_row, my_col = place_ref[0], place_ref[1]
    size = boost_ref.shape[2]
    halves = size // BLOCK
    local_rows = sides_ref.shape[0] // size
    lines = tiles_ref.shape[0] // BLOCK
    per = lines // (local_rows * halves)
    order = sides_ref.shape[1]
    across = jnp.concatenate([across_ref[:, u].reshape(BLOCK, order) for u in range(halves)], axis=0)
    change = times_parts(parts_of(sides_ref[...]), parts_of(across), ROWS_BY_ROWS)
    row = lax.broadcasted_iota(jnp.int32, (BLOCK, BLOCK), 0)
    col = lax.broadcasted_iota(jnp.int32, (BLOCK, BLOCK), 1)
    in_panel = jnp.logical_and(t == 0, my_col < PANELS)
    for i in range(local_rows):
        on_diagonal = i * grid_rows + my_row == t * grid_cols + my_col
        for u in range(halves):
            for h in range(halves):
                start = i * size + u * BLOCK
                value = tiles_ref[pl.ds((i * halves + u) * per + t * halves + h, BLOCK, stride=lines), :]
                value = value - change[start : start + BLOCK, h * BLOCK : (h + 1) * BLOCK]
                if u == h:
                    line = boost_ref[i * grid_rows + my_row][:, h * BLOCK : (h + 1) * BLOCK]
                    value = value + jnp.where(jnp.logical_and(on_diagonal, row == col), line, 0.0)
                lane = pl.multiple_of(jnp.minimum(my_col, PANELS - 1) * size + h * BLOCK, BLOCK)
                value = jnp.where(in_panel, solved_ref[start : start + BLOCK, pl.ds(lane, BLOCK)], value)
                out_ref[pl.ds(start * per + t * halves + h, BLOCK, stride=per), :] = value


def finish(place, tiles, sides, across, solved, boost, grid_rows, grid_cols):
    ranks, lines, cols, order = across.shape
    halves = boost.shape[2] // BLOCK
    steps = lines // halves

    def still(*shape):
        return pl.BlockSpec(shape, lambda t: (0,) * len(shape))

    return pl.pallas_call(
        functools.partial(finish_kernel, grid_rows, grid_cols),
        grid=(steps,),
        out_shape=jax.ShapeDtypeStruct(tiles.shape, jnp.float32),
        in_specs=[
            SCALARS,
            still(*tiles.shape),
            still(*sides.shape),
            pl.BlockSpec((ranks, halves, cols, order), lambda t: (0, t, 0, 0)),
            still(*solved.shape),
            still(*boost.shape),
        ],
        out_specs=still(*tiles.shape),
        compiler_params=pltpu.CompilerParams(vmem_limit_bytes=48 * 2**20),
        cost_estimate=pl.CostEstimate(flops=4 * 10**9, bytes_accessed=12 * 2**20, transcendentals=0),
        name="finish",
    )(place, tiles, sides, across, solved, boost)


def body(front_entries, child_updates, diag_boost, tile_mask, child_parent, child_index):
    grid_rows = lax.axis_size("row")
    grid_cols = lax.axis_size("col")
    groups = lax.axis_size("front")
    my_group = lax.axis_index("front")
    my_row = lax.axis_index("row")
    my_col = lax.axis_index("col")
    local_rows = front_entries.shape[1]
    slices = front_entries.shape[2]
    local_cols = front_entries.shape[7]
    size = front_entries.shape[8]
    held = child_updates.shape[0]
    child_tiles = child_updates.shape[1]
    halves = grid_rows // grid_cols
    order = PANELS * size

    pieces = child_updates.reshape(held, child_tiles, slices, child_tiles, size)
    parents = child_parent.reshape(groups, held)
    mine = lax.dynamic_index_in_dim(parents, my_group, 0, keepdims=False)
    goes = (mine[None, :] == jnp.arange(groups)[:, None])[:, :, None, None, None, None]
    slots = jnp.sum(jnp.where(goes, pieces[None], 0.0), axis=1)
    arrived = lax.all_to_all(slots, "front", split_axis=0, concat_axis=0, tiled=True)
    comes = parents == my_group
    index = jnp.sum(jnp.where(comes[:, :, None], child_index.reshape(groups, held, child_tiles), 0), axis=1)
    weight = jnp.any(comes, axis=1).astype(jnp.float32)

    entries = front_entries.reshape(local_rows, slices, grid_rows, grid_cols, local_cols, size)
    mask_tiles = jnp.transpose(tile_mask[0].reshape(local_rows, grid_rows, local_cols, grid_cols), (0, 1, 3, 2))
    kept = (mask_tiles == 1)[:, None, :, :, :, None]
    row_ids = jnp.arange(local_rows)[:, None] * grid_rows + jnp.arange(grid_rows)[None, :]
    col_ids = jnp.arange(local_cols)[:, None] * grid_cols + jnp.arange(grid_cols)[None, :]
    row_hits = (index[:, None, None, :] == row_ids[None, :, :, None]).astype(jnp.float32) * weight[:, None, None, None]
    col_hits = (index[:, None, None, :] == col_ids[None, :, :, None]).astype(jnp.float32)
    first = index[:, :PANELS, None] == jnp.arange(PANELS)
    narrow = jnp.sum(
        jnp.where(first[:, None, None, :, :, None], arrived[:, :, :, :PANELS, None, :], 0.0), axis=3
    )
    narrow = narrow.reshape(-1, order // BLOCK, BLOCK) * jnp.repeat(weight, child_tiles * slices)[:, None, None]
    within = jnp.arange(slices) * grid_rows * grid_cols + my_row * grid_cols + my_col
    boost = jnp.where(
        within[:, None, None, None] == jnp.arange(size),
        jnp.where(jnp.eye(grid_rows, PANELS, dtype=bool)[:, :, None], diag_boost[0, :PANELS], 0.0),
        0.0,
    )
    boost = jnp.where((jnp.arange(local_rows) == 0)[:, None, None, None, None], boost, 0.0)
    base = jnp.where(kept[:, :, :, :PANELS, 0], entries[:, :, :, :PANELS, 0, :], 0.0) + boost
    lines, split = make_panel(index, base.reshape(-1, order // BLOCK, BLOCK), narrow, grid_rows)

    split = lax.all_to_all(split, "col", split_axis=0, concat_axis=0, tiled=True)
    for_cols = jnp.transpose(split, (1, 0, 2, 3)).reshape(local_cols * slices, grid_cols, order)

    lines = lines.reshape(grid_rows * grid_cols, -1, 1, BLOCK)
    lines, for_cols = lax.optimization_barrier((lines, for_cols))
    across = lax.all_gather(for_cols, "row", axis=0)
    lines = lax.all_to_all(lines, ("row", "col"), split_axis=0, concat_axis=0, tiled=True)
    lines = jnp.transpose(lines.reshape(grid_rows * grid_cols, -1, BLOCK), (1, 0, 2))
    for_rows, for_top = lines[: local_rows * slices].reshape(local_rows * size, BLOCK), lines[local_rows * slices :]

    spread = jnp.einsum("naube,ntpb->nautpe", arrived, col_hits, precision=HIGHEST)
    assembled = jnp.where(kept, entries, 0.0) + jnp.einsum("niqa,nautpe->iuqpte", row_hits, spread, precision=HIGHEST)
    joined = jnp.transpose(assembled, (2, 3, 0, 1, 4, 5))
    joined = joined.reshape(grid_rows * grid_cols, local_rows * slices, local_cols * size // BLOCK, BLOCK)

    for_top, joined = lax.optimization_barrier((for_top, joined))
    tiles = lax.all_to_all(joined, ("row", "col"), split_axis=0, concat_axis=0, tiled=True).reshape(-1, BLOCK)

    def over_chips(value):
        cols = range(grid_cols)
        moved = [lax.ppermute(value, "col", [(c, (c + 2 * d) % grid_cols) for c in cols]) for d in SOURCES[1:]]
        return jnp.stack([value] + moved)

    def over_cores(value):
        return lax.ppermute(value, "col", [(c, c ^ 1) for c in range(grid_cols)])

    place = jnp.stack([my_row, my_col]).astype(jnp.int32)
    own_top = over_chips(for_top)
    own_top, for_rows = lax.optimization_barrier((own_top, for_rows))
    rows = [for_rows]
    for shift in range(1, grid_cols):
        rows.append(lax.ppermute(for_rows, "col", [(c, (c + shift) % grid_cols) for c in range(grid_cols)]))
    other_top = over_cores(own_top)
    lower, inverse = factor(place, own_top, other_top, order)
    solved, sides = solve(place, rows, lower, inverse, grid_rows)
    out = finish(place, tiles, sides, across, solved, diag_boost[0][:, None, :], grid_rows, grid_cols)
    return out.reshape(1, local_rows, 1, size, local_cols, 1, size)


def solution(mesh):
    placed = (
        P("front", None, None, "row", "col", None, None, None, None),
        P("front", None, None, "row", "col", None, None),
        P("front", None, None),
        P("front", None, None),
        P(),
        P(),
    )
    return jax.shard_map(
        body,
        mesh=mesh,
        in_specs=placed,
        out_specs=P("front", None, "row", None, None, "col", None),
        check_vma=False,
    )
```

```python
import functools

import jax
import jax.numpy as jnp
from jax import lax
from jax.experimental import pallas as pl
from jax.experimental.pallas import tpu as pltpu
from jax.sharding import PartitionSpec as P

PANELS = 4
BLOCK = 128
HIGHEST = lax.Precision.HIGHEST
ROWS_BY_ROWS = (((1,), (1,)), ((), ()))
ROWS_BY_COLUMNS = (((1,), (0,)), ((), ()))
WHOLE = pl.BlockSpec(memory_space=pltpu.VMEM)
SCALARS = pl.BlockSpec(memory_space=pltpu.SMEM)


def times(left, right, numbers):
    return lax.dot_general(left, right, numbers, precision=HIGHEST, preferred_element_type=jnp.float32)


def parts_of(value):
    high = value.astype(jnp.bfloat16)
    return high, (value - high.astype(jnp.float32)).astype(jnp.bfloat16)


def times_parts(left, right, numbers):
    pairs = ((left[0], right[0]), (left[0], right[1]), (left[1], right[0]))
    products = [lax.dot_general(x, y, numbers, preferred_element_type=jnp.float32) for x, y in pairs]
    return products[0] + (products[1] + products[2])


def over_lanes(value, lane):
    return jnp.broadcast_to(value[:, lane : lane + 1], value.shape)


def over_sublanes(value, sublane):
    return jnp.broadcast_to(value[sublane : sublane + 1, :], value.shape)


def factor_block(block):
    groups = BLOCK // 8
    row = lax.broadcasted_iota(jnp.int32, (8, BLOCK), 0)
    lane = lax.broadcasted_iota(jnp.int32, (8, BLOCK), 1)
    rest = [block[8 * g : 8 * g + 8, :] for g in range(groups)]
    extra = [jnp.where(lane == row + 8 * g, 1.0, 0.0).astype(jnp.float32) for g in range(groups)]
    upper, inverse = [], []
    for g in range(groups):
        base = 8 * g
        raw = [[over_lanes(rest[h], base + k) for k in range(8)] for h in range(g, groups)]
        small = [[over_sublanes(raw[0][k], i) if i >= k else None for k in range(8)] for i in range(8)]
        scale = []
        for k in range(8):
            inv = lax.rsqrt(small[k][k])
            inv = inv * (1.5 - 0.5 * small[k][k] * inv * inv)
            scale.append(inv)
            for i in range(k + 1, 8):
                small[i][k] = small[i][k] * inv
            for j in range(k + 1, 8):
                for i in range(j, 8):
                    small[i][j] = small[i][j] - small[i][k] * small[j][k]

        def forward(parts, small=small, scale=scale):
            done = []
            for k in range(8):
                part = parts[k]
                for m in range(k):
                    part = part - small[k][m] * done[m]
                done.append(part * scale[k])
            return done

        wide = forward([over_sublanes(rest[g], k) for k in range(8)])
        solved = forward([over_sublanes(extra[g], k) for k in range(8)])
        upper_rows, inverse_rows = wide[0], solved[0]
        for k in range(1, 8):
            upper_rows = jnp.where(row == k, wide[k], upper_rows)
            inverse_rows = jnp.where(row == k, solved[k], inverse_rows)
        upper.append(jnp.where(lane >= row + base, upper_rows, 0.0))
        inverse.append(inverse_rows)
        for h in range(g + 1, groups):
            tall = forward(raw[h - g])
            for k in range(8):
                rest[h] = rest[h] - tall[k] * wide[k]
                extra[h] = extra[h] - tall[k] * solved[k]
    return jnp.concatenate(upper, 0), jnp.concatenate(inverse, 0)


def dealt_pairs(blocks):
    share = (blocks + 2) // 2
    dealt = [None] * blocks
    for a in range(blocks // 2):
        both = [(m, a) for m in range(a, blocks)] + [(m, blocks - 1 - a) for m in range(blocks - 1 - a, blocks)]
        dealt[a], dealt[blocks - 1 - a] = both[:share], both[share:]
    return [pairs + [(0, blocks - 1)] * (share - len(pairs)) for pairs in dealt]


def panel_kernel(grid_rows, index_ref, base_ref, narrow_ref, lines_ref, split_ref, rows_ref):
    groups, child_tiles = index_ref.shape
    total, blocks, _ = base_ref.shape
    slices = narrow_ref.shape[0] // (groups * child_tiles)
    local_rows = total // (slices * grid_rows)
    halves = blocks // PANELS
    dealt = dealt_pairs(blocks)
    share = len(dealt[0])
    per = local_rows * slices + share
    rows_ref[...] = base_ref[...]
    tile_of = lax.broadcasted_iota(jnp.int32, (blocks, BLOCK), 0) // halves
    for g in range(groups):
        moved = []
        for shift in range(PANELS):
            here = jnp.zeros((blocks, BLOCK), jnp.int32)
            for k in range(shift, PANELS):
                here = jnp.where(tile_of == k, (index_ref[g, k - shift] == k).astype(jnp.int32), here)
            moved.append(here == 1)
        for a in range(child_tiles):
            tile = jnp.maximum(index_ref[g, a], 0)
            for u in range(slices):
                at = (tile // grid_rows * slices + u) * grid_rows + lax.rem(tile, grid_rows)
                part = narrow_ref[(g * child_tiles + a) * slices + u]
                added = jnp.where(moved[0], part, 0.0)
                for shift in range(1, PANELS):
                    added = added + jnp.where(moved[shift], pltpu.roll(part, shift * halves, 0), 0.0)
                rows_ref[at] = rows_ref[at] + added
    for q in range(grid_rows):
        for line in range(local_rows * slices):
            value = rows_ref[line * grid_rows + q]
            for p in range(blocks):
                lines_ref[(q * blocks + p) * per + line] = value[p : p + 1, :]
    for p in range(blocks):
        for j, (m, n) in enumerate(dealt[p]):
            value = rows_ref[m % slices * grid_rows + m // slices][n : n + 1, :]
            for q in range(grid_rows):
                lines_ref[(q * blocks + p) * per + local_rows * slices + j] = value
    halves = grid_rows // blocks
    for p in range(blocks):
        for i in range(local_rows):
            for h in range(halves):
                for u in range(slices):
                    split_ref[p, (i * halves + h) * slices + u] = rows_ref[(i * slices + u) * grid_rows + h * blocks + p]


def make_panel(index, base, narrow, grid_rows):
    total, blocks, _ = base.shape
    per = total // grid_rows + len(dealt_pairs(blocks)[0])
    return pl.pallas_call(
        functools.partial(panel_kernel, grid_rows),
        out_shape=(
            jax.ShapeDtypeStruct((grid_rows * blocks * per, 1, BLOCK), jnp.float32),
            jax.ShapeDtypeStruct((blocks, total // blocks, blocks, BLOCK), jnp.float32),
        ),
        in_specs=[SCALARS, WHOLE, WHOLE],
        out_specs=(WHOLE, WHOLE),
        scratch_shapes=[pltpu.VMEM(base.shape, jnp.float32)],
        cost_estimate=pl.CostEstimate(flops=10**6, bytes_accessed=2 * 2**20, transcendentals=0),
        name="panel",
    )(index, base, narrow)


SOURCES = (0, 1, -1, 2)


def source_col(place_ref, step, core):
    chip = lax.rem(place_ref[1] // 2 - SOURCES[step] + 4, 4)
    mine = lax.rem(place_ref[1], 2)
    return chip * 2 + (mine if core == 0 else 1 - mine)


def factor_kernel(place_ref, pairs_ref, own_ref, other_ref, inverse_ref, mine_ref, diagonal_ref, before_ref):
    order = inverse_ref.shape[0]
    blocks = order // BLOCK
    share = own_ref.shape[1]
    held_ref = inverse_ref
    row = lax.broadcasted_iota(jnp.int32, (BLOCK, BLOCK), 0)
    col = lax.broadcasted_iota(jnp.int32, (BLOCK, BLOCK), 1)
    any_row = lax.broadcasted_iota(jnp.int32, (order, BLOCK), 0)
    zeros = jnp.zeros((BLOCK, BLOCK), jnp.float32)
    wide = 2 * BLOCK

    def span(k):
        return pl.ds(pl.multiple_of(k * BLOCK, BLOCK), BLOCK)

    held_ref[...] = jnp.zeros_like(held_ref)
    before_ref[...] = jnp.zeros_like(before_ref)
    for core, source in enumerate((own_ref, other_ref)):
        for step in range(len(SOURCES)):
            first = source_col(place_ref, step, core) * share
            for j in range(share):
                held_ref[span(pairs_ref[0, first + j]), span(pairs_ref[1, first + j])] = source[step, j]

    @pl.loop(0, blocks)
    def _(k):
        here = span(k)
        block = held_ref[here, here]
        block = jnp.where(row >= col, block, 0.0) + jnp.where(col > row, jnp.where(row > col, block, 0.0).T, 0.0)
        before = before_ref[...]
        later = jnp.where(any_row >= (k + 1) * BLOCK, before, 0.0)
        upper, inverse = factor_block(block)
        for start in range(0, order, wide):
            held_ref[:, start : start + wide] = held_ref[:, start : start + wide] - times(
                before, later[start : start + wide], ROWS_BY_ROWS
            )
        diagonal_ref[here, :] = upper.T

        @pl.loop(k + 1, blocks)
        def _(j):
            held_ref[here, span(j)] = zeros

        held_ref[here, here] = jnp.where(row == col, 1.0, 0.0).astype(jnp.float32)
        column = times(held_ref[:, here], inverse, ROWS_BY_ROWS)
        held_ref[:, here] = column
        before_ref[...] = column

        @pl.when(k + 1 < blocks)
        def _():
            held_ref[:, span(k + 1)] = held_ref[:, span(k + 1)] - times(column, before_ref[span(k + 1), :], ROWS_BY_ROWS)

    per = blocks // PANELS
    for h in range(per):
        m = jnp.minimum(place_ref[0], PANELS - 1) * per + h
        for n in range(blocks):
            value = jnp.where(m == n, diagonal_ref[span(m), :], held_ref[span(m), n * BLOCK : (n + 1) * BLOCK])
            mine_ref[h * BLOCK : (h + 1) * BLOCK, n * BLOCK : (n + 1) * BLOCK] = jnp.where(n > m, 0.0, value)
    for n in range(blocks - 1):
        held_ref[(n + 1) * BLOCK :, n * BLOCK : (n + 1) * BLOCK] = jnp.zeros((order - (n + 1) * BLOCK, BLOCK), jnp.float32)


def factor(place, own, other, order):
    pairs = [pair for dealt in dealt_pairs(order // BLOCK) for pair in dealt]
    pairs = jnp.asarray([[m for m, _ in pairs], [n for _, n in pairs]], jnp.int32)
    return pl.pallas_call(
        factor_kernel,
        out_shape=(
            jax.ShapeDtypeStruct((order, order), jnp.float32),
            jax.ShapeDtypeStruct((order // PANELS, order), jnp.float32),
        ),
        in_specs=[SCALARS, SCALARS, WHOLE, WHOLE],
        out_specs=(WHOLE, WHOLE),
        scratch_shapes=[pltpu.VMEM((order, BLOCK), jnp.float32), pltpu.VMEM((order, BLOCK), jnp.float32)],
        compiler_params=pltpu.CompilerParams(vmem_limit_bytes=40 * 2**20),
        cost_estimate=pl.CostEstimate(flops=10**6, bytes_accessed=2**10, transcendentals=0),
        name="factor",
    )(place, pairs, own, other)


def solve_kernel(grid_rows, place_ref, rows_ref, mine_ref, inverse_ref, solved_ref, sides_ref):
    total, order = solved_ref.shape
    size = order // PANELS
    per = size // BLOCK
    my_row = place_ref[0]
    inverse = [
        [parts_of(inverse_ref[j * size : (j + 1) * size, k * size : (k + 1) * size]) if k >= j else None for k in range(PANELS)]
        for j in range(PANELS)
    ]
    rows = [parts_of(jnp.concatenate([rows_ref[per * k + h] for h in range(per)], axis=1)) for k in range(PANELS)]
    for k in range(PANELS):
        total_k = times_parts(rows[0], inverse[0][k], ROWS_BY_COLUMNS)
        for j in range(1, k + 1):
            total_k = total_k + times_parts(rows[j], inverse[j][k], ROWS_BY_COLUMNS)
        solved_ref[:, k * size : (k + 1) * size] = total_k

    @pl.when(my_row < PANELS)
    def _():
        solved_ref[0:size, :] = mine_ref[...]

    tile = lax.broadcasted_iota(jnp.int32, (total, size), 0) // size * grid_rows + my_row
    used = [parts_of(jnp.where(tile > k, solved_ref[:, k * size : (k + 1) * size], 0.0)) for k in range(PANELS)]
    for j in range(PANELS):
        total_j = times_parts(used[j], inverse[j][j], ROWS_BY_ROWS)
        for k in range(j + 1, PANELS):
            total_j = total_j + times_parts(used[k], inverse[j][k], ROWS_BY_ROWS)
        sides_ref[:, j * size : (j + 1) * size] = total_j


def solve(place, rows, mine, inverse, grid_rows):
    out = jax.ShapeDtypeStruct((rows.shape[1], mine.shape[1]), jnp.float32)
    return pl.pallas_call(
        functools.partial(solve_kernel, grid_rows),
        out_shape=(out, out),
        in_specs=[SCALARS, WHOLE, WHOLE, WHOLE],
        out_specs=(WHOLE, WHOLE),
        compiler_params=pltpu.CompilerParams(vmem_limit_bytes=48 * 2**20),
        cost_estimate=pl.CostEstimate(flops=10**6, bytes_accessed=2**10, transcendentals=0),
        name="solve",
    )(place, rows, mine, inverse)


def finish_kernel(grid_rows, grid_cols, place_ref, tiles_ref, sides_ref, across_ref, last_ref, solved_ref, boost_ref, out_ref, line_ref):
    t = pl.program_id(0)
    my_row, my_col = place_ref[0], place_ref[1]
    size = boost_ref.shape[2]
    halves = size // BLOCK
    local_rows = sides_ref.shape[0] // size
    lines = tiles_ref.shape[0] // BLOCK
    per = lines // (local_rows * halves)
    order = sides_ref.shape[1]
    early = pl.num_programs(0) // 2
    for source, taken in ((across_ref, t < early), (last_ref, t >= early)):

        @pl.when(taken)
        def _(source=source):
            for u in range(halves):
                line_ref[u * BLOCK : (u + 1) * BLOCK, :] = source[:, u].reshape(BLOCK, order)

    change = times_parts(parts_of(sides_ref[...]), parts_of(line_ref[...]), ROWS_BY_ROWS)
    row = lax.broadcasted_iota(jnp.int32, (BLOCK, BLOCK), 0)
    col = lax.broadcasted_iota(jnp.int32, (BLOCK, BLOCK), 1)
    in_panel = jnp.logical_and(t == 0, my_col < PANELS)
    for i in range(local_rows):
        on_diagonal = i * grid_rows + my_row == t * grid_cols + my_col
        for u in range(halves):
            for h in range(halves):
                start = i * size + u * BLOCK
                value = tiles_ref[pl.ds((i * halves + u) * per + t * halves + h, BLOCK, stride=lines), :]
                value = value - change[start : start + BLOCK, h * BLOCK : (h + 1) * BLOCK]
                if u == h:
                    line = boost_ref[i * grid_rows + my_row][:, h * BLOCK : (h + 1) * BLOCK]
                    value = value + jnp.where(jnp.logical_and(on_diagonal, row == col), line, 0.0)
                lane = pl.multiple_of(jnp.minimum(my_col, PANELS - 1) * size + h * BLOCK, BLOCK)
                value = jnp.where(in_panel, solved_ref[start : start + BLOCK, pl.ds(lane, BLOCK)], value)
                out_ref[pl.ds(start * per + t * halves + h, BLOCK, stride=per), :] = value


def finish(place, tiles, sides, across, last, solved, boost, grid_rows, grid_cols):
    ranks, lines, cols, order = across.shape
    halves = boost.shape[2] // BLOCK
    early = lines // halves
    steps = 2 * early

    def still(*shape):
        return pl.BlockSpec(shape, lambda t: (0,) * len(shape))

    return pl.pallas_call(
        functools.partial(finish_kernel, grid_rows, grid_cols),
        grid=(steps,),
        out_shape=jax.ShapeDtypeStruct(tiles.shape, jnp.float32),
        in_specs=[
            SCALARS,
            still(*tiles.shape),
            still(*sides.shape),
            pl.BlockSpec((ranks, halves, cols, order), lambda t: (0, jnp.minimum(t, early - 1), 0, 0)),
            pl.BlockSpec((ranks, halves, cols, order), lambda t: (0, jnp.maximum(t - early, 0), 0, 0)),
            still(*solved.shape),
            still(*boost.shape),
        ],
        out_specs=still(*tiles.shape),
        scratch_shapes=[pltpu.VMEM((boost.shape[2], order), jnp.float32)],
        compiler_params=pltpu.CompilerParams(vmem_limit_bytes=48 * 2**20),
        cost_estimate=pl.CostEstimate(flops=4 * 10**9, bytes_accessed=12 * 2**20, transcendentals=0),
        name="finish",
    )(place, tiles, sides, across, last, solved, boost)


def body(front_entries, child_updates, diag_boost, tile_mask, child_parent, child_index):
    grid_rows = lax.axis_size("row")
    grid_cols = lax.axis_size("col")
    groups = lax.axis_size("front")
    my_group = lax.axis_index("front")
    my_row = lax.axis_index("row")
    my_col = lax.axis_index("col")
    local_rows = front_entries.shape[1]
    slices = front_entries.shape[2]
    local_cols = front_entries.shape[7]
    size = front_entries.shape[8]
    held = child_updates.shape[0]
    child_tiles = child_updates.shape[1]
    halves = grid_rows // grid_cols
    order = PANELS * size

    pieces = child_updates.reshape(held, child_tiles, slices, child_tiles, size)
    parents = child_parent.reshape(groups, held)
    comes = parents == my_group
    index = jnp.sum(jnp.where(comes[:, :, None], child_index.reshape(groups, held, child_tiles), 0), axis=1)
    index = jnp.where(jnp.any(comes, axis=1)[:, None], index, -1)
    mine = lax.dynamic_index_in_dim(parents, my_group, 0, keepdims=False)
    goes = (mine[None, :] == jnp.arange(groups)[:, None])[:, :, None, None, None]
    blocks = order // BLOCK
    narrow = pieces[:, :, :, :PANELS].reshape(held, child_tiles * slices, blocks, BLOCK)
    narrow = jnp.sum(jnp.where(goes, narrow[None], 0.0), axis=1)
    narrow = lax.all_to_all(narrow, "front", split_axis=0, concat_axis=0, tiled=True)
    arrived = lax.all_gather(pieces, "front", axis=0)
    arrived = jnp.sum(jnp.where(comes[:, :, None, None, None, None], arrived, 0.0), axis=1)

    entries = front_entries.reshape(local_rows, slices, grid_rows, grid_cols, local_cols, size)
    mask_tiles = jnp.transpose(tile_mask[0].reshape(local_rows, grid_rows, local_cols, grid_cols), (0, 1, 3, 2))
    kept = (mask_tiles == 1)[:, None, :, :, :, None]
    row_ids = jnp.arange(local_rows)[:, None] * grid_rows + jnp.arange(grid_rows)[None, :]
    col_ids = jnp.arange(local_cols)[:, None] * grid_cols + jnp.arange(grid_cols)[None, :]
    row_hits = (index[:, None, None, :] == row_ids[None, :, :, None]).astype(jnp.float32)
    col_hits = (index[:, None, None, :] == col_ids[None, :, :, None]).astype(jnp.float32)
    within = jnp.arange(slices) * grid_rows * grid_cols + my_row * grid_cols + my_col
    boost = jnp.where(
        within[:, None, None, None] == jnp.arange(size),
        jnp.where(jnp.eye(grid_rows, PANELS, dtype=bool)[:, :, None], diag_boost[0, :PANELS], 0.0),
        0.0,
    )
    boost = jnp.where((jnp.arange(local_rows) == 0)[:, None, None, None, None], boost, 0.0)
    base = jnp.where(kept[:, :, :, :PANELS, 0], entries[:, :, :, :PANELS, 0, :], 0.0) + boost
    lines, split = make_panel(index, base.reshape(-1, blocks, BLOCK), narrow.reshape(-1, blocks, BLOCK), grid_rows)

    split = lax.all_to_all(split, "col", split_axis=0, concat_axis=0, tiled=True)
    for_cols = jnp.transpose(split, (1, 0, 2, 3)).reshape(local_cols * slices, grid_cols, order)

    lines = lines.reshape(grid_rows * grid_cols, -1, 1, BLOCK)
    lines, for_cols = lax.optimization_barrier((lines, for_cols))
    part = local_cols * slices // 2
    across = lax.all_gather(for_cols[:part], "row", axis=0)
    lines = lax.all_to_all(lines, ("row", "col"), split_axis=0, concat_axis=0, tiled=True)
    lines = jnp.transpose(lines.reshape(grid_rows * grid_cols, -1, BLOCK), (1, 0, 2))
    for_rows, for_top = lines[: local_rows * slices].reshape(local_rows * size, BLOCK), lines[local_rows * slices :]

    spread = jnp.einsum("naube,ntpb->nautpe", arrived, col_hits, precision=HIGHEST)
    assembled = jnp.where(kept, entries, 0.0) + jnp.einsum("niqa,nautpe->iuqpte", row_hits, spread, precision=HIGHEST)
    joined = jnp.transpose(assembled, (2, 3, 0, 1, 4, 5))
    joined = joined.reshape(grid_rows * grid_cols, local_rows * slices, local_cols * size // BLOCK, BLOCK)

    joined, across, last = lax.optimization_barrier((joined, across, for_cols[part:]))
    tiles = lax.all_to_all(joined, ("row", "col"), split_axis=0, concat_axis=0, tiled=True).reshape(-1, BLOCK)

    def over_chips(value):
        cols = range(grid_cols)
        moved = [lax.ppermute(value, "col", [(c, (c + 2 * d) % grid_cols) for c in cols]) for d in SOURCES[1:]]
        return jnp.stack([value] + moved)

    def over_cores(value):
        return lax.ppermute(value, "col", [(c, c ^ 1) for c in range(grid_cols)])

    place = jnp.stack([my_row, my_col]).astype(jnp.int32)
    own_top = over_chips(for_top)
    other_top = over_cores(own_top)
    rows = lax.all_gather(for_rows, "col", axis=0)
    last = lax.all_gather(last, "row", axis=0)
    inverse, mine = factor(place, own_top, other_top, order)
    solved, sides = solve(place, rows, mine, inverse, grid_rows)
    out = finish(place, tiles, sides, across, last, solved, diag_boost[0][:, None, :], grid_rows, grid_cols)
    return out.reshape(1, local_rows, 1, size, local_cols, 1, size)


def solution(mesh):
    placed = (
        P("front", None, None, "row", "col", None, None, None, None),
        P("front", None, None, "row", "col", None, None),
        P("front", None, None),
        P("front", None, None),
        P(),
        P(),
    )
    return jax.shard_map(
        body,
        mesh=mesh,
        in_specs=placed,
        out_specs=P("front", None, "row", None, None, "col", None),
        check_vma=False,
    )
```

```python
import functools

import jax
import jax.numpy as jnp
from jax import lax
from jax.experimental import pallas as pl
from jax.experimental.pallas import tpu as pltpu
from jax.sharding import PartitionSpec as P

PANELS = 4
BLOCK = 128
HIGHEST = lax.Precision.HIGHEST
ROWS_BY_ROWS = (((1,), (1,)), ((), ()))
ROWS_BY_COLUMNS = (((1,), (0,)), ((), ()))
WHOLE = pl.BlockSpec(memory_space=pltpu.VMEM)
SCALARS = pl.BlockSpec(memory_space=pltpu.SMEM)


def times(left, right, numbers):
    return lax.dot_general(left, right, numbers, precision=HIGHEST, preferred_element_type=jnp.float32)


def parts_of(value):
    high = value.astype(jnp.bfloat16)
    return high, (value - high.astype(jnp.float32)).astype(jnp.bfloat16)


def times_parts(left, right, numbers):
    pairs = ((left[0], right[0]), (left[0], right[1]), (left[1], right[0]))
    products = [lax.dot_general(x, y, numbers, preferred_element_type=jnp.float32) for x, y in pairs]
    return products[0] + (products[1] + products[2])


def over_lanes(value, lane):
    return jnp.broadcast_to(value[:, lane : lane + 1], value.shape)


def over_sublanes(value, sublane):
    return jnp.broadcast_to(value[sublane : sublane + 1, :], value.shape)


def factor_block(block):
    groups = BLOCK // 8
    row = lax.broadcasted_iota(jnp.int32, (8, BLOCK), 0)
    lane = lax.broadcasted_iota(jnp.int32, (8, BLOCK), 1)
    rest = [block[8 * g : 8 * g + 8, :] for g in range(groups)]
    extra = [jnp.where(lane == row + 8 * g, 1.0, 0.0).astype(jnp.float32) for g in range(groups)]
    upper, inverse = [], []
    for g in range(groups):
        base = 8 * g
        raw = [[over_lanes(rest[h], base + k) for k in range(8)] for h in range(g, groups)]
        small = [[over_sublanes(raw[0][k], i) if i >= k else None for k in range(8)] for i in range(8)]
        scale = []
        for k in range(8):
            inv = lax.rsqrt(small[k][k])
            inv = inv * (1.5 - 0.5 * small[k][k] * inv * inv)
            scale.append(inv)
            for i in range(k + 1, 8):
                small[i][k] = small[i][k] * inv
            for j in range(k + 1, 8):
                for i in range(j, 8):
                    small[i][j] = small[i][j] - small[i][k] * small[j][k]

        def forward(parts, small=small, scale=scale):
            done = []
            for k in range(8):
                part = parts[k]
                for m in range(k):
                    part = part - small[k][m] * done[m]
                done.append(part * scale[k])
            return done

        wide = forward([over_sublanes(rest[g], k) for k in range(8)])
        solved = forward([over_sublanes(extra[g], k) for k in range(8)])
        upper_rows, inverse_rows = wide[0], solved[0]
        for k in range(1, 8):
            upper_rows = jnp.where(row == k, wide[k], upper_rows)
            inverse_rows = jnp.where(row == k, solved[k], inverse_rows)
        upper.append(jnp.where(lane >= row + base, upper_rows, 0.0))
        inverse.append(inverse_rows)
        for h in range(g + 1, groups):
            tall = forward(raw[h - g])
            for k in range(8):
                rest[h] = rest[h] - tall[k] * wide[k]
                extra[h] = extra[h] - tall[k] * solved[k]
    return jnp.concatenate(upper, 0), jnp.concatenate(inverse, 0)


def dealt_pairs(blocks):
    share = (blocks + 2) // 2
    dealt = [None] * blocks
    for a in range(blocks // 2):
        both = [(m, a) for m in range(a, blocks)] + [(m, blocks - 1 - a) for m in range(blocks - 1 - a, blocks)]
        dealt[a], dealt[blocks - 1 - a] = both[:share], both[share:]
    return [pairs + [(0, blocks - 1)] * (share - len(pairs)) for pairs in dealt]


def panel_kernel(grid_rows, index_ref, base_ref, narrow_ref, lines_ref, rows_ref):
    groups, child_tiles = index_ref.shape
    total, blocks, _ = base_ref.shape
    slices = narrow_ref.shape[0] // (groups * child_tiles)
    local_rows = total // (slices * grid_rows)
    halves = blocks // PANELS
    dealt = dealt_pairs(blocks)
    share = len(dealt[0])
    wide = share + local_rows * slices
    bands = grid_rows // blocks
    cuts = grid_rows // (bands * local_rows * slices)
    per = wide + blocks // cuts
    rows_ref[...] = base_ref[...]
    tile_of = lax.broadcasted_iota(jnp.int32, (blocks, BLOCK), 0) // halves
    for g in range(groups):
        moved = []
        for shift in range(PANELS):
            here = jnp.zeros((blocks, BLOCK), jnp.int32)
            for k in range(shift, PANELS):
                here = jnp.where(tile_of == k, (index_ref[g, k - shift] == k).astype(jnp.int32), here)
            moved.append(here == 1)
        for a in range(child_tiles):
            tile = jnp.maximum(index_ref[g, a], 0)
            for u in range(slices):
                at = (tile // grid_rows * slices + u) * grid_rows + lax.rem(tile, grid_rows)
                part = narrow_ref[(g * child_tiles + a) * slices + u]
                added = jnp.where(moved[0], part, 0.0)
                for shift in range(1, PANELS):
                    added = added + jnp.where(moved[shift], pltpu.roll(part, shift * halves, 0), 0.0)
                rows_ref[at] = rows_ref[at] + added
    for q in range(grid_rows):
        for line in range(local_rows * slices):
            value = rows_ref[line * grid_rows + q]
            for p in range(blocks):
                lines_ref[(q * blocks + p) * per + line] = value[p : p + 1, :]
    for p in range(blocks):
        for j, (m, n) in enumerate(dealt[p]):
            value = rows_ref[m % slices * grid_rows + m // slices][n : n + 1, :]
            for q in range(grid_rows):
                lines_ref[(q * blocks + p) * per + local_rows * slices + j] = value
    for q in range(grid_rows):
        line, cut = q // cuts, q % cuts
        t, u = line // slices, line % slices
        for p in range(blocks):
            value = rows_ref[(t // bands * slices + u) * grid_rows + t % bands * blocks + p]
            for n in range(blocks // cuts):
                start = cut * (blocks // cuts) + n
                lines_ref[(q * blocks + p) * per + wide + n] = value[start : start + 1, :]


def make_panel(index, base, narrow, grid_rows):
    total, blocks, _ = base.shape
    per = total // grid_rows + len(dealt_pairs(blocks)[0]) + blocks * (total // blocks) // grid_rows
    return pl.pallas_call(
        functools.partial(panel_kernel, grid_rows),
        out_shape=jax.ShapeDtypeStruct((grid_rows * blocks * per, 1, BLOCK), jnp.float32),
        in_specs=[SCALARS, WHOLE, WHOLE],
        out_specs=WHOLE,
        scratch_shapes=[pltpu.VMEM(base.shape, jnp.float32)],
        cost_estimate=pl.CostEstimate(flops=10**6, bytes_accessed=2 * 2**20, transcendentals=0),
        name="panel",
    )(index, base, narrow)


SOURCES = (0, 1, -1, 2)


def source_col(place_ref, step, core):
    chip = lax.rem(place_ref[1] // 2 - SOURCES[step] + 4, 4)
    mine = lax.rem(place_ref[1], 2)
    return chip * 2 + (mine if core == 0 else 1 - mine)


def factor_kernel(place_ref, pairs_ref, own_ref, other_ref, inverse_ref, mine_ref, diagonal_ref, before_ref):
    order = inverse_ref.shape[0]
    blocks = order // BLOCK
    share = own_ref.shape[1]
    held_ref = inverse_ref
    row = lax.broadcasted_iota(jnp.int32, (BLOCK, BLOCK), 0)
    col = lax.broadcasted_iota(jnp.int32, (BLOCK, BLOCK), 1)
    any_row = lax.broadcasted_iota(jnp.int32, (order, BLOCK), 0)
    zeros = jnp.zeros((BLOCK, BLOCK), jnp.float32)
    wide = 2 * BLOCK

    def span(k):
        return pl.ds(pl.multiple_of(k * BLOCK, BLOCK), BLOCK)

    held_ref[...] = jnp.zeros_like(held_ref)
    before_ref[...] = jnp.zeros_like(before_ref)
    for core, source in enumerate((own_ref, other_ref)):
        for step in range(len(SOURCES)):
            first = source_col(place_ref, step, core) * share
            for j in range(share):
                held_ref[span(pairs_ref[0, first + j]), span(pairs_ref[1, first + j])] = source[step, j]

    @pl.loop(0, blocks)
    def _(k):
        here = span(k)
        block = held_ref[here, here]
        block = jnp.where(row >= col, block, 0.0) + jnp.where(col > row, jnp.where(row > col, block, 0.0).T, 0.0)
        before = before_ref[...]
        later = jnp.where(any_row >= (k + 1) * BLOCK, before, 0.0)
        upper, inverse = factor_block(block)
        for start in range(0, order, wide):
            held_ref[:, start : start + wide] = held_ref[:, start : start + wide] - times(
                before, later[start : start + wide], ROWS_BY_ROWS
            )
        diagonal_ref[here, :] = upper.T

        @pl.loop(k + 1, blocks)
        def _(j):
            held_ref[here, span(j)] = zeros

        held_ref[here, here] = jnp.where(row == col, 1.0, 0.0).astype(jnp.float32)
        column = times(held_ref[:, here], inverse, ROWS_BY_ROWS)
        held_ref[:, here] = column
        before_ref[...] = column

        @pl.when(k + 1 < blocks)
        def _():
            held_ref[:, span(k + 1)] = held_ref[:, span(k + 1)] - times(column, before_ref[span(k + 1), :], ROWS_BY_ROWS)

    per = blocks // PANELS
    for h in range(per):
        m = jnp.minimum(place_ref[0], PANELS - 1) * per + h
        for n in range(blocks):
            value = jnp.where(m == n, diagonal_ref[span(m), :], held_ref[span(m), n * BLOCK : (n + 1) * BLOCK])
            mine_ref[h * BLOCK : (h + 1) * BLOCK, n * BLOCK : (n + 1) * BLOCK] = jnp.where(n > m, 0.0, value)
    for n in range(blocks - 1):
        held_ref[(n + 1) * BLOCK :, n * BLOCK : (n + 1) * BLOCK] = jnp.zeros((order - (n + 1) * BLOCK, BLOCK), jnp.float32)


def factor(place, own, other, order):
    pairs = [pair for dealt in dealt_pairs(order // BLOCK) for pair in dealt]
    pairs = jnp.asarray([[m for m, _ in pairs], [n for _, n in pairs]], jnp.int32)
    return pl.pallas_call(
        factor_kernel,
        out_shape=(
            jax.ShapeDtypeStruct((order, order), jnp.float32),
            jax.ShapeDtypeStruct((order // PANELS, order), jnp.float32),
        ),
        in_specs=[SCALARS, SCALARS, WHOLE, WHOLE],
        out_specs=(WHOLE, WHOLE),
        scratch_shapes=[pltpu.VMEM((order, BLOCK), jnp.float32), pltpu.VMEM((order, BLOCK), jnp.float32)],
        compiler_params=pltpu.CompilerParams(vmem_limit_bytes=40 * 2**20),
        cost_estimate=pl.CostEstimate(flops=10**6, bytes_accessed=2**10, transcendentals=0),
        name="factor",
    )(place, pairs, own, other)


def solve_kernel(grid_rows, place_ref, rows_ref, mine_ref, inverse_ref, solved_ref, sides_ref):
    total, order = solved_ref.shape
    size = order // PANELS
    per = size // BLOCK
    my_row = place_ref[0]
    inverse = [
        [parts_of(inverse_ref[j * size : (j + 1) * size, k * size : (k + 1) * size]) if k >= j else None for k in range(PANELS)]
        for j in range(PANELS)
    ]
    rows = [parts_of(jnp.concatenate([rows_ref[per * k + h] for h in range(per)], axis=1)) for k in range(PANELS)]
    for k in range(PANELS):
        total_k = times_parts(rows[0], inverse[0][k], ROWS_BY_COLUMNS)
        for j in range(1, k + 1):
            total_k = total_k + times_parts(rows[j], inverse[j][k], ROWS_BY_COLUMNS)
        solved_ref[:, k * size : (k + 1) * size] = total_k

    @pl.when(my_row < PANELS)
    def _():
        solved_ref[0:size, :] = mine_ref[...]

    tile = lax.broadcasted_iota(jnp.int32, (total, size), 0) // size * grid_rows + my_row
    used = [parts_of(jnp.where(tile > k, solved_ref[:, k * size : (k + 1) * size], 0.0)) for k in range(PANELS)]
    for j in range(PANELS):
        total_j = times_parts(used[j], inverse[j][j], ROWS_BY_ROWS)
        for k in range(j + 1, PANELS):
            total_j = total_j + times_parts(used[k], inverse[j][k], ROWS_BY_ROWS)
        sides_ref[:, j * size : (j + 1) * size] = total_j


def solve(place, rows, mine, inverse, grid_rows):
    out = jax.ShapeDtypeStruct((rows.shape[1], mine.shape[1]), jnp.float32)
    return pl.pallas_call(
        functools.partial(solve_kernel, grid_rows),
        out_shape=(out, out),
        in_specs=[SCALARS, WHOLE, WHOLE, WHOLE],
        out_specs=(WHOLE, WHOLE),
        compiler_params=pltpu.CompilerParams(vmem_limit_bytes=48 * 2**20),
        cost_estimate=pl.CostEstimate(flops=10**6, bytes_accessed=2**10, transcendentals=0),
        name="solve",
    )(place, rows, mine, inverse)


def finish_kernel(grid_rows, grid_cols, place_ref, tiles_ref, sides_ref, across_ref, solved_ref, boost_ref, out_ref, line_ref):
    t = pl.program_id(0)
    my_row, my_col = place_ref[0], place_ref[1]
    size = boost_ref.shape[2]
    halves = size // BLOCK
    local_rows = sides_ref.shape[0] // size
    lines = tiles_ref.shape[0] // BLOCK
    per = lines // (local_rows * halves)
    cuts, width = across_ref.shape[0] // halves, across_ref.shape[1]
    for u in range(halves):
        for n in range(cuts * width):
            line_ref[u * BLOCK : (u + 1) * BLOCK, n * BLOCK : (n + 1) * BLOCK] = across_ref[u * cuts + n // width, n % width]
    change = times_parts(parts_of(sides_ref[...]), parts_of(line_ref[...]), ROWS_BY_ROWS)
    row = lax.broadcasted_iota(jnp.int32, (BLOCK, BLOCK), 0)
    col = lax.broadcasted_iota(jnp.int32, (BLOCK, BLOCK), 1)
    in_panel = jnp.logical_and(t == 0, my_col < PANELS)
    for i in range(local_rows):
        on_diagonal = i * grid_rows + my_row == t * grid_cols + my_col
        for u in range(halves):
            for h in range(halves):
                start = i * size + u * BLOCK
                value = tiles_ref[pl.ds((i * halves + u) * per + t * halves + h, BLOCK, stride=lines), :]
                value = value - change[start : start + BLOCK, h * BLOCK : (h + 1) * BLOCK]
                if u == h:
                    line = boost_ref[i * grid_rows + my_row][:, h * BLOCK : (h + 1) * BLOCK]
                    value = value + jnp.where(jnp.logical_and(on_diagonal, row == col), line, 0.0)
                lane = pl.multiple_of(jnp.minimum(my_col, PANELS - 1) * size + h * BLOCK, BLOCK)
                value = jnp.where(in_panel, solved_ref[start : start + BLOCK, pl.ds(lane, BLOCK)], value)
                out_ref[pl.ds(start * per + t * halves + h, BLOCK, stride=per), :] = value


def finish(place, tiles, sides, across, solved, boost, grid_rows, grid_cols):
    order = sides.shape[1]
    steps = tiles.shape[0] // (sides.shape[0] * (boost.shape[2] // BLOCK))

    def still(*shape):
        return pl.BlockSpec(shape, lambda t: (0,) * len(shape))

    return pl.pallas_call(
        functools.partial(finish_kernel, grid_rows, grid_cols),
        grid=(steps,),
        out_shape=jax.ShapeDtypeStruct(tiles.shape, jnp.float32),
        in_specs=[
            SCALARS,
            still(*tiles.shape),
            still(*sides.shape),
            pl.BlockSpec((across.shape[0] // steps,) + across.shape[1:], lambda t: (t, 0, 0, 0)),
            still(*solved.shape),
            still(*boost.shape),
        ],
        out_specs=still(*tiles.shape),
        scratch_shapes=[pltpu.VMEM((boost.shape[2], order), jnp.float32)],
        compiler_params=pltpu.CompilerParams(vmem_limit_bytes=48 * 2**20),
        cost_estimate=pl.CostEstimate(flops=4 * 10**9, bytes_accessed=12 * 2**20, transcendentals=0),
        name="finish",
    )(place, tiles, sides, across, solved, boost)


def body(front_entries, child_updates, diag_boost, tile_mask, child_parent, child_index):
    grid_rows = lax.axis_size("row")
    grid_cols = lax.axis_size("col")
    groups = lax.axis_size("front")
    my_group = lax.axis_index("front")
    my_row = lax.axis_index("row")
    my_col = lax.axis_index("col")
    local_rows = front_entries.shape[1]
    slices = front_entries.shape[2]
    local_cols = front_entries.shape[7]
    size = front_entries.shape[8]
    held = child_updates.shape[0]
    child_tiles = child_updates.shape[1]
    halves = grid_rows // grid_cols
    order = PANELS * size

    pieces = child_updates.reshape(held, child_tiles, slices, child_tiles, size)
    parents = child_parent.reshape(groups, held)
    comes = parents == my_group
    index = jnp.sum(jnp.where(comes[:, :, None], child_index.reshape(groups, held, child_tiles), 0), axis=1)
    index = jnp.where(jnp.any(comes, axis=1)[:, None], index, -1)
    mine = lax.dynamic_index_in_dim(parents, my_group, 0, keepdims=False)
    goes = (mine[None, :] == jnp.arange(groups)[:, None])[:, :, None, None, None]
    blocks = order // BLOCK
    narrow = pieces[:, :, :, :PANELS].reshape(held, child_tiles * slices, blocks, BLOCK)
    narrow = jnp.sum(jnp.where(goes, narrow[None], 0.0), axis=1)
    narrow = lax.all_to_all(narrow, "front", split_axis=0, concat_axis=0, tiled=True)
    arrived = lax.all_gather(pieces, "front", axis=0)
    arrived = jnp.sum(jnp.where(comes[:, :, None, None, None, None], arrived, 0.0), axis=1)

    entries = front_entries.reshape(local_rows, slices, grid_rows, grid_cols, local_cols, size)
    mask_tiles = jnp.transpose(tile_mask[0].reshape(local_rows, grid_rows, local_cols, grid_cols), (0, 1, 3, 2))
    kept = (mask_tiles == 1)[:, None, :, :, :, None]
    row_ids = jnp.arange(local_rows)[:, None] * grid_rows + jnp.arange(grid_rows)[None, :]
    col_ids = jnp.arange(local_cols)[:, None] * grid_cols + jnp.arange(grid_cols)[None, :]
    row_hits = (index[:, None, None, :] == row_ids[None, :, :, None]).astype(jnp.float32)
    col_hits = (index[:, None, None, :] == col_ids[None, :, :, None]).astype(jnp.float32)
    within = jnp.arange(slices) * grid_rows * grid_cols + my_row * grid_cols + my_col
    boost = jnp.where(
        within[:, None, None, None] == jnp.arange(size),
        jnp.where(jnp.eye(grid_rows, PANELS, dtype=bool)[:, :, None], diag_boost[0, :PANELS], 0.0),
        0.0,
    )
    boost = jnp.where((jnp.arange(local_rows) == 0)[:, None, None, None, None], boost, 0.0)
    base = jnp.where(kept[:, :, :, :PANELS, 0], entries[:, :, :, :PANELS, 0, :], 0.0) + boost
    lines = make_panel(index, base.reshape(-1, blocks, BLOCK), narrow.reshape(-1, blocks, BLOCK), grid_rows)

    lines = lines.reshape(grid_rows * grid_cols, -1, 1, BLOCK)
    lines = lax.all_to_all(lines, ("row", "col"), split_axis=0, concat_axis=0, tiled=True)
    lines = jnp.transpose(lines.reshape(grid_rows * grid_cols, -1, BLOCK), (1, 0, 2))
    wide = lines.shape[0] - local_cols * slices * blocks // grid_rows
    across = lax.all_gather(lines[wide:], "row", axis=0)
    for_rows, for_top = lines[: local_rows * slices].reshape(local_rows * size, BLOCK), lines[local_rows * slices : wide]

    spread = jnp.einsum("naube,ntpb->nautpe", arrived, col_hits, precision=HIGHEST)
    assembled = jnp.where(kept, entries, 0.0) + jnp.einsum("niqa,nautpe->iuqpte", row_hits, spread, precision=HIGHEST)
    joined = jnp.transpose(assembled, (2, 3, 0, 1, 4, 5))
    joined = joined.reshape(grid_rows * grid_cols, local_rows * slices, local_cols * size // BLOCK, BLOCK)

    for_top, joined = lax.optimization_barrier((for_top, joined))
    tiles = lax.all_to_all(joined, ("row", "col"), split_axis=0, concat_axis=0, tiled=True).reshape(-1, BLOCK)

    def over_chips(value):
        cols = range(grid_cols)
        moved = [lax.ppermute(value, "col", [(c, (c + 2 * d) % grid_cols) for c in cols]) for d in SOURCES[1:]]
        return jnp.stack([value] + moved)

    def over_cores(value):
        return lax.ppermute(value, "col", [(c, c ^ 1) for c in range(grid_cols)])

    place = jnp.stack([my_row, my_col]).astype(jnp.int32)
    own_top = over_chips(for_top)
    other_top = over_cores(own_top)
    rows = lax.all_gather(for_rows, "col", axis=0)
    inverse, mine = factor(place, own_top, other_top, order)
    solved, sides = solve(place, rows, mine, inverse, grid_rows)
    out = finish(place, tiles, sides, across, solved, diag_boost[0][:, None, :], grid_rows, grid_cols)
    return out.reshape(1, local_rows, 1, size, local_cols, 1, size)


def solution(mesh):
    placed = (
        P("front", None, None, "row", "col", None, None, None, None),
        P("front", None, None, "row", "col", None, None),
        P("front", None, None),
        P("front", None, None),
        P(),
        P(),
    )
    return jax.shard_map(
        body,
        mesh=mesh,
        in_specs=placed,
        out_specs=P("front", None, "row", None, None, "col", None),
        check_vma=False,
    )
```

```python
import functools

import jax
import jax.numpy as jnp
from jax import lax
from jax.experimental import pallas as pl
from jax.experimental.pallas import tpu as pltpu
from jax.sharding import PartitionSpec as P

PANELS = 4
BLOCK = 128
HIGHEST = lax.Precision.HIGHEST
ROWS_BY_ROWS = (((1,), (1,)), ((), ()))
ROWS_BY_COLUMNS = (((1,), (0,)), ((), ()))
WHOLE = pl.BlockSpec(memory_space=pltpu.VMEM)
SCALARS = pl.BlockSpec(memory_space=pltpu.SMEM)


def times(left, right, numbers):
    return lax.dot_general(left, right, numbers, precision=HIGHEST, preferred_element_type=jnp.float32)


def parts_of(value):
    high = value.astype(jnp.bfloat16)
    return high, (value - high.astype(jnp.float32)).astype(jnp.bfloat16)


def times_parts(left, right, numbers):
    pairs = ((left[0], right[0]), (left[0], right[1]), (left[1], right[0]))
    products = [lax.dot_general(x, y, numbers, preferred_element_type=jnp.float32) for x, y in pairs]
    return products[0] + (products[1] + products[2])


def over_lanes(value, lane):
    return jnp.broadcast_to(value[:, lane : lane + 1], value.shape)


def over_sublanes(value, sublane):
    return jnp.broadcast_to(value[sublane : sublane + 1, :], value.shape)


def factor_block(block):
    groups = BLOCK // 8
    row = lax.broadcasted_iota(jnp.int32, (8, BLOCK), 0)
    lane = lax.broadcasted_iota(jnp.int32, (8, BLOCK), 1)
    rest = [block[8 * g : 8 * g + 8, :] for g in range(groups)]
    extra = [jnp.where(lane == row + 8 * g, 1.0, 0.0).astype(jnp.float32) for g in range(groups)]
    upper, inverse = [], []
    for g in range(groups):
        base = 8 * g
        raw = [[over_lanes(rest[h], base + k) for k in range(8)] for h in range(g, groups)]
        small = [[over_sublanes(raw[0][k], i) if i >= k else None for k in range(8)] for i in range(8)]
        scale = []
        for k in range(8):
            inv = lax.rsqrt(small[k][k])
            inv = inv * (1.5 - 0.5 * small[k][k] * inv * inv)
            scale.append(inv)
            for i in range(k + 1, 8):
                small[i][k] = small[i][k] * inv
            for j in range(k + 1, 8):
                for i in range(j, 8):
                    small[i][j] = small[i][j] - small[i][k] * small[j][k]

        def forward(parts, small=small, scale=scale):
            done = []
            for k in range(8):
                part = parts[k]
                for m in range(k):
                    part = part - small[k][m] * done[m]
                done.append(part * scale[k])
            return done

        wide = forward([over_sublanes(rest[g], k) for k in range(8)])
        solved = forward([over_sublanes(extra[g], k) for k in range(8)])
        upper_rows, inverse_rows = wide[0], solved[0]
        for k in range(1, 8):
            upper_rows = jnp.where(row == k, wide[k], upper_rows)
            inverse_rows = jnp.where(row == k, solved[k], inverse_rows)
        upper.append(jnp.where(lane >= row + base, upper_rows, 0.0))
        inverse.append(inverse_rows)
        for h in range(g + 1, groups):
            tall = forward(raw[h - g])
            for k in range(8):
                rest[h] = rest[h] - tall[k] * wide[k]
                extra[h] = extra[h] - tall[k] * solved[k]
    return jnp.concatenate(upper, 0), jnp.concatenate(inverse, 0)


def dealt_pairs(blocks):
    share = (blocks + 2) // 2
    dealt = [None] * blocks
    for a in range(blocks // 2):
        both = [(m, a) for m in range(a, blocks)] + [(m, blocks - 1 - a) for m in range(blocks - 1 - a, blocks)]
        dealt[a], dealt[blocks - 1 - a] = both[:share], both[share:]
    return [pairs + [(0, blocks - 1)] * (share - len(pairs)) for pairs in dealt]


def panel_kernel(grid_rows, index_ref, base_ref, narrow_ref, lines_ref, split_ref, rows_ref):
    groups, child_tiles = index_ref.shape
    total, blocks, _ = base_ref.shape
    slices = narrow_ref.shape[0] // (groups * child_tiles)
    local_rows = total // (slices * grid_rows)
    halves = blocks // PANELS
    dealt = dealt_pairs(blocks)
    share = len(dealt[0])
    per = local_rows * slices + share
    rows_ref[...] = base_ref[...]
    tile_of = lax.broadcasted_iota(jnp.int32, (blocks, BLOCK), 0) // halves
    for g in range(groups):
        moved = []
        for shift in range(PANELS):
            here = jnp.zeros((blocks, BLOCK), jnp.int32)
            for k in range(shift, PANELS):
                here = jnp.where(tile_of == k, (index_ref[g, k - shift] == k).astype(jnp.int32), here)
            moved.append(here == 1)
        for a in range(child_tiles):
            tile = jnp.maximum(index_ref[g, a], 0)
            for u in range(slices):
                at = (tile // grid_rows * slices + u) * grid_rows + lax.rem(tile, grid_rows)
                part = narrow_ref[(g * child_tiles + a) * slices + u][:blocks]
                added = jnp.where(moved[0], part, 0.0)
                for shift in range(1, PANELS):
                    added = added + jnp.where(moved[shift], pltpu.roll(part, shift * halves, 0), 0.0)
                rows_ref[at] = rows_ref[at] + added
    for q in range(grid_rows):
        for line in range(local_rows * slices):
            value = rows_ref[line * grid_rows + q]
            for p in range(blocks):
                lines_ref[(q * blocks + p) * per + line] = value[p : p + 1, :]
    for p in range(blocks):
        for j, (m, n) in enumerate(dealt[p]):
            value = rows_ref[m % slices * grid_rows + m // slices][n : n + 1, :]
            for q in range(grid_rows):
                lines_ref[(q * blocks + p) * per + local_rows * slices + j] = value
    halves = grid_rows // blocks
    for p in range(blocks):
        for i in range(local_rows):
            for h in range(halves):
                for u in range(slices):
                    split_ref[p, (i * halves + h) * slices + u] = rows_ref[(i * slices + u) * grid_rows + h * blocks + p]


def make_panel(index, base, narrow, grid_rows):
    total, blocks, _ = base.shape
    per = total // grid_rows + len(dealt_pairs(blocks)[0])
    return pl.pallas_call(
        functools.partial(panel_kernel, grid_rows),
        out_shape=(
            jax.ShapeDtypeStruct((grid_rows * blocks * per, 1, BLOCK), jnp.float32),
            jax.ShapeDtypeStruct((blocks, total // blocks, blocks, BLOCK), jnp.float32),
        ),
        in_specs=[SCALARS, WHOLE, WHOLE],
        out_specs=(WHOLE, WHOLE),
        scratch_shapes=[pltpu.VMEM(base.shape, jnp.float32)],
        cost_estimate=pl.CostEstimate(flops=10**6, bytes_accessed=2 * 2**20, transcendentals=0),
        name="panel",
    )(index, base, narrow)


SOURCES = (0, 1, -1, 2)


def source_col(place_ref, step, core):
    chip = lax.rem(place_ref[1] // 2 - SOURCES[step] + 4, 4)
    mine = lax.rem(place_ref[1], 2)
    return chip * 2 + (mine if core == 0 else 1 - mine)


def factor_kernel(place_ref, pairs_ref, own_ref, other_ref, inverse_ref, mine_ref, diagonal_ref, before_ref):
    order = inverse_ref.shape[0]
    blocks = order // BLOCK
    dealt = pairs_ref.shape[1] // blocks
    skipped = own_ref.shape[1] - dealt
    held_ref = inverse_ref
    row = lax.broadcasted_iota(jnp.int32, (BLOCK, BLOCK), 0)
    col = lax.broadcasted_iota(jnp.int32, (BLOCK, BLOCK), 1)
    any_row = lax.broadcasted_iota(jnp.int32, (order, BLOCK), 0)
    zeros = jnp.zeros((BLOCK, BLOCK), jnp.float32)
    wide = 2 * BLOCK

    def span(k):
        return pl.ds(pl.multiple_of(k * BLOCK, BLOCK), BLOCK)

    held_ref[...] = jnp.zeros_like(held_ref)
    before_ref[...] = jnp.zeros_like(before_ref)
    for core, source in enumerate((own_ref, other_ref)):
        for step in range(len(SOURCES)):
            first = source_col(place_ref, step, core) * dealt
            for j in range(dealt):
                held_ref[span(pairs_ref[0, first + j]), span(pairs_ref[1, first + j])] = source[step, skipped + j]

    @pl.loop(0, blocks)
    def _(k):
        here = span(k)
        block = held_ref[here, here]
        block = jnp.where(row >= col, block, 0.0) + jnp.where(col > row, jnp.where(row > col, block, 0.0).T, 0.0)
        before = before_ref[...]
        later = jnp.where(any_row >= (k + 1) * BLOCK, before, 0.0)
        upper, inverse = factor_block(block)
        for start in range(0, order, wide):
            held_ref[:, start : start + wide] = held_ref[:, start : start + wide] - times(
                before, later[start : start + wide], ROWS_BY_ROWS
            )
        diagonal_ref[here, :] = upper.T

        @pl.loop(k + 1, blocks)
        def _(j):
            held_ref[here, span(j)] = zeros

        held_ref[here, here] = jnp.where(row == col, 1.0, 0.0).astype(jnp.float32)
        column = times(held_ref[:, here], inverse, ROWS_BY_ROWS)
        held_ref[:, here] = column
        before_ref[...] = column

        @pl.when(k + 1 < blocks)
        def _():
            held_ref[:, span(k + 1)] = held_ref[:, span(k + 1)] - times(column, before_ref[span(k + 1), :], ROWS_BY_ROWS)

    per = blocks // PANELS
    for h in range(per):
        m = jnp.minimum(place_ref[0], PANELS - 1) * per + h
        for n in range(blocks):
            value = jnp.where(m == n, diagonal_ref[span(m), :], held_ref[span(m), n * BLOCK : (n + 1) * BLOCK])
            mine_ref[h * BLOCK : (h + 1) * BLOCK, n * BLOCK : (n + 1) * BLOCK] = jnp.where(n > m, 0.0, value)
    for n in range(blocks - 1):
        held_ref[(n + 1) * BLOCK :, n * BLOCK : (n + 1) * BLOCK] = jnp.zeros((order - (n + 1) * BLOCK, BLOCK), jnp.float32)


def factor(place, own, other, order):
    pairs = [pair for dealt in dealt_pairs(order // BLOCK) for pair in dealt]
    pairs = jnp.asarray([[m for m, _ in pairs], [n for _, n in pairs]], jnp.int32)
    return pl.pallas_call(
        factor_kernel,
        out_shape=(
            jax.ShapeDtypeStruct((order, order), jnp.float32),
            jax.ShapeDtypeStruct((order // PANELS, order), jnp.float32),
        ),
        in_specs=[SCALARS, SCALARS, WHOLE, WHOLE],
        out_specs=(WHOLE, WHOLE),
        scratch_shapes=[pltpu.VMEM((order, BLOCK), jnp.float32), pltpu.VMEM((order, BLOCK), jnp.float32)],
        compiler_params=pltpu.CompilerParams(vmem_limit_bytes=40 * 2**20),
        cost_estimate=pl.CostEstimate(flops=10**6, bytes_accessed=2**10, transcendentals=0),
        name="factor",
    )(place, pairs, own, other)


def solve_kernel(grid_rows, place_ref, own_ref, other_ref, mine_ref, inverse_ref, solved_ref, sides_ref, rows_ref):
    total, order = solved_ref.shape
    size = order // PANELS
    per = size // BLOCK
    my_row = place_ref[0]
    for core, source in enumerate((own_ref, other_ref)):
        for step in range(len(SOURCES)):
            col = source_col(place_ref, step, core)
            for line in range(total // BLOCK):
                rows_ref[col, line * BLOCK : (line + 1) * BLOCK, :] = source[step, line]
    inverse = [
        [parts_of(inverse_ref[j * size : (j + 1) * size, k * size : (k + 1) * size]) if k >= j else None for k in range(PANELS)]
        for j in range(PANELS)
    ]
    rows = [parts_of(jnp.concatenate([rows_ref[per * k + h] for h in range(per)], axis=1)) for k in range(PANELS)]
    for k in range(PANELS):
        total_k = times_parts(rows[0], inverse[0][k], ROWS_BY_COLUMNS)
        for j in range(1, k + 1):
            total_k = total_k + times_parts(rows[j], inverse[j][k], ROWS_BY_COLUMNS)
        solved_ref[:, k * size : (k + 1) * size] = total_k

    @pl.when(my_row < PANELS)
    def _():
        solved_ref[0:size, :] = mine_ref[...]

    tile = lax.broadcasted_iota(jnp.int32, (total, size), 0) // size * grid_rows + my_row
    used = [parts_of(jnp.where(tile > k, solved_ref[:, k * size : (k + 1) * size], 0.0)) for k in range(PANELS)]
    for j in range(PANELS):
        total_j = times_parts(used[j], inverse[j][j], ROWS_BY_ROWS)
        for k in range(j + 1, PANELS):
            total_j = total_j + times_parts(used[k], inverse[j][k], ROWS_BY_ROWS)
        sides_ref[:, j * size : (j + 1) * size] = total_j


def solve(place, own, other, mine, inverse, grid_rows, local_rows):
    total, order = local_rows * mine.shape[0], mine.shape[1]
    out = jax.ShapeDtypeStruct((total, order), jnp.float32)
    return pl.pallas_call(
        functools.partial(solve_kernel, grid_rows),
        out_shape=(out, out),
        in_specs=[SCALARS, WHOLE, WHOLE, WHOLE, WHOLE],
        out_specs=(WHOLE, WHOLE),
        scratch_shapes=[pltpu.VMEM((order // BLOCK, total, BLOCK), jnp.float32)],
        compiler_params=pltpu.CompilerParams(vmem_limit_bytes=48 * 2**20),
        cost_estimate=pl.CostEstimate(flops=10**6, bytes_accessed=2**10, transcendentals=0),
        name="solve",
    )(place, own, other, mine, inverse)


def finish_kernel(grid_rows, grid_cols, place_ref, tiles_ref, sides_ref, across_ref, solved_ref, boost_ref, out_ref, line_ref):
    t = pl.program_id(0)
    my_row, my_col = place_ref[0], place_ref[1]
    size = boost_ref.shape[2]
    halves = size // BLOCK
    local_rows = sides_ref.shape[0] // size
    lines = tiles_ref.shape[0] // BLOCK
    per = lines // (local_rows * halves)
    for u in range(halves):
        line_ref[u * BLOCK : (u + 1) * BLOCK, :] = across_ref[:, u].reshape(BLOCK, sides_ref.shape[1])
    change = times_parts(parts_of(sides_ref[...]), parts_of(line_ref[...]), ROWS_BY_ROWS)
    row = lax.broadcasted_iota(jnp.int32, (BLOCK, BLOCK), 0)
    col = lax.broadcasted_iota(jnp.int32, (BLOCK, BLOCK), 1)
    in_panel = jnp.logical_and(t == 0, my_col < PANELS)
    for i in range(local_rows):
        on_diagonal = i * grid_rows + my_row == t * grid_cols + my_col
        for u in range(halves):
            for h in range(halves):
                start = i * size + u * BLOCK
                value = tiles_ref[pl.ds((i * halves + u) * per + t * halves + h, BLOCK, stride=lines), :]
                value = value - change[start : start + BLOCK, h * BLOCK : (h + 1) * BLOCK]
                if u == h:
                    line = boost_ref[i * grid_rows + my_row][:, h * BLOCK : (h + 1) * BLOCK]
                    value = value + jnp.where(jnp.logical_and(on_diagonal, row == col), line, 0.0)
                lane = pl.multiple_of(jnp.minimum(my_col, PANELS - 1) * size + h * BLOCK, BLOCK)
                value = jnp.where(in_panel, solved_ref[start : start + BLOCK, pl.ds(lane, BLOCK)], value)
                out_ref[pl.ds(start * per + t * halves + h, BLOCK, stride=per), :] = value


def finish(place, tiles, sides, across, solved, boost, grid_rows, grid_cols):
    order = sides.shape[1]
    steps = tiles.shape[0] // (sides.shape[0] * (boost.shape[2] // BLOCK))

    def still(*shape):
        return pl.BlockSpec(shape, lambda t: (0,) * len(shape))

    return pl.pallas_call(
        functools.partial(finish_kernel, grid_rows, grid_cols),
        grid=(steps,),
        out_shape=jax.ShapeDtypeStruct(tiles.shape, jnp.float32),
        in_specs=[
            SCALARS,
            still(*tiles.shape),
            still(*sides.shape),
            pl.BlockSpec((across.shape[0], across.shape[1] // steps) + across.shape[2:], lambda t: (0, t, 0, 0)),
            still(*solved.shape),
            still(*boost.shape),
        ],
        out_specs=still(*tiles.shape),
        scratch_shapes=[pltpu.VMEM((boost.shape[2], order), jnp.float32)],
        compiler_params=pltpu.CompilerParams(vmem_limit_bytes=48 * 2**20),
        cost_estimate=pl.CostEstimate(flops=4 * 10**9, bytes_accessed=12 * 2**20, transcendentals=0),
        name="finish",
    )(place, tiles, sides, across, solved, boost)


def body(front_entries, child_updates, diag_boost, tile_mask, child_parent, child_index):
    grid_rows = lax.axis_size("row")
    grid_cols = lax.axis_size("col")
    groups = lax.axis_size("front")
    my_group = lax.axis_index("front")
    my_row = lax.axis_index("row")
    my_col = lax.axis_index("col")
    local_rows = front_entries.shape[1]
    slices = front_entries.shape[2]
    local_cols = front_entries.shape[7]
    size = front_entries.shape[8]
    held = child_updates.shape[0]
    child_tiles = child_updates.shape[1]
    halves = grid_rows // grid_cols
    order = PANELS * size

    blocks = order // BLOCK
    parents = child_parent.reshape(groups, held)
    comes = parents == my_group
    index = jnp.sum(jnp.where(comes[:, :, None], child_index.reshape(groups, held, child_tiles), 0), axis=1)
    index = jnp.where(jnp.any(comes, axis=1)[:, None], index, -1)
    mine = lax.dynamic_index_in_dim(parents, my_group, 0, keepdims=False)
    goes = (mine[None, :] == jnp.arange(groups)[:, None])[:, :, None, None, None]
    pieces = child_updates.reshape(held, child_tiles * slices, child_tiles * size // BLOCK, BLOCK)
    slots = jnp.sum(jnp.where(goes, pieces[None], 0.0), axis=1)
    lines_of = lax.all_to_all(slots, "front", split_axis=0, concat_axis=0, tiled=True)
    arrived = lines_of.reshape(groups, child_tiles, slices, child_tiles, size)

    entries = front_entries.reshape(local_rows, slices, grid_rows, grid_cols, local_cols, size)
    mask_tiles = jnp.transpose(tile_mask[0].reshape(local_rows, grid_rows, local_cols, grid_cols), (0, 1, 3, 2))
    kept = (mask_tiles == 1)[:, None, :, :, :, None]
    row_ids = jnp.arange(local_rows)[:, None] * grid_rows + jnp.arange(grid_rows)[None, :]
    col_ids = jnp.arange(local_cols)[:, None] * grid_cols + jnp.arange(grid_cols)[None, :]
    row_hits = (index[:, None, None, :] == row_ids[None, :, :, None]).astype(jnp.float32)
    col_hits = (index[:, None, None, :] == col_ids[None, :, :, None]).astype(jnp.float32)
    within = jnp.arange(slices) * grid_rows * grid_cols + my_row * grid_cols + my_col
    boost = jnp.where(
        within[:, None, None, None] == jnp.arange(size),
        jnp.where(jnp.eye(grid_rows, PANELS, dtype=bool)[:, :, None], diag_boost[0, :PANELS], 0.0),
        0.0,
    )
    boost = jnp.where((jnp.arange(local_rows) == 0)[:, None, None, None, None], boost, 0.0)
    base = jnp.where(kept[:, :, :, :PANELS, 0], entries[:, :, :, :PANELS, 0, :], 0.0) + boost
    children = lines_of.reshape((-1,) + lines_of.shape[2:])
    lines, split = make_panel(index, base.reshape(-1, blocks, BLOCK), children, grid_rows)

    split = lax.all_to_all(split, "col", split_axis=0, concat_axis=0, tiled=True)
    for_cols = jnp.transpose(split, (1, 0, 2, 3)).reshape(local_cols * slices, grid_cols, order)
    lines, for_cols = lax.optimization_barrier((lines, for_cols))
    across = lax.all_gather(for_cols, "row", axis=0)

    lines = lines.reshape(grid_rows * grid_cols, -1, 1, BLOCK)
    lines = lax.all_to_all(lines, ("row", "col"), split_axis=0, concat_axis=0, tiled=True)
    lines = jnp.transpose(lines.reshape(grid_rows * grid_cols, -1, BLOCK), (1, 0, 2))

    spread = jnp.einsum("naube,ntpb->nautpe", arrived, col_hits, precision=HIGHEST)
    assembled = jnp.where(kept, entries, 0.0) + jnp.einsum("niqa,nautpe->iuqpte", row_hits, spread, precision=HIGHEST)
    joined = jnp.transpose(assembled, (2, 3, 0, 1, 4, 5))
    joined = joined.reshape(grid_rows * grid_cols, local_rows * slices, local_cols * size // BLOCK, BLOCK)

    lines, joined = lax.optimization_barrier((lines, joined))
    tiles = lax.all_to_all(joined, ("row", "col"), split_axis=0, concat_axis=0, tiled=True).reshape(-1, BLOCK)

    def over_chips(value):
        cols = range(grid_cols)
        moved = [lax.ppermute(value, "col", [(c, (c + 2 * d) % grid_cols) for c in cols]) for d in SOURCES[1:]]
        return jnp.stack([value] + moved)

    def over_cores(value):
        return lax.ppermute(value, "col", [(c, c ^ 1) for c in range(grid_cols)])

    place = jnp.stack([my_row, my_col]).astype(jnp.int32)
    own = over_chips(lines)
    other = over_cores(own)
    inverse, mine = factor(place, own, other, order)
    solved, sides = solve(place, own, other, mine, inverse, grid_rows, local_rows)
    out = finish(place, tiles, sides, across, solved, diag_boost[0][:, None, :], grid_rows, grid_cols)
    return out.reshape(1, local_rows, 1, size, local_cols, 1, size)


def solution(mesh):
    placed = (
        P("front", None, None, "row", "col", None, None, None, None),
        P("front", None, None, "row", "col", None, None),
        P("front", None, None),
        P("front", None, None),
        P(),
        P(),
    )
    return jax.shard_map(
        body,
        mesh=mesh,
        in_specs=placed,
        out_specs=P("front", None, "row", None, None, "col", None),
        check_vma=False,
    )
```

```python
import functools

import jax
import jax.numpy as jnp
from jax import lax
from jax.experimental import pallas as pl
from jax.experimental.pallas import tpu as pltpu
from jax.sharding import PartitionSpec as P

PANELS = 4
BLOCK = 128
HIGHEST = lax.Precision.HIGHEST
ROWS_BY_ROWS = (((1,), (1,)), ((), ()))
ROWS_BY_COLUMNS = (((1,), (0,)), ((), ()))
WHOLE = pl.BlockSpec(memory_space=pltpu.VMEM)
SCALARS = pl.BlockSpec(memory_space=pltpu.SMEM)


def times(left, right, numbers):
    return lax.dot_general(left, right, numbers, precision=HIGHEST, preferred_element_type=jnp.float32)


def parts_of(value):
    high = value.astype(jnp.bfloat16)
    return high, (value - high.astype(jnp.float32)).astype(jnp.bfloat16)


def times_parts(left, right, numbers):
    pairs = ((left[0], right[0]), (left[0], right[1]), (left[1], right[0]))
    products = [lax.dot_general(x, y, numbers, preferred_element_type=jnp.float32) for x, y in pairs]
    return products[0] + (products[1] + products[2])


def over_lanes(value, lane):
    return jnp.broadcast_to(value[:, lane : lane + 1], value.shape)


def over_sublanes(value, sublane):
    return jnp.broadcast_to(value[sublane : sublane + 1, :], value.shape)


def factor_block(block):
    groups = BLOCK // 8
    row = lax.broadcasted_iota(jnp.int32, (8, BLOCK), 0)
    lane = lax.broadcasted_iota(jnp.int32, (8, BLOCK), 1)
    rest = [block[8 * g : 8 * g + 8, :] for g in range(groups)]
    extra = [jnp.where(lane == row + 8 * g, 1.0, 0.0).astype(jnp.float32) for g in range(groups)]
    upper, inverse = [], []
    for g in range(groups):
        base = 8 * g
        raw = [[over_lanes(rest[h], base + k) for k in range(8)] for h in range(g, groups)]
        small = [[over_sublanes(raw[0][k], i) if i >= k else None for k in range(8)] for i in range(8)]
        scale = []
        for k in range(8):
            inv = lax.rsqrt(small[k][k])
            inv = inv * (1.5 - 0.5 * small[k][k] * inv * inv)
            scale.append(inv)
            for i in range(k + 1, 8):
                small[i][k] = small[i][k] * inv
            for j in range(k + 1, 8):
                for i in range(j, 8):
                    small[i][j] = small[i][j] - small[i][k] * small[j][k]

        def forward(parts, small=small, scale=scale):
            done = []
            for k in range(8):
                part = parts[k]
                for m in range(k):
                    part = part - small[k][m] * done[m]
                done.append(part * scale[k])
            return done

        wide = forward([over_sublanes(rest[g], k) for k in range(8)])
        solved = forward([over_sublanes(extra[g], k) for k in range(8)])
        upper_rows, inverse_rows = wide[0], solved[0]
        for k in range(1, 8):
            upper_rows = jnp.where(row == k, wide[k], upper_rows)
            inverse_rows = jnp.where(row == k, solved[k], inverse_rows)
        upper.append(jnp.where(lane >= row + base, upper_rows, 0.0))
        inverse.append(inverse_rows)
        for h in range(g + 1, groups):
            tall = forward(raw[h - g])
            for k in range(8):
                rest[h] = rest[h] - tall[k] * wide[k]
                extra[h] = extra[h] - tall[k] * solved[k]
    return jnp.concatenate(upper, 0), jnp.concatenate(inverse, 0)


def dealt_pairs(blocks):
    share = (blocks + 2) // 2
    dealt = [None] * blocks
    for a in range(blocks // 2):
        both = [(m, a) for m in range(a, blocks)] + [(m, blocks - 1 - a) for m in range(blocks - 1 - a, blocks)]
        dealt[a], dealt[blocks - 1 - a] = both[:share], both[share:]
    return [pairs + [(0, blocks - 1)] * (share - len(pairs)) for pairs in dealt]


def panel_kernel(grid_rows, index_ref, base_ref, narrow_ref, lines_ref, split_ref, rows_ref):
    groups, child_tiles = index_ref.shape
    total, blocks, _ = base_ref.shape
    slices = narrow_ref.shape[0] // (groups * child_tiles)
    local_rows = total // (slices * grid_rows)
    halves = blocks // PANELS
    dealt = dealt_pairs(blocks)
    share = len(dealt[0])
    per = local_rows * slices + share
    rows_ref[...] = base_ref[...]
    tile_of = lax.broadcasted_iota(jnp.int32, (blocks, BLOCK), 0) // halves
    for g in range(groups):
        moved = []
        for shift in range(PANELS):
            here = jnp.zeros((blocks, BLOCK), jnp.int32)
            for k in range(shift, PANELS):
                here = jnp.where(tile_of == k, (index_ref[g, k - shift] == k).astype(jnp.int32), here)
            moved.append(here == 1)
        for a in range(child_tiles):
            tile = jnp.maximum(index_ref[g, a], 0)
            for u in range(slices):
                at = (tile // grid_rows * slices + u) * grid_rows + lax.rem(tile, grid_rows)
                part = narrow_ref[(g * child_tiles + a) * slices + u][:blocks]
                added = jnp.where(moved[0], part, 0.0)
                for shift in range(1, PANELS):
                    added = added + jnp.where(moved[shift], pltpu.roll(part, shift * halves, 0), 0.0)
                rows_ref[at] = rows_ref[at] + added
    for q in range(grid_rows):
        for line in range(local_rows * slices):
            value = rows_ref[line * grid_rows + q]
            for p in range(blocks):
                lines_ref[(q * blocks + p) * per + line] = value[p : p + 1, :]
    for p in range(blocks):
        for j, (m, n) in enumerate(dealt[p]):
            value = rows_ref[m % slices * grid_rows + m // slices][n : n + 1, :]
            for q in range(grid_rows):
                lines_ref[(q * blocks + p) * per + local_rows * slices + j] = value
    halves = grid_rows // blocks
    for p in range(blocks):
        for i in range(local_rows):
            for h in range(halves):
                for u in range(slices):
                    split_ref[p, (i * halves + h) * slices + u] = rows_ref[(i * slices + u) * grid_rows + h * blocks + p]


def make_panel(index, base, narrow, grid_rows):
    total, blocks, _ = base.shape
    per = total // grid_rows + len(dealt_pairs(blocks)[0])
    return pl.pallas_call(
        functools.partial(panel_kernel, grid_rows),
        out_shape=(
            jax.ShapeDtypeStruct((grid_rows * blocks * per, 1, BLOCK), jnp.float32),
            jax.ShapeDtypeStruct((blocks, total // blocks, blocks, BLOCK), jnp.float32),
        ),
        in_specs=[SCALARS, WHOLE, WHOLE],
        out_specs=(WHOLE, WHOLE),
        scratch_shapes=[pltpu.VMEM(base.shape, jnp.float32)],
        cost_estimate=pl.CostEstimate(flops=10**6, bytes_accessed=2 * 2**20, transcendentals=0),
        name="panel",
    )(index, base, narrow)


def step_after(place, other, cost):
    def kernel(place_ref, _, out_ref):
        for i in range(place_ref.shape[0]):
            out_ref[i] = place_ref[i]

    return pl.pallas_call(
        kernel,
        out_shape=jax.ShapeDtypeStruct(place.shape, place.dtype),
        in_specs=[SCALARS, pl.BlockSpec(memory_space=pl.ANY)],
        out_specs=SCALARS,
        cost_estimate=pl.CostEstimate(flops=cost, bytes_accessed=2**10, transcendentals=0),
        name="step_after",
    )(place, other)


SOURCES = (0, 1, -1, 2)


def source_col(place_ref, step, core):
    chip = lax.rem(place_ref[1] // 2 - SOURCES[step] + 4, 4)
    mine = lax.rem(place_ref[1], 2)
    return chip * 2 + (mine if core == 0 else 1 - mine)


def factor_kernel(place_ref, pairs_ref, own_ref, other_ref, inverse_ref, mine_ref, diagonal_ref, before_ref):
    order = inverse_ref.shape[0]
    blocks = order // BLOCK
    dealt = pairs_ref.shape[1] // blocks
    skipped = own_ref.shape[1] - dealt
    held_ref = inverse_ref
    row = lax.broadcasted_iota(jnp.int32, (BLOCK, BLOCK), 0)
    col = lax.broadcasted_iota(jnp.int32, (BLOCK, BLOCK), 1)
    any_row = lax.broadcasted_iota(jnp.int32, (order, BLOCK), 0)
    zeros = jnp.zeros((BLOCK, BLOCK), jnp.float32)
    wide = 2 * BLOCK

    def span(k):
        return pl.ds(pl.multiple_of(k * BLOCK, BLOCK), BLOCK)

    held_ref[...] = jnp.zeros_like(held_ref)
    before_ref[...] = jnp.zeros_like(before_ref)
    for core, source in enumerate((own_ref, other_ref)):
        for step in range(len(SOURCES)):
            first = source_col(place_ref, step, core) * dealt
            for j in range(dealt):
                held_ref[span(pairs_ref[0, first + j]), span(pairs_ref[1, first + j])] = source[step, skipped + j]

    @pl.loop(0, blocks)
    def _(k):
        here = span(k)
        block = held_ref[here, here]
        block = jnp.where(row >= col, block, 0.0) + jnp.where(col > row, jnp.where(row > col, block, 0.0).T, 0.0)
        before = before_ref[...]
        later = jnp.where(any_row >= (k + 1) * BLOCK, before, 0.0)
        upper, inverse = factor_block(block)
        for start in range(0, order, wide):
            held_ref[:, start : start + wide] = held_ref[:, start : start + wide] - times(
                before, later[start : start + wide], ROWS_BY_ROWS
            )
        diagonal_ref[here, :] = upper.T

        @pl.loop(k + 1, blocks)
        def _(j):
            held_ref[here, span(j)] = zeros

        held_ref[here, here] = jnp.where(row == col, 1.0, 0.0).astype(jnp.float32)
        column = times(held_ref[:, here], inverse, ROWS_BY_ROWS)
        held_ref[:, here] = column
        before_ref[...] = column

        @pl.when(k + 1 < blocks)
        def _():
            held_ref[:, span(k + 1)] = held_ref[:, span(k + 1)] - times(column, before_ref[span(k + 1), :], ROWS_BY_ROWS)

    per = blocks // PANELS
    for h in range(per):
        m = jnp.minimum(place_ref[0], PANELS - 1) * per + h
        for n in range(blocks):
            value = jnp.where(m == n, diagonal_ref[span(m), :], held_ref[span(m), n * BLOCK : (n + 1) * BLOCK])
            mine_ref[h * BLOCK : (h + 1) * BLOCK, n * BLOCK : (n + 1) * BLOCK] = jnp.where(n > m, 0.0, value)
    for n in range(blocks - 1):
        held_ref[(n + 1) * BLOCK :, n * BLOCK : (n + 1) * BLOCK] = jnp.zeros((order - (n + 1) * BLOCK, BLOCK), jnp.float32)


def factor(place, own, other, order):
    pairs = [pair for dealt in dealt_pairs(order // BLOCK) for pair in dealt]
    pairs = jnp.asarray([[m for m, _ in pairs], [n for _, n in pairs]], jnp.int32)
    return pl.pallas_call(
        factor_kernel,
        out_shape=(
            jax.ShapeDtypeStruct((order, order), jnp.float32),
            jax.ShapeDtypeStruct((order // PANELS, order), jnp.float32),
        ),
        in_specs=[SCALARS, SCALARS, WHOLE, WHOLE],
        out_specs=(WHOLE, WHOLE),
        scratch_shapes=[pltpu.VMEM((order, BLOCK), jnp.float32), pltpu.VMEM((order, BLOCK), jnp.float32)],
        compiler_params=pltpu.CompilerParams(vmem_limit_bytes=20 * 2**20),
        cost_estimate=pl.CostEstimate(flops=10**6, bytes_accessed=2**10, transcendentals=0),
        name="factor",
    )(place, pairs, own, other)


def solve_kernel(grid_rows, place_ref, own_ref, other_ref, mine_ref, inverse_ref, solved_ref, sides_ref, rows_ref):
    total, order = solved_ref.shape
    size = order // PANELS
    per = size // BLOCK
    my_row = place_ref[0]
    for core, source in enumerate((own_ref, other_ref)):
        for step in range(len(SOURCES)):
            col = source_col(place_ref, step, core)
            for line in range(total // BLOCK):
                rows_ref[col, line * BLOCK : (line + 1) * BLOCK, :] = source[step, line]
    inverse = [
        [parts_of(inverse_ref[j * size : (j + 1) * size, k * size : (k + 1) * size]) if k >= j else None for k in range(PANELS)]
        for j in range(PANELS)
    ]
    rows = [parts_of(jnp.concatenate([rows_ref[per * k + h] for h in range(per)], axis=1)) for k in range(PANELS)]
    for k in range(PANELS):
        total_k = times_parts(rows[0], inverse[0][k], ROWS_BY_COLUMNS)
        for j in range(1, k + 1):
            total_k = total_k + times_parts(rows[j], inverse[j][k], ROWS_BY_COLUMNS)
        solved_ref[:, k * size : (k + 1) * size] = total_k

    @pl.when(my_row < PANELS)
    def _():
        solved_ref[0:size, :] = mine_ref[...]

    tile = lax.broadcasted_iota(jnp.int32, (total, size), 0) // size * grid_rows + my_row
    used = [parts_of(jnp.where(tile > k, solved_ref[:, k * size : (k + 1) * size], 0.0)) for k in range(PANELS)]
    for j in range(PANELS):
        total_j = times_parts(used[j], inverse[j][j], ROWS_BY_ROWS)
        for k in range(j + 1, PANELS):
            total_j = total_j + times_parts(used[k], inverse[j][k], ROWS_BY_ROWS)
        sides_ref[:, j * size : (j + 1) * size] = total_j


def solve(place, own, other, mine, inverse, grid_rows, local_rows):
    total, order = local_rows * mine.shape[0], mine.shape[1]
    out = jax.ShapeDtypeStruct((total, order), jnp.float32)
    return pl.pallas_call(
        functools.partial(solve_kernel, grid_rows),
        out_shape=(out, out),
        in_specs=[SCALARS, WHOLE, WHOLE, WHOLE, WHOLE],
        out_specs=(WHOLE, WHOLE),
        scratch_shapes=[pltpu.VMEM((order // BLOCK, total, BLOCK), jnp.float32)],
        compiler_params=pltpu.CompilerParams(vmem_limit_bytes=20 * 2**20),
        cost_estimate=pl.CostEstimate(flops=10**6, bytes_accessed=2**10, transcendentals=0),
        name="solve",
    )(place, own, other, mine, inverse)


def finish_kernel(grid_rows, grid_cols, place_ref, tiles_ref, sides_ref, across_ref, solved_ref, boost_ref, out_ref, line_ref):
    t = pl.program_id(0)
    my_row, my_col = place_ref[0], place_ref[1]
    size = boost_ref.shape[2]
    halves = size // BLOCK
    local_rows = sides_ref.shape[0] // size
    lines = tiles_ref.shape[0] // BLOCK
    per = lines // (local_rows * halves)
    for u in range(halves):
        line_ref[u * BLOCK : (u + 1) * BLOCK, :] = across_ref[:, u].reshape(BLOCK, sides_ref.shape[1])
    change = times_parts(parts_of(sides_ref[...]), parts_of(line_ref[...]), ROWS_BY_ROWS)
    row = lax.broadcasted_iota(jnp.int32, (BLOCK, BLOCK), 0)
    col = lax.broadcasted_iota(jnp.int32, (BLOCK, BLOCK), 1)
    in_panel = jnp.logical_and(t == 0, my_col < PANELS)
    for i in range(local_rows):
        on_diagonal = i * grid_rows + my_row == t * grid_cols + my_col
        for u in range(halves):
            for h in range(halves):
                start = i * size + u * BLOCK
                value = tiles_ref[pl.ds((i * halves + u) * per + t * halves + h, BLOCK, stride=lines), :]
                value = value - change[start : start + BLOCK, h * BLOCK : (h + 1) * BLOCK]
                if u == h:
                    line = boost_ref[i * grid_rows + my_row][:, h * BLOCK : (h + 1) * BLOCK]
                    value = value + jnp.where(jnp.logical_and(on_diagonal, row == col), line, 0.0)
                lane = pl.multiple_of(jnp.minimum(my_col, PANELS - 1) * size + h * BLOCK, BLOCK)
                value = jnp.where(in_panel, solved_ref[start : start + BLOCK, pl.ds(lane, BLOCK)], value)
                out_ref[pl.ds(start * per + t * halves + h, BLOCK, stride=per), :] = value


def finish(place, tiles, sides, across, solved, boost, grid_rows, grid_cols):
    order = sides.shape[1]
    steps = tiles.shape[0] // (sides.shape[0] * (boost.shape[2] // BLOCK))

    def still(*shape):
        return pl.BlockSpec(shape, lambda t: (0,) * len(shape))

    return pl.pallas_call(
        functools.partial(finish_kernel, grid_rows, grid_cols),
        grid=(steps,),
        out_shape=jax.ShapeDtypeStruct(tiles.shape, jnp.float32),
        in_specs=[
            SCALARS,
            still(*tiles.shape),
            still(*sides.shape),
            pl.BlockSpec((across.shape[0], across.shape[1] // steps) + across.shape[2:], lambda t: (0, t, 0, 0)),
            still(*solved.shape),
            still(*boost.shape),
        ],
        out_specs=still(*tiles.shape),
        scratch_shapes=[pltpu.VMEM((boost.shape[2], order), jnp.float32)],
        compiler_params=pltpu.CompilerParams(vmem_limit_bytes=20 * 2**20),
        cost_estimate=pl.CostEstimate(flops=4 * 10**9, bytes_accessed=12 * 2**20, transcendentals=0),
        name="finish",
    )(place, tiles, sides, across, solved, boost)


def body(front_entries, child_updates, diag_boost, tile_mask, child_parent, child_index):
    grid_rows = lax.axis_size("row")
    grid_cols = lax.axis_size("col")
    groups = lax.axis_size("front")
    my_group = lax.axis_index("front")
    my_row = lax.axis_index("row")
    my_col = lax.axis_index("col")
    local_rows = front_entries.shape[1]
    slices = front_entries.shape[2]
    local_cols = front_entries.shape[7]
    size = front_entries.shape[8]
    held = child_updates.shape[0]
    child_tiles = child_updates.shape[1]
    halves = grid_rows // grid_cols
    order = PANELS * size

    blocks = order // BLOCK
    parents = child_parent.reshape(groups, held)
    comes = parents == my_group
    index = jnp.sum(jnp.where(comes[:, :, None], child_index.reshape(groups, held, child_tiles), 0), axis=1)
    index = jnp.where(jnp.any(comes, axis=1)[:, None], index, -1)
    mine = lax.dynamic_index_in_dim(parents, my_group, 0, keepdims=False)
    goes = (mine[None, :] == jnp.arange(groups)[:, None])[:, :, None, None, None]
    pieces = child_updates.reshape(held, child_tiles * slices, child_tiles * size // BLOCK, BLOCK)
    slots = jnp.sum(jnp.where(goes, pieces[None], 0.0), axis=1)
    lines_of = lax.all_to_all(slots, "front", split_axis=0, concat_axis=0, tiled=True)
    arrived = lines_of.reshape(groups, child_tiles, slices, child_tiles, size)

    entries = front_entries.reshape(local_rows, slices, grid_rows, grid_cols, local_cols, size)
    mask_tiles = jnp.transpose(tile_mask[0].reshape(local_rows, grid_rows, local_cols, grid_cols), (0, 1, 3, 2))
    kept = (mask_tiles == 1)[:, None, :, :, :, None]
    row_ids = jnp.arange(local_rows)[:, None] * grid_rows + jnp.arange(grid_rows)[None, :]
    col_ids = jnp.arange(local_cols)[:, None] * grid_cols + jnp.arange(grid_cols)[None, :]
    row_hits = (index[:, None, None, :] == row_ids[None, :, :, None]).astype(jnp.float32)
    col_hits = (index[:, None, None, :] == col_ids[None, :, :, None]).astype(jnp.float32)
    within = jnp.arange(slices) * grid_rows * grid_cols + my_row * grid_cols + my_col
    boost = jnp.where(
        within[:, None, None, None] == jnp.arange(size),
        jnp.where(jnp.eye(grid_rows, PANELS, dtype=bool)[:, :, None], diag_boost[0, :PANELS], 0.0),
        0.0,
    )
    boost = jnp.where((jnp.arange(local_rows) == 0)[:, None, None, None, None], boost, 0.0)
    base = jnp.where(kept[:, :, :, :PANELS, 0], entries[:, :, :, :PANELS, 0, :], 0.0) + boost
    children = lines_of.reshape((-1,) + lines_of.shape[2:])
    lines, split = make_panel(index, base.reshape(-1, blocks, BLOCK), children, grid_rows)

    split = lax.all_to_all(split, "col", split_axis=0, concat_axis=0, tiled=True)
    for_cols = jnp.transpose(split, (1, 0, 2, 3)).reshape(local_cols * slices, grid_cols, order)
    lines, for_cols, arrived = lax.optimization_barrier((lines, for_cols, arrived))
    across = lax.all_gather(for_cols, "row", axis=0)

    lines = lines.reshape(grid_rows * grid_cols, -1, 1, BLOCK)
    lines = lax.all_to_all(lines, ("row", "col"), split_axis=0, concat_axis=0, tiled=True)
    lines = jnp.transpose(lines.reshape(grid_rows * grid_cols, -1, BLOCK), (1, 0, 2))

    spread = jnp.einsum("naube,ntpb->nautpe", arrived, col_hits, precision=HIGHEST)
    assembled = jnp.where(kept, entries, 0.0) + jnp.einsum("niqa,nautpe->iuqpte", row_hits, spread, precision=HIGHEST)
    joined = jnp.transpose(assembled, (2, 3, 0, 1, 4, 5))
    joined = joined.reshape(grid_rows * grid_cols, local_rows * slices, local_cols * size // BLOCK, BLOCK)

    lines, joined = lax.optimization_barrier((lines, joined))
    tiles = lax.all_to_all(joined, ("row", "col"), split_axis=0, concat_axis=0, tiled=True).reshape(-1, BLOCK)

    def over_chips(value):
        cols = range(grid_cols)
        moved = [lax.ppermute(value, "col", [(c, (c + 2 * d) % grid_cols) for c in cols]) for d in SOURCES[1:]]
        return jnp.stack([value] + moved)

    def over_cores(value):
        return lax.ppermute(value, "col", [(c, c ^ 1) for c in range(grid_cols)])

    place = jnp.stack([my_row, my_col]).astype(jnp.int32)
    own = over_chips(lines)
    other = over_cores(own)
    place = step_after(step_after(place, lines, 10**10), own, 10**11)
    inverse, mine = factor(place, own, other, order)
    solved, sides = solve(place, own, other, mine, inverse, grid_rows, local_rows)
    out = finish(place, tiles, sides, across, solved, diag_boost[0][:, None, :], grid_rows, grid_cols)
    return out.reshape(1, local_rows, 1, size, local_cols, 1, size)


def solution(mesh):
    placed = (
        P("front", None, None, "row", "col", None, None, None, None),
        P("front", None, None, "row", "col", None, None),
        P("front", None, None),
        P("front", None, None),
        P(),
        P(),
    )
    return jax.shard_map(
        body,
        mesh=mesh,
        in_specs=placed,
        out_specs=P("front", None, "row", None, None, "col", None),
        check_vma=False,
    )
```

```python
import functools

import jax
import jax.numpy as jnp
from jax import lax
from jax.experimental import pallas as pl
from jax.experimental.pallas import tpu as pltpu
from jax.sharding import PartitionSpec as P

PANELS = 4
BLOCK = 128
HIGHEST = lax.Precision.HIGHEST
ROWS_BY_ROWS = (((1,), (1,)), ((), ()))
ROWS_BY_COLUMNS = (((1,), (0,)), ((), ()))
WHOLE = pl.BlockSpec(memory_space=pltpu.VMEM)
SCALARS = pl.BlockSpec(memory_space=pltpu.SMEM)


def times(left, right, numbers):
    return lax.dot_general(left, right, numbers, precision=HIGHEST, preferred_element_type=jnp.float32)


def parts_of(value):
    high = value.astype(jnp.bfloat16)
    return high, (value - high.astype(jnp.float32)).astype(jnp.bfloat16)


def times_parts(left, right, numbers):
    pairs = ((left[0], right[0]), (left[0], right[1]), (left[1], right[0]))
    products = [lax.dot_general(x, y, numbers, preferred_element_type=jnp.float32) for x, y in pairs]
    return products[0] + (products[1] + products[2])


def over_lanes(value, lane):
    return jnp.broadcast_to(value[:, lane : lane + 1], value.shape)


def over_sublanes(value, sublane):
    return jnp.broadcast_to(value[sublane : sublane + 1, :], value.shape)


def factor_block(block):
    groups = BLOCK // 8
    row = lax.broadcasted_iota(jnp.int32, (8, BLOCK), 0)
    lane = lax.broadcasted_iota(jnp.int32, (8, BLOCK), 1)
    rest = [block[8 * g : 8 * g + 8, :] for g in range(groups)]
    extra = [jnp.where(lane == row + 8 * g, 1.0, 0.0).astype(jnp.float32) for g in range(groups)]
    upper, inverse = [], []
    for g in range(groups):
        base = 8 * g
        raw = [[over_lanes(rest[h], base + k) for k in range(8)] for h in range(g, groups)]
        small = [[over_sublanes(raw[0][k], i) if i >= k else None for k in range(8)] for i in range(8)]
        scale = []
        for k in range(8):
            inv = lax.rsqrt(small[k][k])
            inv = inv * (1.5 - 0.5 * small[k][k] * inv * inv)
            scale.append(inv)
            for i in range(k + 1, 8):
                small[i][k] = small[i][k] * inv
            for j in range(k + 1, 8):
                for i in range(j, 8):
                    small[i][j] = small[i][j] - small[i][k] * small[j][k]

        def forward(parts, small=small, scale=scale):
            done = []
            for k in range(8):
                part = parts[k]
                for m in range(k):
                    part = part - small[k][m] * done[m]
                done.append(part * scale[k])
            return done

        wide = forward([over_sublanes(rest[g], k) for k in range(8)])
        solved = forward([over_sublanes(extra[g], k) for k in range(8)])
        upper_rows, inverse_rows = wide[0], solved[0]
        for k in range(1, 8):
            upper_rows = jnp.where(row == k, wide[k], upper_rows)
            inverse_rows = jnp.where(row == k, solved[k], inverse_rows)
        upper.append(jnp.where(lane >= row + base, upper_rows, 0.0))
        inverse.append(inverse_rows)
        for h in range(g + 1, groups):
            tall = forward(raw[h - g])
            for k in range(8):
                rest[h] = rest[h] - tall[k] * wide[k]
                extra[h] = extra[h] - tall[k] * solved[k]
    return jnp.concatenate(upper, 0), jnp.concatenate(inverse, 0)


def dealt_pairs(blocks):
    share = (blocks + 2) // 2
    dealt = [None] * blocks
    for a in range(blocks // 2):
        both = [(m, a) for m in range(a, blocks)] + [(m, blocks - 1 - a) for m in range(blocks - 1 - a, blocks)]
        dealt[a], dealt[blocks - 1 - a] = both[:share], both[share:]
    return [pairs + [(0, blocks - 1)] * (share - len(pairs)) for pairs in dealt]


def panel_kernel(grid_rows, index_ref, base_ref, narrow_ref, lines_ref, split_ref, rows_ref):
    groups, child_tiles = index_ref.shape
    total, blocks, _ = base_ref.shape
    slices = narrow_ref.shape[0] // (groups * child_tiles)
    local_rows = total // (slices * grid_rows)
    halves = blocks // PANELS
    dealt = dealt_pairs(blocks)
    share = len(dealt[0])
    per = local_rows * slices + share
    rows_ref[...] = base_ref[...]
    tile_of = lax.broadcasted_iota(jnp.int32, (blocks, BLOCK), 0) // halves
    for g in range(groups):
        moved = []
        for shift in range(PANELS):
            here = jnp.zeros((blocks, BLOCK), jnp.int32)
            for k in range(shift, PANELS):
                here = jnp.where(tile_of == k, (index_ref[g, k - shift] == k).astype(jnp.int32), here)
            moved.append(here == 1)
        for a in range(child_tiles):
            tile = jnp.maximum(index_ref[g, a], 0)
            for u in range(slices):
                at = (tile // grid_rows * slices + u) * grid_rows + lax.rem(tile, grid_rows)
                part = narrow_ref[(g * child_tiles + a) * slices + u][:blocks]
                added = jnp.where(moved[0], part, 0.0)
                for shift in range(1, PANELS):
                    added = added + jnp.where(moved[shift], pltpu.roll(part, shift * halves, 0), 0.0)
                rows_ref[at] = rows_ref[at] + added
    for q in range(grid_rows):
        for line in range(local_rows * slices):
            value = rows_ref[line * grid_rows + q]
            for p in range(blocks):
                lines_ref[(q * blocks + p) * per + line] = value[p : p + 1, :]
    for p in range(blocks):
        for j, (m, n) in enumerate(dealt[p]):
            value = rows_ref[m % slices * grid_rows + m // slices][n : n + 1, :]
            for q in range(grid_rows):
                lines_ref[(q * blocks + p) * per + local_rows * slices + j] = value
    halves = grid_rows // blocks
    for p in range(blocks):
        for i in range(local_rows):
            for h in range(halves):
                for u in range(slices):
                    split_ref[p, (i * halves + h) * slices + u] = rows_ref[(i * slices + u) * grid_rows + h * blocks + p]


def make_panel(index, base, narrow, grid_rows):
    total, blocks, _ = base.shape
    per = total // grid_rows + len(dealt_pairs(blocks)[0])
    return pl.pallas_call(
        functools.partial(panel_kernel, grid_rows),
        out_shape=(
            jax.ShapeDtypeStruct((grid_rows * blocks * per, 1, BLOCK), jnp.float32),
            jax.ShapeDtypeStruct((blocks, total // blocks, blocks, BLOCK), jnp.float32),
        ),
        in_specs=[SCALARS, WHOLE, WHOLE],
        out_specs=(WHOLE, WHOLE),
        scratch_shapes=[pltpu.VMEM(base.shape, jnp.float32)],
        cost_estimate=pl.CostEstimate(flops=10**6, bytes_accessed=2 * 2**20, transcendentals=0),
        name="panel",
    )(index, base, narrow)


SOURCES = (0, 1, -1, 2)


def source_col(place_ref, step, core):
    chip = lax.rem(place_ref[1] // 2 - SOURCES[step] + 4, 4)
    mine = lax.rem(place_ref[1], 2)
    return chip * 2 + (mine if core == 0 else 1 - mine)


def factor_kernel(place_ref, pairs_ref, own_ref, other_ref, inverse_ref, mine_ref, diagonal_ref, before_ref):
    order = inverse_ref.shape[0]
    blocks = order // BLOCK
    dealt = pairs_ref.shape[1] // blocks
    skipped = own_ref.shape[1] - dealt
    held_ref = inverse_ref
    row = lax.broadcasted_iota(jnp.int32, (BLOCK, BLOCK), 0)
    col = lax.broadcasted_iota(jnp.int32, (BLOCK, BLOCK), 1)
    any_row = lax.broadcasted_iota(jnp.int32, (order, BLOCK), 0)
    zeros = jnp.zeros((BLOCK, BLOCK), jnp.float32)
    wide = 2 * BLOCK

    def span(k):
        return pl.ds(pl.multiple_of(k * BLOCK, BLOCK), BLOCK)

    held_ref[...] = jnp.zeros_like(held_ref)
    before_ref[...] = jnp.zeros_like(before_ref)
    for core, source in enumerate((own_ref, other_ref)):
        for step in range(len(SOURCES)):
            first = source_col(place_ref, step, core) * dealt
            for j in range(dealt):
                held_ref[span(pairs_ref[0, first + j]), span(pairs_ref[1, first + j])] = source[step, skipped + j]

    @pl.loop(0, blocks)
    def _(k):
        here = span(k)
        block = held_ref[here, here]
        block = jnp.where(row >= col, block, 0.0) + jnp.where(col > row, jnp.where(row > col, block, 0.0).T, 0.0)
        before = before_ref[...]
        later = jnp.where(any_row >= (k + 1) * BLOCK, before, 0.0)
        upper, inverse = factor_block(block)
        for start in range(0, order, wide):
            held_ref[:, start : start + wide] = held_ref[:, start : start + wide] - times(
                before, later[start : start + wide], ROWS_BY_ROWS
            )
        diagonal_ref[here, :] = upper.T

        @pl.loop(k + 1, blocks)
        def _(j):
            held_ref[here, span(j)] = zeros

        held_ref[here, here] = jnp.where(row == col, 1.0, 0.0).astype(jnp.float32)
        column = times(held_ref[:, here], inverse, ROWS_BY_ROWS)
        held_ref[:, here] = column
        before_ref[...] = column

        @pl.when(k + 1 < blocks)
        def _():
            held_ref[:, span(k + 1)] = held_ref[:, span(k + 1)] - times(column, before_ref[span(k + 1), :], ROWS_BY_ROWS)

    per = blocks // PANELS
    for h in range(per):
        m = jnp.minimum(place_ref[0], PANELS - 1) * per + h
        for n in range(blocks):
            value = jnp.where(m == n, diagonal_ref[span(m), :], held_ref[span(m), n * BLOCK : (n + 1) * BLOCK])
            mine_ref[h * BLOCK : (h + 1) * BLOCK, n * BLOCK : (n + 1) * BLOCK] = jnp.where(n > m, 0.0, value)
    for n in range(blocks - 1):
        held_ref[(n + 1) * BLOCK :, n * BLOCK : (n + 1) * BLOCK] = jnp.zeros((order - (n + 1) * BLOCK, BLOCK), jnp.float32)


def factor(place, own, other, order):
    pairs = [pair for dealt in dealt_pairs(order // BLOCK) for pair in dealt]
    pairs = jnp.asarray([[m for m, _ in pairs], [n for _, n in pairs]], jnp.int32)
    return pl.pallas_call(
        factor_kernel,
        out_shape=(
            jax.ShapeDtypeStruct((order, order), jnp.float32),
            jax.ShapeDtypeStruct((order // PANELS, order), jnp.float32),
        ),
        in_specs=[SCALARS, SCALARS, WHOLE, WHOLE],
        out_specs=(WHOLE, WHOLE),
        scratch_shapes=[pltpu.VMEM((order, BLOCK), jnp.float32), pltpu.VMEM((order, BLOCK), jnp.float32)],
        compiler_params=pltpu.CompilerParams(vmem_limit_bytes=20 * 2**20),
        cost_estimate=pl.CostEstimate(flops=10**6, bytes_accessed=2**10, transcendentals=0),
        name="factor",
    )(place, pairs, own, other)


def solve_kernel(grid_rows, place_ref, own_ref, other_ref, mine_ref, inverse_ref, solved_ref, sides_ref, rows_ref):
    total, order = solved_ref.shape
    size = order // PANELS
    per = size // BLOCK
    my_row = place_ref[0]
    for core, source in enumerate((own_ref, other_ref)):
        for step in range(len(SOURCES)):
            col = source_col(place_ref, step, core)
            for line in range(total // BLOCK):
                rows_ref[col, line * BLOCK : (line + 1) * BLOCK, :] = source[step, line]
    inverse = [
        [parts_of(inverse_ref[j * size : (j + 1) * size, k * size : (k + 1) * size]) if k >= j else None for k in range(PANELS)]
        for j in range(PANELS)
    ]
    rows = [parts_of(jnp.concatenate([rows_ref[per * k + h] for h in range(per)], axis=1)) for k in range(PANELS)]
    for k in range(PANELS):
        total_k = times_parts(rows[0], inverse[0][k], ROWS_BY_COLUMNS)
        for j in range(1, k + 1):
            total_k = total_k + times_parts(rows[j], inverse[j][k], ROWS_BY_COLUMNS)
        solved_ref[:, k * size : (k + 1) * size] = total_k

    @pl.when(my_row < PANELS)
    def _():
        solved_ref[0:size, :] = mine_ref[...]

    tile = lax.broadcasted_iota(jnp.int32, (total, size), 0) // size * grid_rows + my_row
    used = [parts_of(jnp.where(tile > k, solved_ref[:, k * size : (k + 1) * size], 0.0)) for k in range(PANELS)]
    for j in range(PANELS):
        total_j = times_parts(used[j], inverse[j][j], ROWS_BY_ROWS)
        for k in range(j + 1, PANELS):
            total_j = total_j + times_parts(used[k], inverse[j][k], ROWS_BY_ROWS)
        sides_ref[:, j * size : (j + 1) * size] = total_j


def solve(place, own, other, mine, inverse, grid_rows, local_rows):
    total, order = local_rows * mine.shape[0], mine.shape[1]
    out = jax.ShapeDtypeStruct((total, order), jnp.float32)
    return pl.pallas_call(
        functools.partial(solve_kernel, grid_rows),
        out_shape=(out, out),
        in_specs=[SCALARS, WHOLE, WHOLE, WHOLE, WHOLE],
        out_specs=(WHOLE, WHOLE),
        scratch_shapes=[pltpu.VMEM((order // BLOCK, total, BLOCK), jnp.float32)],
        compiler_params=pltpu.CompilerParams(vmem_limit_bytes=20 * 2**20),
        cost_estimate=pl.CostEstimate(flops=10**6, bytes_accessed=2**10, transcendentals=0),
        name="solve",
    )(place, own, other, mine, inverse)


def change_kernel(sides_ref, across_ref, change_ref):
    order = sides_ref.shape[1]
    across = jnp.concatenate([across_ref[:, u].reshape(BLOCK, order) for u in range(across_ref.shape[1])], axis=0)
    change_ref[...] = times_parts(parts_of(sides_ref[...]), parts_of(across), ROWS_BY_ROWS)


def changes(sides, across, steps, cost):
    total, order = sides.shape
    size = across.shape[0] * across.shape[1] * across.shape[2] // steps
    return pl.pallas_call(
        change_kernel,
        grid=(steps,),
        out_shape=jax.ShapeDtypeStruct((total, steps * size), jnp.float32),
        in_specs=[
            pl.BlockSpec((total, order), lambda t: (0, 0)),
            pl.BlockSpec((across.shape[0], across.shape[1] // steps) + across.shape[2:], lambda t: (0, t, 0, 0)),
        ],
        out_specs=pl.BlockSpec((total, size), lambda t: (0, t)),
        compiler_params=pltpu.CompilerParams(vmem_limit_bytes=20 * 2**20),
        cost_estimate=pl.CostEstimate(flops=cost, bytes_accessed=2**10, transcendentals=0),
        name="changes",
    )(sides, across)


def finish_kernel(grid_rows, grid_cols, place_ref, tiles_ref, change_ref, solved_ref, boost_ref, out_ref):
    my_row, my_col = place_ref[0], place_ref[1]
    size = boost_ref.shape[2]
    halves = size // BLOCK
    local_rows = change_ref.shape[0] // size
    local_cols = change_ref.shape[1] // size
    per = local_cols * halves
    lines = local_rows * halves * per
    row = lax.broadcasted_iota(jnp.int32, (BLOCK, BLOCK), 0)
    col = lax.broadcasted_iota(jnp.int32, (BLOCK, BLOCK), 1)
    for i in range(local_rows):
        for t in range(local_cols):
            on_diagonal = i * grid_rows + my_row == t * grid_cols + my_col
            for u in range(halves):
                start = i * size + u * BLOCK
                for h in range(halves):
                    value = tiles_ref[pl.ds((i * halves + u) * per + t * halves + h, BLOCK, stride=lines), :]
                    first = t * size + h * BLOCK
                    value = value - change_ref[start : start + BLOCK, first : first + BLOCK]
                    if u == h:
                        line = boost_ref[i * grid_rows + my_row][:, h * BLOCK : (h + 1) * BLOCK]
                        value = value + jnp.where(jnp.logical_and(on_diagonal, row == col), line, 0.0)
                    if t == 0:
                        lane = pl.multiple_of(jnp.minimum(my_col, PANELS - 1) * size + h * BLOCK, BLOCK)
                        value = jnp.where(my_col < PANELS, solved_ref[start : start + BLOCK, pl.ds(lane, BLOCK)], value)
                    out_ref[pl.ds(start * per + t * halves + h, BLOCK, stride=per), :] = value


def finish(place, tiles, change, solved, boost, grid_rows, grid_cols):
    return pl.pallas_call(
        functools.partial(finish_kernel, grid_rows, grid_cols),
        out_shape=jax.ShapeDtypeStruct(tiles.shape, jnp.float32),
        in_specs=[SCALARS, WHOLE, WHOLE, WHOLE, WHOLE],
        out_specs=WHOLE,
        compiler_params=pltpu.CompilerParams(vmem_limit_bytes=16 * 2**20),
        cost_estimate=pl.CostEstimate(flops=10**6, bytes_accessed=2**10, transcendentals=0),
        name="finish",
    )(place, tiles, change, solved, boost)


def body(front_entries, child_updates, diag_boost, tile_mask, child_parent, child_index):
    grid_rows = lax.axis_size("row")
    grid_cols = lax.axis_size("col")
    groups = lax.axis_size("front")
    my_group = lax.axis_index("front")
    my_row = lax.axis_index("row")
    my_col = lax.axis_index("col")
    local_rows = front_entries.shape[1]
    slices = front_entries.shape[2]
    local_cols = front_entries.shape[7]
    size = front_entries.shape[8]
    held = child_updates.shape[0]
    child_tiles = child_updates.shape[1]
    halves = grid_rows // grid_cols
    order = PANELS * size

    blocks = order // BLOCK
    parents = child_parent.reshape(groups, held)
    comes = parents == my_group
    index = jnp.sum(jnp.where(comes[:, :, None], child_index.reshape(groups, held, child_tiles), 0), axis=1)
    index = jnp.where(jnp.any(comes, axis=1)[:, None], index, -1)
    mine = lax.dynamic_index_in_dim(parents, my_group, 0, keepdims=False)
    goes = (mine[None, :] == jnp.arange(groups)[:, None])[:, :, None, None, None]
    pieces = child_updates.reshape(held, child_tiles * slices, child_tiles * size // BLOCK, BLOCK)
    slots = jnp.sum(jnp.where(goes, pieces[None], 0.0), axis=1)
    lines_of = lax.all_to_all(slots, "front", split_axis=0, concat_axis=0, tiled=True)
    arrived = lines_of.reshape(groups, child_tiles, slices, child_tiles, size)

    entries = front_entries.reshape(local_rows, slices, grid_rows, grid_cols, local_cols, size)
    mask_tiles = jnp.transpose(tile_mask[0].reshape(local_rows, grid_rows, local_cols, grid_cols), (0, 1, 3, 2))
    kept = (mask_tiles == 1)[:, None, :, :, :, None]
    row_ids = jnp.arange(local_rows)[:, None] * grid_rows + jnp.arange(grid_rows)[None, :]
    col_ids = jnp.arange(local_cols)[:, None] * grid_cols + jnp.arange(grid_cols)[None, :]
    row_hits = (index[:, None, None, :] == row_ids[None, :, :, None]).astype(jnp.float32)
    col_hits = (index[:, None, None, :] == col_ids[None, :, :, None]).astype(jnp.float32)
    within = jnp.arange(slices) * grid_rows * grid_cols + my_row * grid_cols + my_col
    boost = jnp.where(
        within[:, None, None, None] == jnp.arange(size),
        jnp.where(jnp.eye(grid_rows, PANELS, dtype=bool)[:, :, None], diag_boost[0, :PANELS], 0.0),
        0.0,
    )
    boost = jnp.where((jnp.arange(local_rows) == 0)[:, None, None, None, None], boost, 0.0)
    base = jnp.where(kept[:, :, :, :PANELS, 0], entries[:, :, :, :PANELS, 0, :], 0.0) + boost
    children = lines_of.reshape((-1,) + lines_of.shape[2:])
    lines, split = make_panel(index, base.reshape(-1, blocks, BLOCK), children, grid_rows)

    split = lax.all_to_all(split, "col", split_axis=0, concat_axis=0, tiled=True)
    for_cols = jnp.transpose(split, (1, 0, 2, 3)).reshape(local_cols * slices, grid_cols, order)
    lines, for_cols, arrived = lax.optimization_barrier((lines, for_cols, arrived))
    across = lax.all_gather(for_cols, "row", axis=0)

    lines = lines.reshape(grid_rows * grid_cols, -1, 1, BLOCK)
    lines = lax.all_to_all(lines, ("row", "col"), split_axis=0, concat_axis=0, tiled=True)
    lines = jnp.transpose(lines.reshape(grid_rows * grid_cols, -1, BLOCK), (1, 0, 2))

    spread = jnp.einsum("naube,ntpb->nautpe", arrived, col_hits, precision=HIGHEST)
    assembled = jnp.where(kept, entries, 0.0) + jnp.einsum("niqa,nautpe->iuqpte", row_hits, spread, precision=HIGHEST)
    joined = jnp.transpose(assembled, (2, 3, 0, 1, 4, 5))
    joined = joined.reshape(grid_rows * grid_cols, local_rows * slices, local_cols * size // BLOCK, BLOCK)

    lines, joined = lax.optimization_barrier((lines, joined))
    tiles = lax.all_to_all(joined, ("row", "col"), split_axis=0, concat_axis=0, tiled=True).reshape(-1, BLOCK)

    def over_chips(value):
        cols = range(grid_cols)
        moved = [lax.ppermute(value, "col", [(c, (c + 2 * d) % grid_cols) for c in cols]) for d in SOURCES[1:]]
        return jnp.stack([value] + moved)

    def over_cores(value):
        return lax.ppermute(value, "col", [(c, c ^ 1) for c in range(grid_cols)])

    place = jnp.stack([my_row, my_col]).astype(jnp.int32)
    own = over_chips(lines)
    other = over_cores(own)
    inverse, mine = factor(place, own, other, order)
    solved, sides = solve(place, own, other, mine, inverse, grid_rows, local_rows)
    change = changes(sides, across, local_cols, 37 * 10**9)
    out = finish(place, tiles, change, solved, diag_boost[0][:, None, :], grid_rows, grid_cols)
    return out.reshape(1, local_rows, 1, size, local_cols, 1, size)


def solution(mesh):
    placed = (
        P("front", None, None, "row", "col", None, None, None, None),
        P("front", None, None, "row", "col", None, None),
        P("front", None, None),
        P("front", None, None),
        P(),
        P(),
    )
    return jax.shard_map(
        body,
        mesh=mesh,
        in_specs=placed,
        out_specs=P("front", None, "row", None, None, "col", None),
        check_vma=False,
    )
```

```python
import functools

import jax
import jax.numpy as jnp
from jax import lax
from jax.experimental import pallas as pl
from jax.experimental.pallas import tpu as pltpu
from jax.sharding import PartitionSpec as P

PANELS = 4
BLOCK = 128
HIGHEST = lax.Precision.HIGHEST
ROWS_BY_ROWS = (((1,), (1,)), ((), ()))
ROWS_BY_COLUMNS = (((1,), (0,)), ((), ()))
WHOLE = pl.BlockSpec(memory_space=pltpu.VMEM)
SCALARS = pl.BlockSpec(memory_space=pltpu.SMEM)


def times(left, right, numbers):
    return lax.dot_general(left, right, numbers, precision=HIGHEST, preferred_element_type=jnp.float32)


def parts_of(value):
    high = value.astype(jnp.bfloat16)
    return high, (value - high.astype(jnp.float32)).astype(jnp.bfloat16)


def times_parts(left, right, numbers):
    pairs = ((left[0], right[0]), (left[0], right[1]), (left[1], right[0]))
    products = [lax.dot_general(x, y, numbers, preferred_element_type=jnp.float32) for x, y in pairs]
    return products[0] + (products[1] + products[2])


def over_lanes(value, lane):
    return jnp.broadcast_to(value[:, lane : lane + 1], value.shape)


def over_sublanes(value, sublane):
    return jnp.broadcast_to(value[sublane : sublane + 1, :], value.shape)


def factor_block(block):
    groups = BLOCK // 8
    row = lax.broadcasted_iota(jnp.int32, (8, BLOCK), 0)
    lane = lax.broadcasted_iota(jnp.int32, (8, BLOCK), 1)
    rest = [block[8 * g : 8 * g + 8, :] for g in range(groups)]
    extra = [jnp.where(lane == row + 8 * g, 1.0, 0.0).astype(jnp.float32) for g in range(groups)]
    upper, inverse = [], []
    for g in range(groups):
        base = 8 * g
        raw = [[over_lanes(rest[h], base + k) for k in range(8)] for h in range(g, groups)]
        small = [[over_sublanes(raw[0][k], i) if i >= k else None for k in range(8)] for i in range(8)]
        scale = []
        for k in range(8):
            inv = lax.rsqrt(small[k][k])
            inv = inv * (1.5 - 0.5 * small[k][k] * inv * inv)
            scale.append(inv)
            for i in range(k + 1, 8):
                small[i][k] = small[i][k] * inv
            for j in range(k + 1, 8):
                for i in range(j, 8):
                    small[i][j] = small[i][j] - small[i][k] * small[j][k]

        def forward(parts, small=small, scale=scale):
            done = []
            for k in range(8):
                part = parts[k]
                for m in range(k):
                    part = part - small[k][m] * done[m]
                done.append(part * scale[k])
            return done

        wide = forward([over_sublanes(rest[g], k) for k in range(8)])
        solved = forward([over_sublanes(extra[g], k) for k in range(8)])
        upper_rows, inverse_rows = wide[0], solved[0]
        for k in range(1, 8):
            upper_rows = jnp.where(row == k, wide[k], upper_rows)
            inverse_rows = jnp.where(row == k, solved[k], inverse_rows)
        upper.append(jnp.where(lane >= row + base, upper_rows, 0.0))
        inverse.append(inverse_rows)
        for h in range(g + 1, groups):
            tall = forward(raw[h - g])
            for k in range(8):
                rest[h] = rest[h] - tall[k] * wide[k]
                extra[h] = extra[h] - tall[k] * solved[k]
    return jnp.concatenate(upper, 0), jnp.concatenate(inverse, 0)


def dealt_pairs(blocks):
    share = (blocks + 2) // 2
    dealt = [None] * blocks
    for a in range(blocks // 2):
        both = [(m, a) for m in range(a, blocks)] + [(m, blocks - 1 - a) for m in range(blocks - 1 - a, blocks)]
        dealt[a], dealt[blocks - 1 - a] = both[:share], both[share:]
    return [pairs + [(0, blocks - 1)] * (share - len(pairs)) for pairs in dealt]


def panel_kernel(grid_rows, index_ref, base_ref, narrow_ref, lines_ref, split_ref, rows_ref):
    groups, child_tiles = index_ref.shape
    total, blocks, _ = base_ref.shape
    slices = narrow_ref.shape[0] // (groups * child_tiles)
    local_rows = total // (slices * grid_rows)
    halves = blocks // PANELS
    dealt = dealt_pairs(blocks)
    share = len(dealt[0])
    per = local_rows * slices + share
    rows_ref[...] = base_ref[...]
    tile_of = lax.broadcasted_iota(jnp.int32, (blocks, BLOCK), 0) // halves
    for g in range(groups):
        moved = []
        for shift in range(PANELS):
            here = jnp.zeros((blocks, BLOCK), jnp.int32)
            for k in range(shift, PANELS):
                here = jnp.where(tile_of == k, (index_ref[g, k - shift] == k).astype(jnp.int32), here)
            moved.append(here == 1)
        for a in range(child_tiles):
            tile = jnp.maximum(index_ref[g, a], 0)
            for u in range(slices):
                at = (tile // grid_rows * slices + u) * grid_rows + lax.rem(tile, grid_rows)
                part = narrow_ref[(g * child_tiles + a) * slices + u][:blocks]
                added = jnp.where(moved[0], part, 0.0)
                for shift in range(1, PANELS):
                    added = added + jnp.where(moved[shift], pltpu.roll(part, shift * halves, 0), 0.0)
                rows_ref[at] = rows_ref[at] + added
    for q in range(grid_rows):
        for line in range(local_rows * slices):
            value = rows_ref[line * grid_rows + q]
            for p in range(blocks):
                lines_ref[(q * blocks + p) * per + line] = value[p : p + 1, :]
    for p in range(blocks):
        for j, (m, n) in enumerate(dealt[p]):
            value = rows_ref[m % slices * grid_rows + m // slices][n : n + 1, :]
            for q in range(grid_rows):
                lines_ref[(q * blocks + p) * per + local_rows * slices + j] = value
    halves = grid_rows // blocks
    for p in range(blocks):
        for i in range(local_rows):
            for h in range(halves):
                for u in range(slices):
                    split_ref[p, (i * halves + h) * slices + u] = rows_ref[(i * slices + u) * grid_rows + h * blocks + p]


def make_panel(index, base, narrow, grid_rows):
    total, blocks, _ = base.shape
    per = total // grid_rows + len(dealt_pairs(blocks)[0])
    return pl.pallas_call(
        functools.partial(panel_kernel, grid_rows),
        out_shape=(
            jax.ShapeDtypeStruct((grid_rows * blocks * per, 1, BLOCK), jnp.float32),
            jax.ShapeDtypeStruct((blocks, total // blocks, blocks, BLOCK), jnp.float32),
        ),
        in_specs=[SCALARS, WHOLE, WHOLE],
        out_specs=(WHOLE, WHOLE),
        scratch_shapes=[pltpu.VMEM(base.shape, jnp.float32)],
        cost_estimate=pl.CostEstimate(flops=10**6, bytes_accessed=2 * 2**20, transcendentals=0),
        name="panel",
    )(index, base, narrow)


SOURCES = (0, 1, -1, 2)


def source_col(place_ref, step, core):
    chip = lax.rem(place_ref[1] // 2 - SOURCES[step] + 4, 4)
    mine = lax.rem(place_ref[1], 2)
    return chip * 2 + (mine if core == 0 else 1 - mine)


def factor_kernel(place_ref, pairs_ref, own_ref, other_ref, inverse_ref, mine_ref, diagonal_ref, before_ref):
    order = inverse_ref.shape[0]
    blocks = order // BLOCK
    dealt = pairs_ref.shape[1] // blocks
    skipped = own_ref.shape[1] - dealt
    held_ref = inverse_ref
    row = lax.broadcasted_iota(jnp.int32, (BLOCK, BLOCK), 0)
    col = lax.broadcasted_iota(jnp.int32, (BLOCK, BLOCK), 1)
    any_row = lax.broadcasted_iota(jnp.int32, (order, BLOCK), 0)
    zeros = jnp.zeros((BLOCK, BLOCK), jnp.float32)
    wide = 2 * BLOCK

    def span(k):
        return pl.ds(pl.multiple_of(k * BLOCK, BLOCK), BLOCK)

    held_ref[...] = jnp.zeros_like(held_ref)
    before_ref[...] = jnp.zeros_like(before_ref)
    for core, source in enumerate((own_ref, other_ref)):
        for step in range(len(SOURCES)):
            first = source_col(place_ref, step, core) * dealt
            for j in range(dealt):
                held_ref[span(pairs_ref[0, first + j]), span(pairs_ref[1, first + j])] = source[step, skipped + j]

    @pl.loop(0, blocks)
    def _(k):
        here = span(k)
        block = held_ref[here, here]
        block = jnp.where(row >= col, block, 0.0) + jnp.where(col > row, jnp.where(row > col, block, 0.0).T, 0.0)
        before = before_ref[...]
        later = jnp.where(any_row >= (k + 1) * BLOCK, before, 0.0)
        upper, inverse = factor_block(block)
        for start in range(0, order, wide):
            held_ref[:, start : start + wide] = held_ref[:, start : start + wide] - times(
                before, later[start : start + wide], ROWS_BY_ROWS
            )
        diagonal_ref[here, :] = upper.T

        @pl.loop(k + 1, blocks)
        def _(j):
            held_ref[here, span(j)] = zeros

        held_ref[here, here] = jnp.where(row == col, 1.0, 0.0).astype(jnp.float32)
        column = times(held_ref[:, here], inverse, ROWS_BY_ROWS)
        held_ref[:, here] = column
        before_ref[...] = column

        @pl.when(k + 1 < blocks)
        def _():
            held_ref[:, span(k + 1)] = held_ref[:, span(k + 1)] - times(column, before_ref[span(k + 1), :], ROWS_BY_ROWS)

    per = blocks // PANELS
    for h in range(per):
        m = jnp.minimum(place_ref[0], PANELS - 1) * per + h
        for n in range(blocks):
            value = jnp.where(m == n, diagonal_ref[span(m), :], held_ref[span(m), n * BLOCK : (n + 1) * BLOCK])
            mine_ref[h * BLOCK : (h + 1) * BLOCK, n * BLOCK : (n + 1) * BLOCK] = jnp.where(n > m, 0.0, value)
    for n in range(blocks - 1):
        held_ref[(n + 1) * BLOCK :, n * BLOCK : (n + 1) * BLOCK] = jnp.zeros((order - (n + 1) * BLOCK, BLOCK), jnp.float32)


def factor(place, own, other, order):
    pairs = [pair for dealt in dealt_pairs(order // BLOCK) for pair in dealt]
    pairs = jnp.asarray([[m for m, _ in pairs], [n for _, n in pairs]], jnp.int32)
    return pl.pallas_call(
        factor_kernel,
        out_shape=(
            jax.ShapeDtypeStruct((order, order), jnp.float32),
            jax.ShapeDtypeStruct((order // PANELS, order), jnp.float32),
        ),
        in_specs=[SCALARS, SCALARS, WHOLE, WHOLE],
        out_specs=(WHOLE, WHOLE),
        scratch_shapes=[pltpu.VMEM((order, BLOCK), jnp.float32), pltpu.VMEM((order, BLOCK), jnp.float32)],
        compiler_params=pltpu.CompilerParams(vmem_limit_bytes=20 * 2**20),
        cost_estimate=pl.CostEstimate(flops=10**6, bytes_accessed=2**10, transcendentals=0),
        name="factor",
    )(place, pairs, own, other)


def solve_kernel(
    grid_rows, place_ref, own_ref, other_ref, mine_ref, inverse_ref, solved_out, sides_out, solved_ref, sides_ref, rows_ref, sems
):
    total, order = solved_ref.shape
    size = order // PANELS
    per = size // BLOCK
    my_row = place_ref[0]
    for core, source in enumerate((own_ref, other_ref)):
        for step in range(len(SOURCES)):
            col = source_col(place_ref, step, core)
            for line in range(total // BLOCK):
                rows_ref[col, line * BLOCK : (line + 1) * BLOCK, :] = source[step, line]
    inverse = [
        [parts_of(inverse_ref[j * size : (j + 1) * size, k * size : (k + 1) * size]) if k >= j else None for k in range(PANELS)]
        for j in range(PANELS)
    ]
    rows = [parts_of(jnp.concatenate([rows_ref[per * k + h] for h in range(per)], axis=1)) for k in range(PANELS)]
    for k in range(PANELS):
        total_k = times_parts(rows[0], inverse[0][k], ROWS_BY_COLUMNS)
        for j in range(1, k + 1):
            total_k = total_k + times_parts(rows[j], inverse[j][k], ROWS_BY_COLUMNS)
        solved_ref[:, k * size : (k + 1) * size] = total_k

    @pl.when(my_row < PANELS)
    def _():
        solved_ref[0:size, :] = mine_ref[...]

    first = pltpu.make_async_copy(solved_ref, solved_out, sems.at[0])
    first.start()
    tile = lax.broadcasted_iota(jnp.int32, (total, size), 0) // size * grid_rows + my_row
    used = [parts_of(jnp.where(tile > k, solved_ref[:, k * size : (k + 1) * size], 0.0)) for k in range(PANELS)]
    for j in range(PANELS):
        total_j = times_parts(used[j], inverse[j][j], ROWS_BY_ROWS)
        for k in range(j + 1, PANELS):
            total_j = total_j + times_parts(used[k], inverse[j][k], ROWS_BY_ROWS)
        sides_ref[:, j * size : (j + 1) * size] = total_j
    second = pltpu.make_async_copy(sides_ref, sides_out, sems.at[1])
    second.start()
    first.wait()
    second.wait()


def solve(place, own, other, mine, inverse, grid_rows, local_rows):
    total, order = local_rows * mine.shape[0], mine.shape[1]
    out = jax.ShapeDtypeStruct((total, order), jnp.float32)
    return pl.pallas_call(
        functools.partial(solve_kernel, grid_rows),
        out_shape=(out, out),
        in_specs=[SCALARS, WHOLE, WHOLE, WHOLE, WHOLE],
        out_specs=(pl.BlockSpec(memory_space=pltpu.HBM),) * 2,
        scratch_shapes=[
            pltpu.VMEM((total, order), jnp.float32),
            pltpu.VMEM((total, order), jnp.float32),
            pltpu.VMEM((order // BLOCK, total, BLOCK), jnp.float32),
            pltpu.SemaphoreType.DMA((2,)),
        ],
        compiler_params=pltpu.CompilerParams(vmem_limit_bytes=20 * 2**20),
        cost_estimate=pl.CostEstimate(flops=10**6, bytes_accessed=2**10, transcendentals=0),
        name="solve",
    )(place, own, other, mine, inverse)


def change_kernel(sides_ref, across_ref, change_ref):
    order = sides_ref.shape[1]
    across = jnp.concatenate([across_ref[:, u].reshape(BLOCK, order) for u in range(across_ref.shape[1])], axis=0)
    change_ref[...] = times_parts(parts_of(sides_ref[...]), parts_of(across), ROWS_BY_ROWS)


def changes(sides, across, steps, cost):
    total, order = sides.shape
    size = across.shape[0] * across.shape[1] * across.shape[2] // steps
    return pl.pallas_call(
        change_kernel,
        grid=(steps,),
        out_shape=jax.ShapeDtypeStruct((total, steps * size), jnp.float32),
        in_specs=[
            pl.BlockSpec((total, order), lambda t: (0, 0)),
            pl.BlockSpec((across.shape[0], across.shape[1] // steps) + across.shape[2:], lambda t: (0, t, 0, 0)),
        ],
        out_specs=pl.BlockSpec((total, size), lambda t: (0, t)),
        compiler_params=pltpu.CompilerParams(vmem_limit_bytes=60 * 2**20),
        cost_estimate=pl.CostEstimate(flops=cost, bytes_accessed=2**10, transcendentals=0),
        name="changes",
    )(sides, across)


def finish_kernel(grid_rows, grid_cols, place_ref, tiles_ref, change_ref, solved_ref, boost_ref, out_ref):
    my_row, my_col = place_ref[0], place_ref[1]
    size = boost_ref.shape[2]
    halves = size // BLOCK
    bands, count, order = change_ref.shape
    local_cols = order // size
    per = local_cols * halves
    row = lax.broadcasted_iota(jnp.int32, (count, BLOCK), 0) + pl.program_id(0) * count
    col = lax.broadcasted_iota(jnp.int32, (count, BLOCK), 1)
    for band in range(bands):
        i, u = band // halves, band % halves
        line = boost_ref[i * grid_rows + my_row][:, u * BLOCK : (u + 1) * BLOCK]
        for t in range(local_cols):
            on_diagonal = i * grid_rows + my_row == t * grid_cols + my_col
            for h in range(halves):
                first = t * size + h * BLOCK
                value = tiles_ref[pl.ds(band * per + t * halves + h, count, stride=bands * per), :]
                value = value - change_ref[band, :, first : first + BLOCK]
                if u == h:
                    value = value + jnp.where(jnp.logical_and(on_diagonal, row == col), line, 0.0)
                if t == 0:
                    lane = pl.multiple_of(jnp.minimum(my_col, PANELS - 1) * size + h * BLOCK, BLOCK)
                    value = jnp.where(my_col < PANELS, solved_ref[band, :, pl.ds(lane, BLOCK)], value)
                out_ref[band, pl.ds(t * halves + h, count, stride=per), :] = value


def finish(place, tiles, change, solved, boost, grid_rows, grid_cols, steps=4):
    total, order = change.shape
    bands, count = total // BLOCK, BLOCK // steps
    per = order // BLOCK
    rows = pl.BlockSpec((bands, count, order), lambda s: (0, s, 0))
    out = pl.pallas_call(
        functools.partial(finish_kernel, grid_rows, grid_cols),
        grid=(steps,),
        out_shape=jax.ShapeDtypeStruct((bands, BLOCK * per, BLOCK), jnp.float32),
        in_specs=[
            SCALARS,
            pl.BlockSpec((count * bands * per, BLOCK), lambda s: (s, 0)),
            rows,
            rows,
            pl.BlockSpec(boost.shape, lambda s: (0, 0, 0)),
        ],
        out_specs=pl.BlockSpec((bands, count * per, BLOCK), lambda s: (0, s, 0)),
        compiler_params=pltpu.CompilerParams(vmem_limit_bytes=60 * 2**20),
        cost_estimate=pl.CostEstimate(flops=10**6, bytes_accessed=2**10, transcendentals=0),
        name="finish",
    )(place, tiles, change.reshape(bands, BLOCK, order), solved.reshape(bands, BLOCK, order), boost)
    return out


def body(front_entries, child_updates, diag_boost, tile_mask, child_parent, child_index):
    grid_rows = lax.axis_size("row")
    grid_cols = lax.axis_size("col")
    groups = lax.axis_size("front")
    my_group = lax.axis_index("front")
    my_row = lax.axis_index("row")
    my_col = lax.axis_index("col")
    local_rows = front_entries.shape[1]
    slices = front_entries.shape[2]
    local_cols = front_entries.shape[7]
    size = front_entries.shape[8]
    held = child_updates.shape[0]
    child_tiles = child_updates.shape[1]
    halves = grid_rows // grid_cols
    order = PANELS * size

    blocks = order // BLOCK
    parents = child_parent.reshape(groups, held)
    comes = parents == my_group
    index = jnp.sum(jnp.where(comes[:, :, None], child_index.reshape(groups, held, child_tiles), 0), axis=1)
    index = jnp.where(jnp.any(comes, axis=1)[:, None], index, -1)
    mine = lax.dynamic_index_in_dim(parents, my_group, 0, keepdims=False)
    goes = (mine[None, :] == jnp.arange(groups)[:, None])[:, :, None, None, None]
    pieces = child_updates.reshape(held, child_tiles * slices, child_tiles * size // BLOCK, BLOCK)
    slots = jnp.sum(jnp.where(goes, pieces[None], 0.0), axis=1)
    lines_of = lax.all_to_all(slots, "front", split_axis=0, concat_axis=0, tiled=True)
    arrived = lines_of.reshape(groups, child_tiles, slices, child_tiles, size)

    entries = front_entries.reshape(local_rows, slices, grid_rows, grid_cols, local_cols, size)
    mask_tiles = jnp.transpose(tile_mask[0].reshape(local_rows, grid_rows, local_cols, grid_cols), (0, 1, 3, 2))
    kept = (mask_tiles == 1)[:, None, :, :, :, None]
    row_ids = jnp.arange(local_rows)[:, None] * grid_rows + jnp.arange(grid_rows)[None, :]
    col_ids = jnp.arange(local_cols)[:, None] * grid_cols + jnp.arange(grid_cols)[None, :]
    row_hits = (index[:, None, None, :] == row_ids[None, :, :, None]).astype(jnp.float32)
    col_hits = (index[:, None, None, :] == col_ids[None, :, :, None]).astype(jnp.float32)
    within = jnp.arange(slices) * grid_rows * grid_cols + my_row * grid_cols + my_col
    boost = jnp.where(
        within[:, None, None, None] == jnp.arange(size),
        jnp.where(jnp.eye(grid_rows, PANELS, dtype=bool)[:, :, None], diag_boost[0, :PANELS], 0.0),
        0.0,
    )
    boost = jnp.where((jnp.arange(local_rows) == 0)[:, None, None, None, None], boost, 0.0)
    base = jnp.where(kept[:, :, :, :PANELS, 0], entries[:, :, :, :PANELS, 0, :], 0.0) + boost
    children = lines_of.reshape((-1,) + lines_of.shape[2:])
    lines, split = make_panel(index, base.reshape(-1, blocks, BLOCK), children, grid_rows)

    split = lax.all_to_all(split, "col", split_axis=0, concat_axis=0, tiled=True)
    for_cols = jnp.transpose(split, (1, 0, 2, 3)).reshape(local_cols * slices, grid_cols, order)
    lines, for_cols, arrived = lax.optimization_barrier((lines, for_cols, arrived))
    across = lax.all_gather(for_cols, "row", axis=0)

    lines = lines.reshape(grid_rows * grid_cols, -1, 1, BLOCK)
    lines = lax.all_to_all(lines, ("row", "col"), split_axis=0, concat_axis=0, tiled=True)
    lines = jnp.transpose(lines.reshape(grid_rows * grid_cols, -1, BLOCK), (1, 0, 2))

    spread = jnp.einsum("naube,ntpb->nautpe", arrived, col_hits, precision=HIGHEST)
    assembled = jnp.where(kept, entries, 0.0) + jnp.einsum("niqa,nautpe->iuqpte", row_hits, spread, precision=HIGHEST)
    joined = jnp.transpose(assembled, (2, 3, 0, 1, 4, 5))
    joined = joined.reshape(grid_rows * grid_cols, local_rows * slices, local_cols * size // BLOCK, BLOCK)

    lines, joined = lax.optimization_barrier((lines, joined))
    tiles = lax.all_to_all(joined, ("row", "col"), split_axis=0, concat_axis=0, tiled=True).reshape(-1, BLOCK)

    def over_chips(value):
        cols = range(grid_cols)
        moved = [lax.ppermute(value, "col", [(c, (c + 2 * d) % grid_cols) for c in cols]) for d in SOURCES[1:]]
        return jnp.stack([value] + moved)

    def over_cores(value):
        return lax.ppermute(value, "col", [(c, c ^ 1) for c in range(grid_cols)])

    place = jnp.stack([my_row, my_col]).astype(jnp.int32)
    own = over_chips(lines)
    other = over_cores(own)
    inverse, mine = factor(place, own, other, order)
    solved, sides = solve(place, own, other, mine, inverse, grid_rows, local_rows)
    change = changes(sides, across, local_cols, 37 * 10**9)
    out = finish(place, tiles, change, solved, diag_boost[0][:, None, :], grid_rows, grid_cols)
    return out.reshape(1, local_rows, 1, size, local_cols, 1, size)


def solution(mesh):
    placed = (
        P("front", None, None, "row", "col", None, None, None, None),
        P("front", None, None, "row", "col", None, None),
        P("front", None, None),
        P("front", None, None),
        P(),
        P(),
    )
    return jax.shard_map(
        body,
        mesh=mesh,
        in_specs=placed,
        out_specs=P("front", None, "row", None, None, "col", None),
        check_vma=False,
    )
```

```python
import functools

import jax
import jax.numpy as jnp
from jax import lax
from jax.experimental import pallas as pl
from jax.experimental.pallas import tpu as pltpu
from jax.sharding import PartitionSpec as P

PANELS = 4
BLOCK = 128
HIGHEST = lax.Precision.HIGHEST
ROWS_BY_ROWS = (((1,), (1,)), ((), ()))
ROWS_BY_COLUMNS = (((1,), (0,)), ((), ()))
WHOLE = pl.BlockSpec(memory_space=pltpu.VMEM)
SCALARS = pl.BlockSpec(memory_space=pltpu.SMEM)


def times(left, right, numbers):
    return lax.dot_general(left, right, numbers, precision=HIGHEST, preferred_element_type=jnp.float32)


def parts_of(value):
    high = value.astype(jnp.bfloat16)
    return high, (value - high.astype(jnp.float32)).astype(jnp.bfloat16)


def times_parts(left, right, numbers):
    pairs = ((left[0], right[0]), (left[0], right[1]), (left[1], right[0]))
    products = [lax.dot_general(x, y, numbers, preferred_element_type=jnp.float32) for x, y in pairs]
    return products[0] + (products[1] + products[2])


def over_lanes(value, lane):
    return jnp.broadcast_to(value[:, lane : lane + 1], value.shape)


def over_sublanes(value, sublane):
    return jnp.broadcast_to(value[sublane : sublane + 1, :], value.shape)


def factor_block(block):
    groups = BLOCK // 8
    row = lax.broadcasted_iota(jnp.int32, (8, BLOCK), 0)
    lane = lax.broadcasted_iota(jnp.int32, (8, BLOCK), 1)
    rest = [block[8 * g : 8 * g + 8, :] for g in range(groups)]
    extra = [jnp.where(lane == row + 8 * g, 1.0, 0.0).astype(jnp.float32) for g in range(groups)]
    upper, inverse = [], []
    for g in range(groups):
        base = 8 * g
        raw = [[over_lanes(rest[h], base + k) for k in range(8)] for h in range(g, groups)]
        small = [[over_sublanes(raw[0][k], i) if i >= k else None for k in range(8)] for i in range(8)]
        scale = []
        for k in range(8):
            inv = lax.rsqrt(small[k][k])
            inv = inv * (1.5 - 0.5 * small[k][k] * inv * inv)
            scale.append(inv)
            for i in range(k + 1, 8):
                small[i][k] = small[i][k] * inv
            for j in range(k + 1, 8):
                for i in range(j, 8):
                    small[i][j] = small[i][j] - small[i][k] * small[j][k]

        def forward(parts, small=small, scale=scale):
            done = []
            for k in range(8):
                part = parts[k]
                for m in range(k):
                    part = part - small[k][m] * done[m]
                done.append(part * scale[k])
            return done

        wide = forward([over_sublanes(rest[g], k) for k in range(8)])
        solved = forward([over_sublanes(extra[g], k) for k in range(8)])
        upper_rows, inverse_rows = wide[0], solved[0]
        for k in range(1, 8):
            upper_rows = jnp.where(row == k, wide[k], upper_rows)
            inverse_rows = jnp.where(row == k, solved[k], inverse_rows)
        upper.append(jnp.where(lane >= row + base, upper_rows, 0.0))
        inverse.append(inverse_rows)
        for h in range(g + 1, groups):
            tall = forward(raw[h - g])
            for k in range(8):
                rest[h] = rest[h] - tall[k] * wide[k]
                extra[h] = extra[h] - tall[k] * solved[k]
    return jnp.concatenate(upper, 0), jnp.concatenate(inverse, 0)


def dealt_pairs(blocks):
    share = (blocks + 2) // 2
    dealt = [None] * blocks
    for a in range(blocks // 2):
        both = [(m, a) for m in range(a, blocks)] + [(m, blocks - 1 - a) for m in range(blocks - 1 - a, blocks)]
        dealt[a], dealt[blocks - 1 - a] = both[:share], both[share:]
    return [pairs + [(0, blocks - 1)] * (share - len(pairs)) for pairs in dealt]


def panel_kernel(grid_rows, index_ref, base_ref, narrow_ref, lines_ref, split_ref, rows_ref):
    groups, child_tiles = index_ref.shape
    total, blocks, _ = base_ref.shape
    slices = narrow_ref.shape[0] // (groups * child_tiles)
    local_rows = total // (slices * grid_rows)
    halves = blocks // PANELS
    dealt = dealt_pairs(blocks)
    share = len(dealt[0])
    per = local_rows * slices + share
    rows_ref[...] = base_ref[...]
    tile_of = lax.broadcasted_iota(jnp.int32, (blocks, BLOCK), 0) // halves
    for g in range(groups):
        moved = []
        for shift in range(PANELS):
            here = jnp.zeros((blocks, BLOCK), jnp.int32)
            for k in range(shift, PANELS):
                here = jnp.where(tile_of == k, (index_ref[g, k - shift] == k).astype(jnp.int32), here)
            moved.append(here == 1)
        for a in range(child_tiles):
            tile = jnp.maximum(index_ref[g, a], 0)
            for u in range(slices):
                at = (tile // grid_rows * slices + u) * grid_rows + lax.rem(tile, grid_rows)
                part = narrow_ref[(g * child_tiles + a) * slices + u][:blocks]
                added = jnp.where(moved[0], part, 0.0)
                for shift in range(1, PANELS):
                    added = added + jnp.where(moved[shift], pltpu.roll(part, shift * halves, 0), 0.0)
                rows_ref[at] = rows_ref[at] + added
    for q in range(grid_rows):
        for line in range(local_rows * slices):
            value = rows_ref[line * grid_rows + q]
            for p in range(blocks):
                lines_ref[(q * blocks + p) * per + line] = value[p : p + 1, :]
    for p in range(blocks):
        for j, (m, n) in enumerate(dealt[p]):
            value = rows_ref[m % slices * grid_rows + m // slices][n : n + 1, :]
            for q in range(grid_rows):
                lines_ref[(q * blocks + p) * per + local_rows * slices + j] = value
    halves = grid_rows // blocks
    for p in range(blocks):
        for i in range(local_rows):
            for h in range(halves):
                for u in range(slices):
                    split_ref[p, (i * halves + h) * slices + u] = rows_ref[(i * slices + u) * grid_rows + h * blocks + p]


def make_panel(index, base, narrow, grid_rows):
    total, blocks, _ = base.shape
    per = total // grid_rows + len(dealt_pairs(blocks)[0])
    return pl.pallas_call(
        functools.partial(panel_kernel, grid_rows),
        out_shape=(
            jax.ShapeDtypeStruct((grid_rows * blocks * per, 1, BLOCK), jnp.float32),
            jax.ShapeDtypeStruct((blocks, total // blocks, blocks, BLOCK), jnp.float32),
        ),
        in_specs=[SCALARS, WHOLE, WHOLE],
        out_specs=(WHOLE, WHOLE),
        scratch_shapes=[pltpu.VMEM(base.shape, jnp.float32)],
        cost_estimate=pl.CostEstimate(flops=10**6, bytes_accessed=2 * 2**20, transcendentals=0),
        name="panel",
    )(index, base, narrow)


SOURCES = (0, 1, -1, 2)


def source_col(place_ref, step, core):
    chip = lax.rem(place_ref[1] // 2 - SOURCES[step] + 4, 4)
    mine = lax.rem(place_ref[1], 2)
    return chip * 2 + (mine if core == 0 else 1 - mine)


def factor_kernel(place_ref, pairs_ref, own_ref, other_ref, inverse_ref, mine_ref, diagonal_ref, before_ref):
    order = inverse_ref.shape[0]
    blocks = order // BLOCK
    dealt = pairs_ref.shape[1] // blocks
    skipped = own_ref.shape[1] - dealt
    held_ref = inverse_ref
    row = lax.broadcasted_iota(jnp.int32, (BLOCK, BLOCK), 0)
    col = lax.broadcasted_iota(jnp.int32, (BLOCK, BLOCK), 1)
    any_row = lax.broadcasted_iota(jnp.int32, (order, BLOCK), 0)
    zeros = jnp.zeros((BLOCK, BLOCK), jnp.float32)
    wide = 2 * BLOCK

    def span(k):
        return pl.ds(pl.multiple_of(k * BLOCK, BLOCK), BLOCK)

    held_ref[...] = jnp.zeros_like(held_ref)
    before_ref[...] = jnp.zeros_like(before_ref)
    for core, source in enumerate((own_ref, other_ref)):
        for step in range(len(SOURCES)):
            first = source_col(place_ref, step, core) * dealt
            for j in range(dealt):
                held_ref[span(pairs_ref[0, first + j]), span(pairs_ref[1, first + j])] = source[step, skipped + j]

    @pl.loop(0, blocks)
    def _(k):
        here = span(k)
        block = held_ref[here, here]
        block = jnp.where(row >= col, block, 0.0) + jnp.where(col > row, jnp.where(row > col, block, 0.0).T, 0.0)
        before = before_ref[...]
        later = jnp.where(any_row >= (k + 1) * BLOCK, before, 0.0)
        upper, inverse = factor_block(block)
        for start in range(0, order, wide):
            held_ref[:, start : start + wide] = held_ref[:, start : start + wide] - times(
                before, later[start : start + wide], ROWS_BY_ROWS
            )
        diagonal_ref[here, :] = upper.T

        @pl.loop(k + 1, blocks)
        def _(j):
            held_ref[here, span(j)] = zeros

        held_ref[here, here] = jnp.where(row == col, 1.0, 0.0).astype(jnp.float32)
        column = times(held_ref[:, here], inverse, ROWS_BY_ROWS)
        held_ref[:, here] = column
        before_ref[...] = column

        @pl.when(k + 1 < blocks)
        def _():
            held_ref[:, span(k + 1)] = held_ref[:, span(k + 1)] - times(column, before_ref[span(k + 1), :], ROWS_BY_ROWS)

    per = blocks // PANELS
    for h in range(per):
        m = jnp.minimum(place_ref[0], PANELS - 1) * per + h
        for n in range(blocks):
            value = jnp.where(m == n, diagonal_ref[span(m), :], held_ref[span(m), n * BLOCK : (n + 1) * BLOCK])
            mine_ref[h * BLOCK : (h + 1) * BLOCK, n * BLOCK : (n + 1) * BLOCK] = jnp.where(n > m, 0.0, value)
    for n in range(blocks - 1):
        held_ref[(n + 1) * BLOCK :, n * BLOCK : (n + 1) * BLOCK] = jnp.zeros((order - (n + 1) * BLOCK, BLOCK), jnp.float32)


def factor(place, own, other, order):
    pairs = [pair for dealt in dealt_pairs(order // BLOCK) for pair in dealt]
    pairs = jnp.asarray([[m for m, _ in pairs], [n for _, n in pairs]], jnp.int32)
    return pl.pallas_call(
        factor_kernel,
        out_shape=(
            jax.ShapeDtypeStruct((order, order), jnp.float32),
            jax.ShapeDtypeStruct((order // PANELS, order), jnp.float32),
        ),
        in_specs=[SCALARS, SCALARS, WHOLE, WHOLE],
        out_specs=(WHOLE, WHOLE),
        scratch_shapes=[pltpu.VMEM((order, BLOCK), jnp.float32), pltpu.VMEM((order, BLOCK), jnp.float32)],
        compiler_params=pltpu.CompilerParams(vmem_limit_bytes=20 * 2**20),
        cost_estimate=pl.CostEstimate(flops=10**6, bytes_accessed=2**10, transcendentals=0),
        name="factor",
    )(place, pairs, own, other)


def solve_kernel(
    grid_rows, place_ref, own_ref, other_ref, mine_ref, inverse_ref, solved_out, sides_out, solved_ref, sides_ref, rows_ref, sems
):
    total, order = solved_ref.shape
    size = order // PANELS
    per = size // BLOCK
    my_row = place_ref[0]
    for core, source in enumerate((own_ref, other_ref)):
        for step in range(len(SOURCES)):
            col = source_col(place_ref, step, core)
            for line in range(total // BLOCK):
                rows_ref[col, line * BLOCK : (line + 1) * BLOCK, :] = source[step, line]
    inverse = [
        [parts_of(inverse_ref[j * size : (j + 1) * size, k * size : (k + 1) * size]) if k >= j else None for k in range(PANELS)]
        for j in range(PANELS)
    ]
    rows = [parts_of(jnp.concatenate([rows_ref[per * k + h] for h in range(per)], axis=1)) for k in range(PANELS)]
    for k in range(PANELS):
        total_k = times_parts(rows[0], inverse[0][k], ROWS_BY_COLUMNS)
        for j in range(1, k + 1):
            total_k = total_k + times_parts(rows[j], inverse[j][k], ROWS_BY_COLUMNS)
        solved_ref[:, k * size : (k + 1) * size] = total_k

    @pl.when(my_row < PANELS)
    def _():
        solved_ref[0:size, :] = mine_ref[...]

    first = pltpu.make_async_copy(solved_ref, solved_out, sems.at[0])
    first.start()
    tile = lax.broadcasted_iota(jnp.int32, (total, size), 0) // size * grid_rows + my_row
    used = [parts_of(jnp.where(tile > k, solved_ref[:, k * size : (k + 1) * size], 0.0)) for k in range(PANELS)]
    for j in range(PANELS):
        total_j = times_parts(used[j], inverse[j][j], ROWS_BY_ROWS)
        for k in range(j + 1, PANELS):
            total_j = total_j + times_parts(used[k], inverse[j][k], ROWS_BY_ROWS)
        sides_ref[:, j * size : (j + 1) * size] = total_j
    second = pltpu.make_async_copy(sides_ref, sides_out, sems.at[1])
    second.start()
    first.wait()
    second.wait()


def solve(place, own, other, mine, inverse, grid_rows, local_rows):
    total, order = local_rows * mine.shape[0], mine.shape[1]
    out = jax.ShapeDtypeStruct((total, order), jnp.float32)
    return pl.pallas_call(
        functools.partial(solve_kernel, grid_rows),
        out_shape=(out, out),
        in_specs=[SCALARS, WHOLE, WHOLE, WHOLE, WHOLE],
        out_specs=(pl.BlockSpec(memory_space=pltpu.HBM),) * 2,
        scratch_shapes=[
            pltpu.VMEM((total, order), jnp.float32),
            pltpu.VMEM((total, order), jnp.float32),
            pltpu.VMEM((order // BLOCK, total, BLOCK), jnp.float32),
            pltpu.SemaphoreType.DMA((2,)),
        ],
        compiler_params=pltpu.CompilerParams(vmem_limit_bytes=20 * 2**20),
        cost_estimate=pl.CostEstimate(flops=10**6, bytes_accessed=2**10, transcendentals=0),
        name="solve",
    )(place, own, other, mine, inverse)


def change_kernel(sides_ref, across_ref, change_ref, high_ref, low_ref):
    order = sides_ref.shape[1]

    @pl.when(pl.program_id(0) == 0)
    def _():
        high_ref[...], low_ref[...] = parts_of(sides_ref[...])

    across = jnp.concatenate([across_ref[:, u].reshape(BLOCK, order) for u in range(across_ref.shape[1])], axis=0)
    change_ref[...] = times_parts((high_ref[...], low_ref[...]), parts_of(across), ROWS_BY_ROWS)


def changes(sides, across, steps, cost):
    total, order = sides.shape
    size = across.shape[0] * across.shape[1] * across.shape[2] // steps
    return pl.pallas_call(
        change_kernel,
        grid=(steps,),
        out_shape=jax.ShapeDtypeStruct((total, steps * size), jnp.float32),
        in_specs=[
            pl.BlockSpec((total, order), lambda t: (0, 0)),
            pl.BlockSpec((across.shape[0], across.shape[1] // steps) + across.shape[2:], lambda t: (0, t, 0, 0)),
        ],
        out_specs=pl.BlockSpec((total, size), lambda t: (0, t)),
        scratch_shapes=[pltpu.VMEM((total, order), jnp.bfloat16), pltpu.VMEM((total, order), jnp.bfloat16)],
        compiler_params=pltpu.CompilerParams(vmem_limit_bytes=60 * 2**20),
        cost_estimate=pl.CostEstimate(flops=cost, bytes_accessed=2**10, transcendentals=0),
        name="changes",
    )(sides, across)


def finish_kernel(grid_rows, grid_cols, place_ref, tiles_ref, change_ref, solved_ref, boost_ref, out_ref):
    my_row, my_col = place_ref[0], place_ref[1]
    size = boost_ref.shape[2]
    halves = size // BLOCK
    bands, count, order = change_ref.shape
    local_cols = order // size
    per = local_cols * halves
    row = lax.broadcasted_iota(jnp.int32, (count, BLOCK), 0) + pl.program_id(0) * count
    col = lax.broadcasted_iota(jnp.int32, (count, BLOCK), 1)
    for band in range(bands):
        i, u = band // halves, band % halves
        line = boost_ref[i * grid_rows + my_row][:, u * BLOCK : (u + 1) * BLOCK]
        for t in range(local_cols):
            on_diagonal = i * grid_rows + my_row == t * grid_cols + my_col
            for h in range(halves):
                first = t * size + h * BLOCK
                value = tiles_ref[pl.ds(band * per + t * halves + h, count, stride=bands * per), :]
                value = value - change_ref[band, :, first : first + BLOCK]
                if u == h:
                    value = value + jnp.where(jnp.logical_and(on_diagonal, row == col), line, 0.0)
                if t == 0:
                    lane = pl.multiple_of(jnp.minimum(my_col, PANELS - 1) * size + h * BLOCK, BLOCK)
                    value = jnp.where(my_col < PANELS, solved_ref[band, :, pl.ds(lane, BLOCK)], value)
                out_ref[band, pl.ds(t * halves + h, count, stride=per), :] = value


def finish(place, tiles, change, solved, boost, grid_rows, grid_cols, steps=4):
    total, order = change.shape
    bands, count = total // BLOCK, BLOCK // steps
    per = order // BLOCK
    rows = pl.BlockSpec((bands, count, order), lambda s: (0, s, 0))
    out = pl.pallas_call(
        functools.partial(finish_kernel, grid_rows, grid_cols),
        grid=(steps,),
        out_shape=jax.ShapeDtypeStruct((bands, BLOCK * per, BLOCK), jnp.float32),
        in_specs=[
            SCALARS,
            pl.BlockSpec((count * bands * per, BLOCK), lambda s: (s, 0)),
            rows,
            rows,
            pl.BlockSpec(boost.shape, lambda s: (0, 0, 0)),
        ],
        out_specs=pl.BlockSpec((bands, count * per, BLOCK), lambda s: (0, s, 0)),
        compiler_params=pltpu.CompilerParams(vmem_limit_bytes=60 * 2**20),
        cost_estimate=pl.CostEstimate(flops=10**6, bytes_accessed=2**10, transcendentals=0),
        name="finish",
    )(place, tiles, change.reshape(bands, BLOCK, order), solved.reshape(bands, BLOCK, order), boost)
    return out


def body(front_entries, child_updates, diag_boost, tile_mask, child_parent, child_index):
    grid_rows = lax.axis_size("row")
    grid_cols = lax.axis_size("col")
    groups = lax.axis_size("front")
    my_group = lax.axis_index("front")
    my_row = lax.axis_index("row")
    my_col = lax.axis_index("col")
    local_rows = front_entries.shape[1]
    slices = front_entries.shape[2]
    local_cols = front_entries.shape[7]
    size = front_entries.shape[8]
    held = child_updates.shape[0]
    child_tiles = child_updates.shape[1]
    halves = grid_rows // grid_cols
    order = PANELS * size

    blocks = order // BLOCK
    parents = child_parent.reshape(groups, held)
    comes = parents == my_group
    index = jnp.sum(jnp.where(comes[:, :, None], child_index.reshape(groups, held, child_tiles), 0), axis=1)
    index = jnp.where(jnp.any(comes, axis=1)[:, None], index, -1)
    mine = lax.dynamic_index_in_dim(parents, my_group, 0, keepdims=False)
    goes = (mine[None, :] == jnp.arange(groups)[:, None])[:, :, None, None, None]
    pieces = child_updates.reshape(held, child_tiles * slices, child_tiles * size // BLOCK, BLOCK)
    slots = jnp.sum(jnp.where(goes, pieces[None], 0.0), axis=1)
    lines_of = lax.all_to_all(slots, "front", split_axis=0, concat_axis=0, tiled=True)
    arrived = lines_of.reshape(groups, child_tiles, slices, child_tiles, size)

    entries = front_entries.reshape(local_rows, slices, grid_rows, grid_cols, local_cols, size)
    mask_tiles = jnp.transpose(tile_mask[0].reshape(local_rows, grid_rows, local_cols, grid_cols), (0, 1, 3, 2))
    kept = (mask_tiles == 1)[:, None, :, :, :, None]
    row_ids = jnp.arange(local_rows)[:, None] * grid_rows + jnp.arange(grid_rows)[None, :]
    col_ids = jnp.arange(local_cols)[:, None] * grid_cols + jnp.arange(grid_cols)[None, :]
    row_hits = (index[:, None, None, :] == row_ids[None, :, :, None]).astype(jnp.float32)
    col_hits = (index[:, None, None, :] == col_ids[None, :, :, None]).astype(jnp.float32)
    within = jnp.arange(slices) * grid_rows * grid_cols + my_row * grid_cols + my_col
    boost = jnp.where(
        within[:, None, None, None] == jnp.arange(size),
        jnp.where(jnp.eye(grid_rows, PANELS, dtype=bool)[:, :, None], diag_boost[0, :PANELS], 0.0),
        0.0,
    )
    boost = jnp.where((jnp.arange(local_rows) == 0)[:, None, None, None, None], boost, 0.0)
    base = jnp.where(kept[:, :, :, :PANELS, 0], entries[:, :, :, :PANELS, 0, :], 0.0) + boost
    children = lines_of.reshape((-1,) + lines_of.shape[2:])
    lines, split = make_panel(index, base.reshape(-1, blocks, BLOCK), children, grid_rows)

    split = lax.all_to_all(split, "col", split_axis=0, concat_axis=0, tiled=True)
    for_cols = jnp.transpose(split, (1, 0, 2, 3)).reshape(local_cols * slices, grid_cols, order)
    lines, for_cols, arrived = lax.optimization_barrier((lines, for_cols, arrived))
    across = lax.all_gather(for_cols, "row", axis=0)

    lines = lines.reshape(grid_rows * grid_cols, -1, 1, BLOCK)
    lines = lax.all_to_all(lines, ("row", "col"), split_axis=0, concat_axis=0, tiled=True)
    lines = jnp.transpose(lines.reshape(grid_rows * grid_cols, -1, BLOCK), (1, 0, 2))

    spread = jnp.einsum("naube,ntpb->nautpe", arrived, col_hits, precision=HIGHEST)
    assembled = jnp.where(kept, entries, 0.0) + jnp.einsum("niqa,nautpe->iuqpte", row_hits, spread, precision=HIGHEST)
    joined = jnp.transpose(assembled, (2, 3, 0, 1, 4, 5))
    joined = joined.reshape(grid_rows * grid_cols, local_rows * slices, local_cols * size // BLOCK, BLOCK)

    lines, joined = lax.optimization_barrier((lines, joined))
    tiles = lax.all_to_all(joined, ("row", "col"), split_axis=0, concat_axis=0, tiled=True).reshape(-1, BLOCK)

    def over_chips(value):
        cols = range(grid_cols)
        moved = [lax.ppermute(value, "col", [(c, (c + 2 * d) % grid_cols) for c in cols]) for d in SOURCES[1:]]
        return jnp.stack([value] + moved)

    def over_cores(value):
        return lax.ppermute(value, "col", [(c, c ^ 1) for c in range(grid_cols)])

    place = jnp.stack([my_row, my_col]).astype(jnp.int32)
    own = over_chips(lines)
    other = over_cores(own)
    inverse, mine = factor(place, own, other, order)
    solved, sides = solve(place, own, other, mine, inverse, grid_rows, local_rows)
    change = changes(sides, across, local_cols, 59 * 10**9)
    out = finish(place, tiles, change, solved, diag_boost[0][:, None, :], grid_rows, grid_cols)
    return out.reshape(1, local_rows, 1, size, local_cols, 1, size)


def solution(mesh):
    placed = (
        P("front", None, None, "row", "col", None, None, None, None),
        P("front", None, None, "row", "col", None, None),
        P("front", None, None),
        P("front", None, None),
        P(),
        P(),
    )
    return jax.shard_map(
        body,
        mesh=mesh,
        in_specs=placed,
        out_specs=P("front", None, "row", None, None, "col", None),
        check_vma=False,
    )
```

```python
import functools

import jax
import jax.numpy as jnp
from jax import lax
from jax.experimental import pallas as pl
from jax.experimental.pallas import tpu as pltpu
from jax.sharding import PartitionSpec as P

PANELS = 4
BLOCK = 128
HIGHEST = lax.Precision.HIGHEST
ROWS_BY_ROWS = (((1,), (1,)), ((), ()))
ROWS_BY_COLUMNS = (((1,), (0,)), ((), ()))
WHOLE = pl.BlockSpec(memory_space=pltpu.VMEM)
SCALARS = pl.BlockSpec(memory_space=pltpu.SMEM)


def times(left, right, numbers):
    return lax.dot_general(left, right, numbers, precision=HIGHEST, preferred_element_type=jnp.float32)


def parts_of(value):
    high = value.astype(jnp.bfloat16)
    return high, (value - high.astype(jnp.float32)).astype(jnp.bfloat16)


def times_parts(left, right, numbers):
    pairs = ((left[0], right[0]), (left[0], right[1]), (left[1], right[0]))
    products = [lax.dot_general(x, y, numbers, preferred_element_type=jnp.float32) for x, y in pairs]
    return products[0] + (products[1] + products[2])


def over_lanes(value, lane):
    return jnp.broadcast_to(value[:, lane : lane + 1], value.shape)


def over_sublanes(value, sublane):
    return jnp.broadcast_to(value[sublane : sublane + 1, :], value.shape)


def factor_block(block):
    groups = BLOCK // 8
    row = lax.broadcasted_iota(jnp.int32, (8, BLOCK), 0)
    lane = lax.broadcasted_iota(jnp.int32, (8, BLOCK), 1)
    rest = [block[8 * g : 8 * g + 8, :] for g in range(groups)]
    extra = [jnp.where(lane == row + 8 * g, 1.0, 0.0).astype(jnp.float32) for g in range(groups)]
    upper, inverse = [], []
    for g in range(groups):
        base = 8 * g
        raw = [[over_lanes(rest[h], base + k) for k in range(8)] for h in range(g, groups)]
        small = [[over_sublanes(raw[0][k], i) if i >= k else None for k in range(8)] for i in range(8)]
        scale = []
        for k in range(8):
            inv = lax.rsqrt(small[k][k])
            inv = inv * (1.5 - 0.5 * small[k][k] * inv * inv)
            scale.append(inv)
            for i in range(k + 1, 8):
                small[i][k] = small[i][k] * inv
            for j in range(k + 1, 8):
                for i in range(j, 8):
                    small[i][j] = small[i][j] - small[i][k] * small[j][k]

        def forward(parts, small=small, scale=scale):
            done = []
            for k in range(8):
                part = parts[k]
                for m in range(k):
                    part = part - small[k][m] * done[m]
                done.append(part * scale[k])
            return done

        wide = forward([over_sublanes(rest[g], k) for k in range(8)])
        solved = forward([over_sublanes(extra[g], k) for k in range(8)])
        upper_rows, inverse_rows = wide[0], solved[0]
        for k in range(1, 8):
            upper_rows = jnp.where(row == k, wide[k], upper_rows)
            inverse_rows = jnp.where(row == k, solved[k], inverse_rows)
        upper.append(jnp.where(lane >= row + base, upper_rows, 0.0))
        inverse.append(inverse_rows)
        for h in range(g + 1, groups):
            tall = forward(raw[h - g])
            for k in range(8):
                rest[h] = rest[h] - tall[k] * wide[k]
                extra[h] = extra[h] - tall[k] * solved[k]
    return jnp.concatenate(upper, 0), jnp.concatenate(inverse, 0)


def dealt_pairs(blocks):
    share = (blocks + 2) // 2
    dealt = [None] * blocks
    for a in range(blocks // 2):
        both = [(m, a) for m in range(a, blocks)] + [(m, blocks - 1 - a) for m in range(blocks - 1 - a, blocks)]
        dealt[a], dealt[blocks - 1 - a] = both[:share], both[share:]
    return [pairs + [(0, blocks - 1)] * (share - len(pairs)) for pairs in dealt]


def panel_kernel(grid_rows, index_ref, base_ref, narrow_ref, lines_ref, split_ref, rows_ref):
    groups, child_tiles = index_ref.shape
    total, blocks, _ = base_ref.shape
    slices = narrow_ref.shape[0] // (groups * child_tiles)
    local_rows = total // (slices * grid_rows)
    halves = blocks // PANELS
    dealt = dealt_pairs(blocks)
    share = len(dealt[0])
    per = local_rows * slices + share
    rows_ref[...] = base_ref[...]
    tile_of = lax.broadcasted_iota(jnp.int32, (blocks, BLOCK), 0) // halves
    for g in range(groups):
        moved = []
        for shift in range(PANELS):
            here = jnp.zeros((blocks, BLOCK), jnp.int32)
            for k in range(shift, PANELS):
                here = jnp.where(tile_of == k, (index_ref[g, k - shift] == k).astype(jnp.int32), here)
            moved.append(here == 1)
        for a in range(child_tiles):
            tile = jnp.maximum(index_ref[g, a], 0)
            for u in range(slices):
                at = (tile // grid_rows * slices + u) * grid_rows + lax.rem(tile, grid_rows)
                part = narrow_ref[(g * child_tiles + a) * slices + u][:blocks]
                added = jnp.where(moved[0], part, 0.0)
                for shift in range(1, PANELS):
                    added = added + jnp.where(moved[shift], pltpu.roll(part, shift * halves, 0), 0.0)
                rows_ref[at] = rows_ref[at] + added
    for q in range(grid_rows):
        for line in range(local_rows * slices):
            value = rows_ref[line * grid_rows + q]
            for p in range(blocks):
                lines_ref[(q * blocks + p) * per + line] = value[p : p + 1, :]
    for p in range(blocks):
        for j, (m, n) in enumerate(dealt[p]):
            value = rows_ref[m % slices * grid_rows + m // slices][n : n + 1, :]
            for q in range(grid_rows):
                lines_ref[(q * blocks + p) * per + local_rows * slices + j] = value
    halves = grid_rows // blocks
    for p in range(blocks):
        for i in range(local_rows):
            for h in range(halves):
                for u in range(slices):
                    split_ref[p, (i * halves + h) * slices + u] = rows_ref[(i * slices + u) * grid_rows + h * blocks + p]


def make_panel(index, base, narrow, grid_rows):
    total, blocks, _ = base.shape
    per = total // grid_rows + len(dealt_pairs(blocks)[0])
    return pl.pallas_call(
        functools.partial(panel_kernel, grid_rows),
        out_shape=(
            jax.ShapeDtypeStruct((grid_rows * blocks * per, 1, BLOCK), jnp.float32),
            jax.ShapeDtypeStruct((blocks, total // blocks, blocks, BLOCK), jnp.float32),
        ),
        in_specs=[SCALARS, WHOLE, WHOLE],
        out_specs=(WHOLE, WHOLE),
        scratch_shapes=[pltpu.VMEM(base.shape, jnp.float32)],
        cost_estimate=pl.CostEstimate(flops=10**6, bytes_accessed=2 * 2**20, transcendentals=0),
        name="panel",
    )(index, base, narrow)


SOURCES = (0, 1, -1, 2)


def source_col(place_ref, step, core):
    chip = lax.rem(place_ref[1] // 2 - SOURCES[step] + 4, 4)
    mine = lax.rem(place_ref[1], 2)
    return chip * 2 + (mine if core == 0 else 1 - mine)


def factor_kernel(place_ref, pairs_ref, own_ref, other_ref, inverse_ref, mine_ref, diagonal_ref, before_ref):
    order = inverse_ref.shape[0]
    blocks = order // BLOCK
    dealt = pairs_ref.shape[1] // blocks
    skipped = own_ref.shape[1] - dealt
    held_ref = inverse_ref
    row = lax.broadcasted_iota(jnp.int32, (BLOCK, BLOCK), 0)
    col = lax.broadcasted_iota(jnp.int32, (BLOCK, BLOCK), 1)
    any_row = lax.broadcasted_iota(jnp.int32, (order, BLOCK), 0)
    zeros = jnp.zeros((BLOCK, BLOCK), jnp.float32)
    wide = 2 * BLOCK

    def span(k):
        return pl.ds(pl.multiple_of(k * BLOCK, BLOCK), BLOCK)

    held_ref[...] = jnp.zeros_like(held_ref)
    before_ref[...] = jnp.zeros_like(before_ref)
    for core, source in enumerate((own_ref, other_ref)):
        for step in range(len(SOURCES)):
            first = source_col(place_ref, step, core) * dealt
            for j in range(dealt):
                held_ref[span(pairs_ref[0, first + j]), span(pairs_ref[1, first + j])] = source[step, skipped + j]

    @pl.loop(0, blocks)
    def _(k):
        here = span(k)
        block = held_ref[here, here]
        block = jnp.where(row >= col, block, 0.0) + jnp.where(col > row, jnp.where(row > col, block, 0.0).T, 0.0)
        before = before_ref[...]
        later = jnp.where(any_row >= (k + 1) * BLOCK, before, 0.0)
        upper, inverse = factor_block(block)
        for start in range(0, order, wide):
            held_ref[:, start : start + wide] = held_ref[:, start : start + wide] - times(
                before, later[start : start + wide], ROWS_BY_ROWS
            )
        diagonal_ref[here, :] = upper.T

        @pl.loop(k + 1, blocks)
        def _(j):
            held_ref[here, span(j)] = zeros

        held_ref[here, here] = jnp.where(row == col, 1.0, 0.0).astype(jnp.float32)
        column = times(held_ref[:, here], inverse, ROWS_BY_ROWS)
        held_ref[:, here] = column
        before_ref[...] = column

        @pl.when(k + 1 < blocks)
        def _():
            held_ref[:, span(k + 1)] = held_ref[:, span(k + 1)] - times(column, before_ref[span(k + 1), :], ROWS_BY_ROWS)

    per = blocks // PANELS
    for h in range(per):
        m = jnp.minimum(place_ref[0], PANELS - 1) * per + h
        for n in range(blocks):
            value = jnp.where(m == n, diagonal_ref[span(m), :], held_ref[span(m), n * BLOCK : (n + 1) * BLOCK])
            mine_ref[h * BLOCK : (h + 1) * BLOCK, n * BLOCK : (n + 1) * BLOCK] = jnp.where(n > m, 0.0, value)
    for n in range(blocks - 1):
        held_ref[(n + 1) * BLOCK :, n * BLOCK : (n + 1) * BLOCK] = jnp.zeros((order - (n + 1) * BLOCK, BLOCK), jnp.float32)


def factor(place, own, other, order):
    pairs = [pair for dealt in dealt_pairs(order // BLOCK) for pair in dealt]
    pairs = jnp.asarray([[m for m, _ in pairs], [n for _, n in pairs]], jnp.int32)
    return pl.pallas_call(
        factor_kernel,
        out_shape=(
            jax.ShapeDtypeStruct((order, order), jnp.float32),
            jax.ShapeDtypeStruct((order // PANELS, order), jnp.float32),
        ),
        in_specs=[SCALARS, SCALARS, WHOLE, WHOLE],
        out_specs=(WHOLE, WHOLE),
        scratch_shapes=[pltpu.VMEM((order, BLOCK), jnp.float32), pltpu.VMEM((order, BLOCK), jnp.float32)],
        compiler_params=pltpu.CompilerParams(vmem_limit_bytes=20 * 2**20),
        cost_estimate=pl.CostEstimate(flops=10**6, bytes_accessed=2**10, transcendentals=0),
        name="factor",
    )(place, pairs, own, other)


def solve_kernel(
    grid_rows, place_ref, own_ref, other_ref, mine_ref, inverse_ref, solved_out, sides_out, solved_ref, sides_ref, rows_ref, sems
):
    total, order = solved_ref.shape
    size = order // PANELS
    per = size // BLOCK
    my_row = place_ref[0]
    for core, source in enumerate((own_ref, other_ref)):
        for step in range(len(SOURCES)):
            col = source_col(place_ref, step, core)
            for line in range(total // BLOCK):
                rows_ref[col, line * BLOCK : (line + 1) * BLOCK, :] = source[step, line]
    inverse = [
        [parts_of(inverse_ref[j * size : (j + 1) * size, k * size : (k + 1) * size]) if k >= j else None for k in range(PANELS)]
        for j in range(PANELS)
    ]
    rows = [parts_of(jnp.concatenate([rows_ref[per * k + h] for h in range(per)], axis=1)) for k in range(PANELS)]
    for k in range(PANELS):
        total_k = times_parts(rows[0], inverse[0][k], ROWS_BY_COLUMNS)
        for j in range(1, k + 1):
            total_k = total_k + times_parts(rows[j], inverse[j][k], ROWS_BY_COLUMNS)
        solved_ref[:, k * size : (k + 1) * size] = total_k

    @pl.when(my_row < PANELS)
    def _():
        solved_ref[0:size, :] = mine_ref[...]

    first = pltpu.make_async_copy(solved_ref, solved_out, sems.at[0])
    first.start()
    tile = lax.broadcasted_iota(jnp.int32, (total, size), 0) // size * grid_rows + my_row
    used = [parts_of(jnp.where(tile > k, solved_ref[:, k * size : (k + 1) * size], 0.0)) for k in range(PANELS)]
    for j in range(PANELS):
        total_j = times_parts(used[j], inverse[j][j], ROWS_BY_ROWS)
        for k in range(j + 1, PANELS):
            total_j = total_j + times_parts(used[k], inverse[j][k], ROWS_BY_ROWS)
        sides_ref[:, j * size : (j + 1) * size] = total_j
    second = pltpu.make_async_copy(sides_ref, sides_out, sems.at[1])
    second.start()
    first.wait()
    second.wait()


def solve(place, own, other, mine, inverse, grid_rows, local_rows):
    total, order = local_rows * mine.shape[0], mine.shape[1]
    out = jax.ShapeDtypeStruct((total, order), jnp.float32)
    return pl.pallas_call(
        functools.partial(solve_kernel, grid_rows),
        out_shape=(out, out),
        in_specs=[SCALARS, WHOLE, WHOLE, WHOLE, WHOLE],
        out_specs=(pl.BlockSpec(memory_space=pltpu.HBM),) * 2,
        scratch_shapes=[
            pltpu.VMEM((total, order), jnp.float32),
            pltpu.VMEM((total, order), jnp.float32),
            pltpu.VMEM((order // BLOCK, total, BLOCK), jnp.float32),
            pltpu.SemaphoreType.DMA((2,)),
        ],
        compiler_params=pltpu.CompilerParams(vmem_limit_bytes=20 * 2**20),
        cost_estimate=pl.CostEstimate(flops=10**6, bytes_accessed=2**10, transcendentals=0),
        name="solve",
    )(place, own, other, mine, inverse)


def change_kernel(sides_ref, across_ref, change_ref, high_ref, low_ref):
    order = sides_ref.shape[1]

    @pl.when(pl.program_id(0) == 0)
    def _():
        high_ref[...], low_ref[...] = parts_of(sides_ref[...])

    across = jnp.concatenate([across_ref[:, u].reshape(BLOCK, order) for u in range(across_ref.shape[1])], axis=0)
    change_ref[...] = times_parts((high_ref[...], low_ref[...]), parts_of(across), ROWS_BY_ROWS)


def changes(sides, across, steps, cost):
    total, order = sides.shape
    size = across.shape[0] * across.shape[1] * across.shape[2] // steps
    return pl.pallas_call(
        change_kernel,
        grid=(steps,),
        out_shape=jax.ShapeDtypeStruct((total, steps * size), jnp.float32),
        in_specs=[
            pl.BlockSpec((total, order), lambda t: (0, 0)),
            pl.BlockSpec((across.shape[0], across.shape[1] // steps) + across.shape[2:], lambda t: (0, t, 0, 0)),
        ],
        out_specs=pl.BlockSpec((total, size), lambda t: (0, t)),
        scratch_shapes=[pltpu.VMEM((total, order), jnp.bfloat16), pltpu.VMEM((total, order), jnp.bfloat16)],
        compiler_params=pltpu.CompilerParams(vmem_limit_bytes=60 * 2**20),
        cost_estimate=pl.CostEstimate(flops=cost, bytes_accessed=2**10, transcendentals=0),
        name="changes",
    )(sides, across)


def finish_kernel(grid_rows, grid_cols, place_ref, tiles_ref, change_ref, solved_ref, boost_ref, out_ref):
    my_row, my_col = place_ref[0], place_ref[1]
    size = boost_ref.shape[2]
    halves = size // BLOCK
    bands, count, order = change_ref.shape
    local_cols = order // size
    per = local_cols * halves
    row = lax.broadcasted_iota(jnp.int32, (count, BLOCK), 0) + pl.program_id(0) * count
    col = lax.broadcasted_iota(jnp.int32, (count, BLOCK), 1)
    for band in range(bands):
        i, u = band // halves, band % halves
        line = boost_ref[i * grid_rows + my_row][:, u * BLOCK : (u + 1) * BLOCK]
        for t in range(local_cols):
            on_diagonal = i * grid_rows + my_row == t * grid_cols + my_col
            for h in range(halves):
                first = t * size + h * BLOCK
                value = tiles_ref[pl.ds(band * per + t * halves + h, count, stride=bands * per), :]
                value = value - change_ref[band, :, first : first + BLOCK]
                if u == h:
                    value = value + jnp.where(jnp.logical_and(on_diagonal, row == col), line, 0.0)
                if t == 0:
                    lane = pl.multiple_of(jnp.minimum(my_col, PANELS - 1) * size + h * BLOCK, BLOCK)
                    value = jnp.where(my_col < PANELS, solved_ref[band, :, pl.ds(lane, BLOCK)], value)
                out_ref[band, pl.ds(t * halves + h, count, stride=per), :] = value


def finish(place, tiles, change, solved, boost, grid_rows, grid_cols, steps=4):
    total, order = change.shape
    bands, count = total // BLOCK, BLOCK // steps
    per = order // BLOCK
    rows = pl.BlockSpec((bands, count, order), lambda s: (0, s, 0))
    out = pl.pallas_call(
        functools.partial(finish_kernel, grid_rows, grid_cols),
        grid=(steps,),
        out_shape=jax.ShapeDtypeStruct((bands, BLOCK * per, BLOCK), jnp.float32),
        in_specs=[
            SCALARS,
            pl.BlockSpec((count * bands * per, BLOCK), lambda s: (s, 0)),
            rows,
            rows,
            pl.BlockSpec(boost.shape, lambda s: (0, 0, 0)),
        ],
        out_specs=pl.BlockSpec((bands, count * per, BLOCK), lambda s: (0, s, 0)),
        compiler_params=pltpu.CompilerParams(vmem_limit_bytes=57 * 2**20),
        cost_estimate=pl.CostEstimate(flops=10**6, bytes_accessed=2**10, transcendentals=0),
        name="finish",
    )(place, tiles, change.reshape(bands, BLOCK, order), solved.reshape(bands, BLOCK, order), boost)
    return out


def body(front_entries, child_updates, diag_boost, tile_mask, child_parent, child_index):
    grid_rows = lax.axis_size("row")
    grid_cols = lax.axis_size("col")
    groups = lax.axis_size("front")
    my_group = lax.axis_index("front")
    my_row = lax.axis_index("row")
    my_col = lax.axis_index("col")
    local_rows = front_entries.shape[1]
    slices = front_entries.shape[2]
    local_cols = front_entries.shape[7]
    size = front_entries.shape[8]
    held = child_updates.shape[0]
    child_tiles = child_updates.shape[1]
    halves = grid_rows // grid_cols
    order = PANELS * size

    blocks = order // BLOCK
    parents = child_parent.reshape(groups, held)
    comes = parents == my_group
    index = jnp.sum(jnp.where(comes[:, :, None], child_index.reshape(groups, held, child_tiles), 0), axis=1)
    index = jnp.where(jnp.any(comes, axis=1)[:, None], index, -1)
    mine = lax.dynamic_index_in_dim(parents, my_group, 0, keepdims=False)
    goes = (mine[None, :] == jnp.arange(groups)[:, None])[:, :, None, None, None]
    pieces = child_updates.reshape(held, child_tiles * slices, child_tiles * size // BLOCK, BLOCK)
    slots = jnp.sum(jnp.where(goes, pieces[None], 0.0), axis=1)
    lines_of = lax.all_to_all(slots, "front", split_axis=0, concat_axis=0, tiled=True)
    arrived = lines_of.reshape(groups, child_tiles, slices, child_tiles, size)

    entries = front_entries.reshape(local_rows, slices, grid_rows, grid_cols, local_cols, size)
    mask_tiles = jnp.transpose(tile_mask[0].reshape(local_rows, grid_rows, local_cols, grid_cols), (0, 1, 3, 2))
    kept = (mask_tiles == 1)[:, None, :, :, :, None]
    row_ids = jnp.arange(local_rows)[:, None] * grid_rows + jnp.arange(grid_rows)[None, :]
    col_ids = jnp.arange(local_cols)[:, None] * grid_cols + jnp.arange(grid_cols)[None, :]
    row_hits = (index[:, None, None, :] == row_ids[None, :, :, None]).astype(jnp.float32)
    col_hits = (index[:, None, None, :] == col_ids[None, :, :, None]).astype(jnp.float32)
    within = jnp.arange(slices) * grid_rows * grid_cols + my_row * grid_cols + my_col
    boost = jnp.where(
        within[:, None, None, None] == jnp.arange(size),
        jnp.where(jnp.eye(grid_rows, PANELS, dtype=bool)[:, :, None], diag_boost[0, :PANELS], 0.0),
        0.0,
    )
    boost = jnp.where((jnp.arange(local_rows) == 0)[:, None, None, None, None], boost, 0.0)
    base = jnp.where(kept[:, :, :, :PANELS, 0], entries[:, :, :, :PANELS, 0, :], 0.0) + boost
    children = lines_of.reshape((-1,) + lines_of.shape[2:])
    lines, split = make_panel(index, base.reshape(-1, blocks, BLOCK), children, grid_rows)

    split = lax.all_to_all(split, "col", split_axis=0, concat_axis=0, tiled=True)
    for_cols = jnp.transpose(split, (1, 0, 2, 3)).reshape(local_cols * slices, grid_cols, order)
    lines, for_cols, arrived = lax.optimization_barrier((lines, for_cols, arrived))
    across = lax.all_gather(for_cols, "row", axis=0)

    lines = lines.reshape(grid_rows * grid_cols, -1, 1, BLOCK)
    lines = lax.all_to_all(lines, ("row", "col"), split_axis=0, concat_axis=0, tiled=True)
    lines = jnp.transpose(lines.reshape(grid_rows * grid_cols, -1, BLOCK), (1, 0, 2))

    spread = jnp.einsum("naube,ntpb->nautpe", arrived, col_hits, precision=HIGHEST)
    assembled = jnp.where(kept, entries, 0.0) + jnp.einsum("niqa,nautpe->iuqpte", row_hits, spread, precision=HIGHEST)
    joined = jnp.transpose(assembled, (2, 3, 0, 1, 4, 5))
    joined = joined.reshape(grid_rows * grid_cols, local_rows * slices, local_cols * size // BLOCK, BLOCK)

    lines, joined = lax.optimization_barrier((lines, joined))
    tiles = lax.all_to_all(joined, ("row", "col"), split_axis=0, concat_axis=0, tiled=True).reshape(-1, BLOCK)

    def over_chips(value):
        cols = range(grid_cols)
        moved = [lax.ppermute(value, "col", [(c, (c + 2 * d) % grid_cols) for c in cols]) for d in SOURCES[1:]]
        return jnp.stack([value] + moved)

    def over_cores(value):
        return lax.ppermute(value, "col", [(c, c ^ 1) for c in range(grid_cols)])

    place = jnp.stack([my_row, my_col]).astype(jnp.int32)
    own = over_chips(lines)
    other = over_cores(own)
    inverse, mine = factor(place, own, other, order)
    solved, sides = solve(place, own, other, mine, inverse, grid_rows, local_rows)
    change = changes(sides, across, local_cols, 59 * 10**9)
    out = finish(place, tiles, change, solved, diag_boost[0][:, None, :], grid_rows, grid_cols)
    return out.reshape(1, local_rows, 1, size, local_cols, 1, size)


def solution(mesh):
    placed = (
        P("front", None, None, "row", "col", None, None, None, None),
        P("front", None, None, "row", "col", None, None),
        P("front", None, None),
        P("front", None, None),
        P(),
        P(),
    )
    return jax.shard_map(
        body,
        mesh=mesh,
        in_specs=placed,
        out_specs=P("front", None, "row", None, None, "col", None),
        check_vma=False,
    )
```
